128 devices in a mesh: rows: 128 (over y, z, x, core).
Axes of the slice: x: 4, y: 4, z: 4, core: 2. Of those that a mesh axis runs over, the one named last changes fastest.
Arguments:
- parent_old: float32 [3, 512, 8192], P(None, 'rows'), may hold values from -3 to 3
- parent_now: float32 [3, 512, 8192], P(None, 'rows'), may hold values from -3 to 3
- child_old: float32 [4, 3, 1024, 4096], P(None, None, 'rows'), may hold values from -3 to 3
- child_now: float32 [4, 3, 1024, 4096], P(None, None, 'rows'), may hold values from -3 to 3
- parent_depth: float32 [512, 8192], P('rows'), may hold values from 0.5 to 2
- child_depth: float32 [4, 1024, 4096], P(None, 'rows'), may hold values from 0.5 to 2
- child_rows: int32 [4], replicated, may hold values from 0 to 384, as said below
- child_cols: int32 [4], replicated, may hold values from 1 to 7679, as said below
- parent_cot_mid: float32 [3, 512, 8192], P(None, 'rows'), may hold values from -6 to 6
- parent_cot_end: float32 [3, 512, 8192], P(None, 'rows'), may hold values from -6 to 6
- child_cot_mid: float32 [4, 3, 1024, 4096], P(None, None, 'rows'), may hold values from -6 to 6
- child_cot_end: float32 [4, 3, 1024, 4096], P(None, None, 'rows'), may hold values from -6 to 6
Outputs:
- parent_end: float32 [3, 512, 8192], P(None, 'rows')
- child_end: float32 [4, 3, 1024, 4096], P(None, None, 'rows')
- parent_grad_old: float32 [3, 512, 8192], P(None, 'rows')
- parent_grad_now: float32 [3, 512, 8192], P(None, 'rows')
- child_grad_old: float32 [4, 3, 1024, 4096], P(None, None, 'rows')
- child_grad_now: float32 [4, 3, 1024, 4096], P(None, None, 'rows')
The draws below stay inside these ranges and needn't reach their ends.
Inputs may be any that keep to these rules, and one draw needn't show every extreme that they name: Coastal grid k covers the ocean rows child_rows[k] to child_rows[k] + 127, all inside the ocean grid. Coastal grid k covers the ocean columns child_cols[k] to child_cols[k] + 511, which lie, with one more column on each side, in columns k * 2048 to (k + 1) * 2048 - 1.
All inputs are finite; a program needn't handle non-finite values.
Results may differ from the reference program's by a relative error of at most 0.0001.
Values sent between devices are 32-bit elements; how exact they have to be, the bound alone decides.
A program may use at most 128 MiB of HBM per device.

```python
import math
import jax
import jax.numpy as jnp
from jax import lax

P_COLS = 8192
C_COLS = 4096
NCHILD = 4
RATIO = 8
STEPS = 2
PROWS = 512
CROWS = 1024
FOOT_ROWS = 128
FOOT_COLS = 512
BAND = 2048


def draw_child_rows(key, part):
    key = jax.random.fold_in(key, 11)
    drawn = jax.random.randint(key, (NCHILD,), 0, PROWS - FOOT_ROWS + 1)
    drawn = drawn.at[0].set(0)
    drawn = drawn.at[1].set(PROWS - FOOT_ROWS)
    return drawn.astype(jnp.int32)


def draw_child_cols(key, part):
    key = jax.random.fold_in(key, 12)
    inside = jax.random.randint(key, (NCHILD,), 1, BAND - FOOT_COLS)
    inside = inside.at[0].set(1)
    inside = inside.at[NCHILD - 1].set(BAND - FOOT_COLS - 1)
    return (jnp.arange(NCHILD) * BAND + inside).astype(jnp.int32)


def shard_levels(key, shape, cuts, smallest, largest):
    level, own = 1.0, jax.random.fold_in(key, 6)
    for dim, parts in cuts:
        draws = jnp.exp(jax.random.uniform(jax.random.fold_in(own, dim), (parts,), jnp.float32, smallest / len(cuts), largest / len(cuts)))
        level = level * jnp.repeat(draws, shape[dim] // parts).reshape([-1 if axis == dim else 1 for axis in range(len(shape))])
    return level


def noise(key, shape, spread, reach, split=(), dtype=jnp.bfloat16):
    loudness = shard_levels(key, shape, split, -0.22, 0.18) if split else 1.0
    result = jax.random.normal(key, shape, jnp.float32) * spread * loudness
    return jnp.minimum(jnp.maximum(result, -reach), reach).astype(dtype)


def setup_inputs(seed: int = 0) -> dict:
    key_of = jax.random.split(jax.random.key(seed), 13)
    parent_old = noise(key_of[0], (3, PROWS, P_COLS), 0.5, 3.0, ((1, 128),), jnp.float32)
    parent_now = noise(key_of[1], (3, PROWS, P_COLS), 0.5, 3.0, ((1, 128),), jnp.float32)
    child_old = noise(key_of[2], (NCHILD, 3, CROWS, C_COLS), 0.5, 3.0, ((2, 128),), jnp.float32)
    child_now = noise(key_of[3], (NCHILD, 3, CROWS, C_COLS), 0.5, 3.0, ((2, 128),), jnp.float32)
    parent_depth = jnp.clip(jnp.exp(math.log(2.0) - 1.3862944 * jax.random.uniform(key_of[4], (PROWS, P_COLS), jnp.float32) ** shard_levels(key_of[4], (PROWS, P_COLS), ((0, 128),), -0.2, 0.2)), 0.5, 2.0)
    child_depth = jnp.clip(jnp.exp(math.log(2.0) - 1.3862944 * jax.random.uniform(key_of[5], (NCHILD, CROWS, C_COLS), jnp.float32) ** shard_levels(key_of[5], (NCHILD, CROWS, C_COLS), ((1, 128),), -0.2, 0.2)), 0.5, 2.0)
    child_rows = draw_child_rows(jax.random.fold_in(key_of[12], 71), 0)
    child_cols = draw_child_cols(jax.random.fold_in(key_of[12], 71), 0)
    parent_cot_mid = noise(key_of[8], (3, PROWS, P_COLS), 1.0, 6.0, ((1, 128),), jnp.float32)
    parent_cot_end = noise(key_of[9], (3, PROWS, P_COLS), 1.0, 6.0, ((1, 128),), jnp.float32)
    child_cot_mid = noise(key_of[10], (NCHILD, 3, CROWS, C_COLS), 1.0, 6.0, ((2, 128),), jnp.float32)
    child_cot_end = noise(key_of[11], (NCHILD, 3, CROWS, C_COLS), 1.0, 6.0, ((2, 128),), jnp.float32)
    return {"parent_old": parent_old, "parent_now": parent_now, "child_old": child_old, "child_now": child_now, "parent_depth": parent_depth, "child_depth": child_depth, "child_rows": child_rows, "child_cols": child_cols, "parent_cot_mid": parent_cot_mid, "parent_cot_end": parent_cot_end, "child_cot_mid": child_cot_mid, "child_cot_end": child_cot_end}


TIME_STEP = 0.15
GRAVITY = 1.0
FRICTION = 0.05

def east_west(field):
    return 0.5 * (field[..., 1:-1, 2:] - field[..., 1:-1, :-2])

def north_south(field):
    return 0.5 * (field[..., 2:, 1:-1] - field[..., :-2, 1:-1])

def tendency(padded, bathymetry):
    surface = padded[..., 0, :, :]
    east_flow = padded[..., 1, :, :]
    north_flow = padded[..., 2, :, :]
    east_mid = east_flow[..., 1:-1, 1:-1]
    north_mid = north_flow[..., 1:-1, 1:-1]
    surface_rate = -bathymetry * (east_west(east_flow) + north_south(north_flow)) - east_west(surface * east_flow) - north_south(surface * north_flow)
    east_rate = -(east_mid * east_west(east_flow) + north_mid * north_south(east_flow)) - GRAVITY * east_west(surface) - FRICTION * east_mid
    north_rate = -(east_mid * east_west(north_flow) + north_mid * north_south(north_flow)) - GRAVITY * north_south(surface) - FRICTION * north_mid
    return jnp.stack([surface_rate, east_rate, north_rate], axis=-3)

def leapfrog(states, parent_depth, child_depth, child_rows, child_cols):
    parent_old, parent_now, child_old, child_now = states
    padded = jnp.pad(parent_now, ((0, 0), (1, 1), (1, 1)))
    parent_next = parent_old + 2.0 * TIME_STEP * tendency(padded, parent_depth)
    left_cols = []
    right_cols = []
    for nested in range(NCHILD):
        row_band = lax.dynamic_slice_in_dim(parent_now, child_rows[nested].astype(jnp.int32), FOOT_ROWS, 1)
        left_edge = lax.dynamic_slice_in_dim(row_band, (child_cols[nested] - 1).astype(jnp.int32), 1, 2)
        right_edge = lax.dynamic_slice_in_dim(row_band, (child_cols[nested] + FOOT_COLS).astype(jnp.int32), 1, 2)
        left_cols.append(jnp.repeat(left_edge, RATIO, axis=1))
        right_cols.append(jnp.repeat(right_edge, RATIO, axis=1))
    framed = jnp.concatenate([jnp.stack(left_cols), child_now, jnp.stack(right_cols)], axis=3)
    framed = jnp.pad(framed, ((0, 0), (0, 0), (1, 1), (0, 0)))
    child_next = child_old + 2.0 * TIME_STEP * tendency(framed, child_depth)
    coarse_means = child_next.reshape(NCHILD, 3, FOOT_ROWS, RATIO, FOOT_COLS, RATIO).mean(axis=(3, 5))
    zero_index = jnp.zeros((), jnp.int32)
    for nested in range(NCHILD):
        parent_next = lax.dynamic_update_slice(parent_next, coarse_means[nested], (zero_index, child_rows[nested].astype(jnp.int32), child_cols[nested].astype(jnp.int32)))
    return (parent_now, parent_next, child_now, child_next)

def reference(parent_old, parent_now, child_old, child_now, parent_depth, child_depth, child_rows, child_cols, parent_cot_mid, parent_cot_end, child_cot_mid, child_cot_end):

    def advance(parent_first, parent_second, child_first, child_second):
        states = (parent_first, parent_second, child_first, child_second)
        for step_index in range(STEPS):
            states = leapfrog(states, parent_depth, child_depth, child_rows, child_cols)
        return states
    outputs, pullback = jax.vjp(advance, parent_old, parent_now, child_old, child_now)
    gradients = pullback((parent_cot_mid, parent_cot_end, child_cot_mid, child_cot_end))
    return (outputs[1], outputs[3], gradients[0], gradients[1], gradients[2], gradients[3])
```

```python
import functools

import jax
import jax.numpy as jnp
from jax import lax
from jax.experimental import pallas as pl
from jax.experimental.pallas import tpu as pltpu
from jax.sharding import PartitionSpec as P

MESH = pl.DeviceIdType.MESH
P_ROWS = 4
P_COLS = 8192
C_ROWS = 8
C_COLS = 4096
NCHILD = 4
RATIO = 8
FOOT_ROWS = 128
FOOT_COLS = 512
BAND = 2048
TILE = 128
PADDED = C_COLS + 2 * TILE
CHUNK = 512
HALF = 0.15
DRAG = 0.015
FIELDS = 11
UNIT = 256
UNITS = FIELDS * NCHILD * (FOOT_COLS // UNIT)
ROW_UNITS = 6 * NCHILD * (FOOT_COLS // UNIT)
BACK = 3 * NCHILD * (FOOT_COLS // TILE)
BACK_FIRST = 80
EDGE = 8


def column_shifts(wide, width):
    ahead = pltpu.roll(wide, wide.shape[1] - 1, 1)[:, TILE : TILE + width]
    behind = pltpu.roll(wide, 1, 1)[:, TILE : TILE + width]
    return ahead, behind


def row_shifts(block, before, after):
    row = lax.broadcasted_iota(jnp.int32, block.shape, 0)
    ahead = jnp.where(row == C_ROWS - 1, after, pltpu.roll(block, C_ROWS - 1, 0))
    behind = jnp.where(row == 0, before, pltpu.roll(block, 1, 0))
    return ahead, behind


def split3(value):
    high = value.astype(jnp.bfloat16)
    rest = value - high.astype(jnp.float32)
    mid = rest.astype(jnp.bfloat16)
    low = (rest - mid.astype(jnp.float32)).astype(jnp.bfloat16)
    return high, mid, low


def exact_dot(rows, matrix):
    return sum(jnp.dot(part, matrix, preferred_element_type=jnp.float32) for part in split3(rows))


def coastal_kernel(
    n,
    rows_smem,
    win_hbm,
    frame_hbm,
    halo_hbm,
    old_hbm,
    now_hbm,
    depth_hbm,
    mid_hbm,
    end_hbm,
    next_out,
    gold_out,
    gnow_out,
    edge_out,
    back_out,
    halo_out,
    old,
    now,
    nxt,
    depth,
    mid,
    end,
    a2,
    a1,
    slopes1,
    slopes2,
    send_rows,
    halo_rows,
    win,
    frame,
    frames,
    fvals,
    gathered,
    picked,
    special,
    rowbuf,
    specbuf,
    lhs,
    spread,
    sums,
    rest,
    pairs,
    returned,
    placed,
    qrow,
    edges,
    packet,
    load_sem,
    store_sem,
    halo_send,
    halo_recv,
    ag_send,
    ag_recv,
    t_send,
    t_recv,
):
    me = lax.axis_index("rows")
    up = lax.rem(me + 1, n)
    down = lax.rem(me + n - 1, n)
    has_before = jnp.where(me > 0, 1.0, 0.0)
    has_after = jnp.where(me < n - 1, 1.0, 0.0)
    centre = pl.ds(TILE, C_COLS)

    barrier = pltpu.get_barrier_semaphore()

    def greet(j, carry):
        pl.semaphore_signal(barrier, inc=1, device_id=(lax.rem(me + j, n),), device_id_type=MESH)
        return carry

    lax.fori_loop(1, n, greet, 0)

    loads = [
        pltpu.make_async_copy(now_hbm, now.at[:, :, :, centre], load_sem.at[0]),
        pltpu.make_async_copy(old_hbm, old, load_sem.at[1]),
        pltpu.make_async_copy(depth_hbm, depth.at[:, :, centre], load_sem.at[2]),
        pltpu.make_async_copy(mid_hbm, mid, load_sem.at[3]),
        pltpu.make_async_copy(end_hbm, end, load_sem.at[4]),
        pltpu.make_async_copy(win_hbm, win, load_sem.at[5]),
        pltpu.make_async_copy(frame_hbm, frame, load_sem.at[6]),
    ]
    for load in loads:
        load.start()

    for array in (a2, a1):
        array[:, :, :, 0:TILE] = jnp.zeros((NCHILD, 3, C_ROWS, TILE), jnp.float32)
        array[:, :, :, TILE + C_COLS :] = jnp.zeros((NCHILD, 3, C_ROWS, TILE), jnp.float32)
    depth[:, :, 0:TILE] = jnp.zeros((NCHILD, C_ROWS, TILE), jnp.float32)
    depth[:, :, TILE + C_COLS :] = jnp.zeros((NCHILD, C_ROWS, TILE), jnp.float32)
    ocean_rows = n * P_ROWS
    frames[0:EDGE] = jnp.zeros((EDGE, 1, TILE), jnp.float32)
    frames[pl.ds(EDGE + ocean_rows, EDGE)] = jnp.zeros((EDGE, 1, TILE), jnp.float32)
    gathered[0:EDGE] = jnp.zeros((EDGE, 1, UNIT), jnp.float32)
    gathered[pl.ds(EDGE + ocean_rows, EDGE)] = jnp.zeros((EDGE, 1, UNIT), jnp.float32)
    qrow[...] = jnp.zeros_like(qrow)
    packet[...] = jnp.zeros_like(packet)

    loads[0].wait()
    loads[6].wait()
    for nested in range(NCHILD):
        for part in range(3):
            send_rows[0, nested, 0, part : part + 1, :] = now[nested, part, 0:1, centre]
            send_rows[0, nested, 1, part : part + 1, :] = now[nested, part, C_ROWS - 1 : C_ROWS, centre]

    pl.semaphore_wait(barrier, n - 1)

    def halo_copies(stage, nested):
        return (
            pltpu.make_async_remote_copy(
                send_rows.at[stage, nested, 0],
                halo_rows.at[stage, nested, 1],
                halo_send.at[stage, nested, 0],
                halo_recv.at[stage, nested, 1],
                device_id=(down,),
                device_id_type=MESH,
            ),
            pltpu.make_async_remote_copy(
                send_rows.at[stage, nested, 1],
                halo_rows.at[stage, nested, 0],
                halo_send.at[stage, nested, 1],
                halo_recv.at[stage, nested, 0],
                device_id=(up,),
                device_id_type=MESH,
            ),
        )

    def halo_start(stage, nested):
        for copy in halo_copies(stage, nested):
            copy.start()

    def halo_wait(stage, nested):
        for copy in halo_copies(stage, nested):
            copy.wait_recv()

    mine = pl.ds(EDGE + me * P_ROWS, P_ROWS)
    frames[mine] = frame[...]

    def send_frame(j, carry):
        pltpu.make_async_remote_copy(
            frame,
            frames.at[mine],
            ag_send.at[0],
            ag_recv.at[0],
            device_id=(lax.rem(me + j, n),),
            device_id_type=MESH,
        ).start()
        return carry

    lax.fori_loop(1, n, send_frame, 0)
    for nested in range(NCHILD):
        halo_start(0, nested)

    loads[5].wait()

    def send_unit(j, carry):
        unit = lax.rem(me + j, UNITS)

        @pl.when(unit != me)
        def _():
            pltpu.make_async_remote_copy(
                win.at[unit],
                gathered.at[mine],
                t_send.at[0],
                t_recv.at[0],
                device_id=(unit,),
                device_id_type=MESH,
            ).start()

        @pl.when(unit == me)
        def _():
            pltpu.make_async_copy(win.at[unit], gathered.at[mine], t_recv.at[0]).start()

        return carry

    lax.fori_loop(0, UNITS, send_unit, 0)

    @pl.when(me < UNITS)
    def _():
        whole = gathered.at[pl.ds(EDGE, ocean_rows)]
        pltpu.make_async_copy(whole, whole, t_recv.at[0]).wait()
        grid_index = lax.rem(me // (FOOT_COLS // UNIT), NCHILD)
        first = rows_smem[0]
        for nested in range(1, NCHILD):
            first = jnp.where(grid_index == nested, rows_smem[nested], first)
        special[0:3] = gathered[pl.ds(EDGE + first - 2, 3)]
        special[3:6] = gathered[pl.ds(EDGE + first + FOOT_ROWS - 1, 3)]

        def pick(j, carry):
            picked[j] = gathered[EDGE + first + j]
            return carry

        lax.fori_loop(0, FOOT_ROWS, pick, 0)

        for side, target in ((0, 0), (1, n - 1)):
            source = special.at[pl.ds(3 * side, 3)]

            @pl.when(me != target)
            def _():
                pltpu.make_async_remote_copy(
                    source,
                    specbuf.at[me],
                    t_send.at[1],
                    t_recv.at[1],
                    device_id=(target,),
                    device_id_type=MESH,
                ).start()

            @pl.when(me == target)
            def _():
                pltpu.make_async_copy(source, specbuf.at[me], t_recv.at[1]).start()

        @pl.when(me < ROW_UNITS)
        def _():
            def send_row(j, carry):
                target = lax.rem(me + j, n)
                pltpu.make_async_remote_copy(
                    picked.at[target],
                    rowbuf.at[me],
                    t_send.at[2],
                    t_recv.at[2],
                    device_id=(target,),
                    device_id_type=MESH,
                ).start()
                return carry

            lax.fori_loop(1, n, send_row, 0)
            pltpu.make_async_copy(picked.at[me], rowbuf.at[me], t_recv.at[2]).start()

    all_but = frames.at[pl.ds(0, (n - 1) * P_ROWS)]
    pltpu.make_async_copy(all_but, all_but, ag_recv.at[0]).wait()
    lane = lax.broadcasted_iota(jnp.int32, (1, TILE), 1)

    def lanes_of(offset):
        value = frames[EDGE + rows_smem[0] + me + offset]
        for nested in range(1, NCHILD):
            other = frames[EDGE + rows_smem[nested] + me + offset]
            value = jnp.where(lane >= 32 * nested, other, value)
        return value

    south, middle, north = lanes_of(-1), lanes_of(0), lanes_of(1)

    def lane_field(row, index):
        return row if index == 0 else pltpu.roll(row, TILE - index, 1)

    e_w, e_c, e_e = [lane_field(middle, i) for i in (0, 1, 2)]
    u_w, u_c, u_e = [lane_field(middle, i) for i in (3, 4, 5)]
    v_w, v_c, v_e = [lane_field(middle, i) for i in (6, 7, 8)]
    e_s, u_s, v_s = [lane_field(south, i) for i in (1, 4, 7)]
    e_n, u_n, v_n = [lane_field(north, i) for i in (1, 4, 7)]
    e_o, u_o, v_o, b_c, ce_c, cu_c, cv_c = [lane_field(middle, i) for i in range(9, 16)]
    e_2 = e_o - HALF * (
        b_c * ((u_e - u_w) + (v_n - v_s)) + (e_e * u_e - e_w * u_w) + (e_n * v_n - e_s * v_s)
    )
    u_2 = u_o - HALF * (u_c * (u_e - u_w) + v_c * (u_n - u_s) + (e_e - e_w)) - DRAG * u_c
    v_2 = v_o - HALF * (u_c * (v_e - v_w) + v_c * (v_n - v_s) + (e_n - e_s)) - DRAG * v_c
    for index, value in enumerate((e_c, u_c, v_c, e_2, u_2, v_2, b_c, ce_c, cu_c, cv_c)):
        fvals[index : index + 1, :] = value
    for nested in range(NCHILD):
        for side in range(2):
            where = 32 * nested + 16 * side
            lanes = slice(0, TILE) if side == 0 else slice(TILE + C_COLS, PADDED)
            for part in range(3):
                for base, array in ((0, now), (3, nxt)):
                    cell = fvals[base + part : base + part + 1, where : where + 1]
                    array[nested, part, :, lanes] = jnp.broadcast_to(cell, (C_ROWS, TILE))

    def forward(stage, nested, state, base, target, slopes):
        def chunk(j, carry):
            here = pl.multiple_of(j * CHUNK, CHUNK)
            wide = pl.ds(here, CHUNK + 2 * TILE)
            plain = pl.ds(here, CHUNK)
            inner = pl.ds(here + TILE, CHUNK)
            shifted = []
            for part in range(3):
                block = state[nested, part, :, wide]
                mid_block = block[:, TILE : TILE + CHUNK]
                before = halo_rows[stage, nested, 0, part : part + 1, plain] * has_before
                after = halo_rows[stage, nested, 1, part : part + 1, plain] * has_after
                shifted.append(
                    (mid_block,) + column_shifts(block, CHUNK) + row_shifts(mid_block, before, after)
                )
            (e, ee, ew, en, es), (u, ue, uw, un, us), (v, ve, vw, vn, vs) = shifted
            bed = depth[nested, :, inner]
            ux, uy, vx, vy = ue - uw, un - us, ve - vw, vn - vs
            slopes[0, nested, :, plain] = ux
            slopes[1, nested, :, plain] = uy
            slopes[2, nested, :, plain] = vx
            slopes[3, nested, :, plain] = vy
            news = (
                base(0, inner, plain)
                - HALF * (bed * (ux + vy) + (ee * ue - ew * uw) + (en * vn - es * vs)),
                base(1, inner, plain) - HALF * (u * ux + v * uy + (ee - ew)) - DRAG * u,
                base(2, inner, plain) - HALF * (u * vx + v * vy + (en - es)) - DRAG * v,
            )
            for part in range(3):
                target(part, inner, plain, news[part], j)
            return carry

        lax.fori_loop(0, C_COLS // CHUNK, chunk, 0)

    def add_sums(which, nested, part, value, j):
        row = (nested * 3 + part) * 4 + j // 2
        sums[which, pl.ds(row, 1), pl.ds(pl.multiple_of(lax.rem(j, 2) * CHUNK, CHUNK), CHUNK)] = (
            jnp.sum(value, axis=0, keepdims=True)
        )

    def stage_a(nested, carry):
        halo_wait(0, nested)

        def target(part, inner, plain, value, j):
            nxt[nested, part, :, inner] = value
            send_rows[1, nested, 0, part : part + 1, plain] = value[0:1]
            send_rows[1, nested, 1, part : part + 1, plain] = value[C_ROWS - 1 :]
            add_sums(0, nested, part, value, j)

        forward(0, nested, now, lambda part, inner, plain: old[nested, part, :, plain], target, slopes1)
        halo_start(1, nested)
        return carry

    for index in (1, 2, 3, 4):
        loads[index].wait()
    lax.fori_loop(0, NCHILD, stage_a, 0)

    def stage_b(nested, carry):
        halo_wait(1, nested)

        def target(part, inner, plain, value, j):
            old[nested, part, :, plain] = value
            add_sums(1, nested, part, value, j)

        forward(1, nested, nxt, lambda part, inner, plain: now[nested, part, :, inner], target, slopes2)
        return carry

    lax.fori_loop(0, NCHILD, stage_b, 0)
    store_next = pltpu.make_async_copy(old, next_out, store_sem.at[0])
    store_next.start()

    fine = lax.broadcasted_iota(jnp.int32, (RATIO * TILE, TILE), 0) // RATIO
    coarse = lax.broadcasted_iota(jnp.int32, (RATIO * TILE, TILE), 1)
    gather_matrix = jnp.where(fine == coarse, 1.0 / (RATIO * RATIO), 0.0).astype(jnp.bfloat16)
    fine_t = lax.broadcasted_iota(jnp.int32, (TILE, RATIO * TILE), 1) // RATIO
    coarse_t = lax.broadcasted_iota(jnp.int32, (TILE, RATIO * TILE), 0)
    spread_matrix = jnp.where(fine_t == coarse_t, 1.0 / (RATIO * RATIO), 0.0).astype(jnp.bfloat16)
    for which in range(2):
        rest[which] = exact_dot(sums[which], gather_matrix)
    for unit in range(BACK):
        for which in range(2):
            pairs[unit, which : which + 1, :] = rest[which, unit : unit + 1, :]

    span = FOOT_ROWS
    pad = ocean_rows
    returned[0:pad] = jnp.zeros((pad, 2, TILE), jnp.float32)
    returned[pl.ds(pad + span, pad)] = jnp.zeros((pad, 2, TILE), jnp.float32)

    def send_back(j, carry):
        unit = lax.rem(me + j, BACK)
        owner = unit + BACK_FIRST

        @pl.when(owner != me)
        def _():
            pltpu.make_async_remote_copy(
                pairs.at[unit],
                returned.at[pad + me],
                t_send.at[3],
                t_recv.at[3],
                device_id=(owner,),
                device_id_type=MESH,
            ).start()

        @pl.when(owner == me)
        def _():
            pltpu.make_async_copy(pairs.at[unit], returned.at[pad + me], t_recv.at[3]).start()

        return carry

    lax.fori_loop(0, BACK, send_back, 0)

    all_rows = rowbuf.at[pl.ds(0, ROW_UNITS)]
    pltpu.make_async_copy(all_rows, all_rows, t_recv.at[2]).wait()
    parts_of = FOOT_COLS // UNIT
    for which in range(2):
        for nested in range(NCHILD):
            for part in range(3):
                for half in range(parts_of):
                    unit = ((3 * which + part) * NCHILD + nested) * parts_of + half
                    for piece in range(UNIT // TILE):
                        row = (nested * 3 + part) * 4 + half * (UNIT // TILE) + piece
                        lhs[which, row : row + 1, :] = rowbuf[unit, :, TILE * piece : TILE * (piece + 1)]
    spread[0] = exact_dot(lhs[0], spread_matrix)

    def spread_at(which, nested, part, j):
        row = (nested * 3 + part) * 4 + j // 2
        return spread[which, pl.ds(row, 1), pl.ds(pl.multiple_of(lax.rem(j, 2) * CHUNK, CHUNK), CHUNK)]

    def put_products(stage, nested, plain, bed, v, ae, au, av):
        for index, value in enumerate((ae, av, v * au, bed * ae + v * av)):
            send_rows[stage, nested, 0, index : index + 1, plain] = value[0:1]
            send_rows[stage, nested, 1, index : index + 1, plain] = value[C_ROWS - 1 :]

    def stage_c(nested, carry):
        def chunk(j, inner_carry):
            here = pl.multiple_of(j * CHUNK, CHUNK)
            plain = pl.ds(here, CHUNK)
            inner = pl.ds(here + TILE, CHUNK)
            scaled = []
            for part in range(3):
                total = end[nested, part, :, plain] + spread_at(0, nested, part, j)
                end[nested, part, :, plain] = total
                scaled.append(HALF * total)
                a2[nested, part, :, inner] = scaled[-1]
            put_products(2, nested, plain, depth[nested, :, inner], nxt[nested, 2, :, inner], *scaled)
            return inner_carry

        lax.fori_loop(0, C_COLS // CHUNK, chunk, 0)
        halo_start(2, nested)
        return carry

    lax.fori_loop(0, NCHILD, stage_c, 0)

    @pl.when((me == 0) | (me == n - 1))
    def _():
        all_special = specbuf.at[pl.ds(0, UNITS)]
        pltpu.make_async_copy(all_special, all_special, t_recv.at[1]).wait()
        sign = jnp.where(me == 0, -1.0, 1.0)
        offset = jnp.where(me == 0, -1, 1)
        wide_lane = lax.broadcasted_iota(jnp.int32, (1, FOOT_COLS), 1)
        for nested in range(NCHILD):

            def line(field, row):
                unit = (field * NCHILD + nested) * parts_of
                return jnp.concatenate([specbuf[unit + half, row] for half in range(parts_of)], axis=1)

            ce, cu, cv = [HALF * line(field, 1) for field in range(3)]
            u1, v1 = line(7, 1), line(8, 1)
            side_row = frames[EDGE + rows_smem[nested] + me + offset]
            west = side_row[:, 32 * nested + 7 : 32 * nested + 8]
            east = side_row[:, 32 * nested + 23 : 32 * nested + 24]
            v_east = jnp.where(
                wide_lane == FOOT_COLS - 1, east, pltpu.roll(v1, FOOT_COLS - 1, 1)
            )
            v_west = jnp.where(wide_lane == 0, west, pltpu.roll(v1, 1, 1))
            v2 = (
                line(9, 1)
                - HALF
                * (
                    u1 * (v_east - v_west)
                    + v1 * (line(8, 2) - line(8, 0))
                    + (line(6, 2) - line(6, 0))
                )
                - DRAG * v1
            )
            e_q, v_q = [
                jnp.concatenate(
                    [rest[0, (nested * 3 + part) * 4 + q : (nested * 3 + part) * 4 + q + 1, :] for q in range(4)],
                    axis=1,
                )
                for part in (0, 2)
            ]
            qrow[nested, 0:1, :] = sign * (v_q * ce + cv)
            qrow[nested, 1:2, :] = sign * (v2 * cu)
            qrow[nested, 2:3, :] = sign * (line(10, 1) * ce + v2 * cv + e_q * ce)

    for nested in range(NCHILD):
        row0 = nested * 12
        for side in range(2):
            sign = -1.0 if side == 0 else 1.0
            where = 32 * nested + 16 * side
            cell = 0 if side == 0 else TILE - 1
            chunk_row = 0 if side == 0 else 3
            u2, bed, ce, cu, cv = [fvals[i : i + 1, where : where + 1] for i in (4, 6, 7, 8, 9)]
            ce, cu, cv = HALF * ce, HALF * cu, HALF * cv
            e_q = rest[0, row0 + chunk_row : row0 + chunk_row + 1, cell : cell + 1]
            u_q = rest[0, row0 + 4 + chunk_row : row0 + 5 + chunk_row, cell : cell + 1]
            adds = (
                sign * (u_q * ce + cu),
                sign * (bed * ce + u2 * cu + e_q * ce),
                sign * (u2 * cv),
            )
            for part in range(3):
                row = row0 + 4 * part + chunk_row
                lhs[1, row : row + 1, :] += jnp.where(lane == cell, adds[part], 0.0)
        for part in range(3):
            for q in range(4):
                row = row0 + 4 * part + q
                lhs[1, row : row + 1, :] += qrow[nested, part : part + 1, TILE * q : TILE * (q + 1)]
    spread[1] = exact_dot(lhs[1], spread_matrix)

    def adjoint(stage, nested, state, cots, slopes, target):
        def chunk(j, carry):
            here = pl.multiple_of(j * CHUNK, CHUNK)
            wide = pl.ds(here, CHUNK + 2 * TILE)
            plain = pl.ds(here, CHUNK)
            inner = pl.ds(here + TILE, CHUNK)
            cut = slice(TILE, TILE + CHUNK)
            wae, wau, wav = [cots[nested, part, :, wide] for part in range(3)]
            wu = state[nested, 1, :, wide]
            wbed = depth[nested, :, wide]
            ae, au, av, u, bed = wae[:, cut], wau[:, cut], wav[:, cut], wu[:, cut], wbed[:, cut]
            e, v = state[nested, 0, :, inner], state[nested, 2, :, inner]

            def dx(field):
                ahead, behind = column_shifts(field, CHUNK)
                return ahead - behind

            def dy(field, index):
                before = halo_rows[stage, nested, 0, index : index + 1, plain] * has_before
                after = halo_rows[stage, nested, 1, index : index + 1, plain] * has_after
                ahead, behind = row_shifts(field, before, after)
                return ahead - behind

            xe, ye = dx(wae), dy(ae, 0)
            ge = u * xe + v * ye + dx(wau) + dy(av, 1)
            gu = (
                dx(wbed * wae + wu * wau)
                + dy(v * au, 2)
                + e * xe
                - slopes[0, nested, :, plain] * au
                - slopes[2, nested, :, plain] * av
                - 0.1 * au
            )
            gv = (
                dy(bed * ae + v * av, 3)
                + dx(wu * wav)
                + e * ye
                - slopes[1, nested, :, plain] * au
                - slopes[3, nested, :, plain] * av
                - 0.1 * av
            )
            target(inner, plain, j, (ge, gu, gv))
            return carry

        lax.fori_loop(0, C_COLS // CHUNK, chunk, 0)

    def frame_cots(nested, state, cots, first):
        for side in range(2):
            near = pl.ds(TILE, TILE) if side == 0 else pl.ds(C_COLS, TILE)
            far = pl.ds(0, TILE) if side == 0 else pl.ds(TILE + C_COLS, TILE)
            cell = 0 if side == 0 else TILE - 1
            sign = 1.0 if side == 0 else -1.0
            ae, au, av = [cots[nested, part, :, near] for part in range(3)]
            u, bed = state[nested, 1, :, near], depth[nested, :, near]
            ef, uf = state[nested, 0, :, far], state[nested, 1, :, far]
            values = (uf * ae + au, bed * ae + u * au + ef * ae, u * av)
            for part in range(3):
                column = sign * jnp.sum(values[part], axis=0, keepdims=True)[:, cell : cell + 1]
                packet[...] = jnp.where(
                    lane == nested * 16 + side * 8 + first + part, column, packet[...]
                )

    def stage_d(nested, carry):
        halo_wait(2, nested)

        def target(inner, plain, j, grads):
            scaled = []
            for part in range(3):
                total = mid[nested, part, :, plain] + grads[part] + spread_at(1, nested, part, j)
                mid[nested, part, :, plain] = total
                scaled.append(HALF * total)
                a1[nested, part, :, inner] = scaled[-1]
            put_products(3, nested, plain, depth[nested, :, inner], now[nested, 2, :, inner], *scaled)

        adjoint(2, nested, nxt, a2, slopes2, target)
        halo_start(3, nested)
        frame_cots(nested, nxt, a2, 0)
        return carry

    lax.fori_loop(0, NCHILD, stage_d, 0)
    store_gold = pltpu.make_async_copy(mid, gold_out, store_sem.at[1])
    store_gold.start()

    def stage_e1(nested, carry):
        frame_cots(nested, now, a1, 3)
        return carry

    lax.fori_loop(0, NCHILD, stage_e1, 0)

    edges[me] = packet[...]

    def send_edge(j, carry):
        pltpu.make_async_remote_copy(
            packet,
            edges.at[me],
            ag_send.at[1],
            ag_recv.at[1],
            device_id=(lax.rem(me + j, n),),
            device_id_type=MESH,
        ).start()
        return carry

    lax.fori_loop(1, n, send_edge, 0)

    @pl.when(me >= BACK_FIRST)
    def _():
        all_back = returned.at[pl.ds(pad, span)]
        pltpu.make_async_copy(all_back, all_back, t_recv.at[3]).wait()
        grid_index = (me - BACK_FIRST) // 12
        first = rows_smem[0]
        for nested in range(1, NCHILD):
            first = jnp.where(grid_index == nested, rows_smem[nested], first)
        placed[0:EDGE] = jnp.zeros((EDGE, 2, TILE), jnp.float32)
        placed[pl.ds(EDGE + ocean_rows, EDGE)] = jnp.zeros((EDGE, 2, TILE), jnp.float32)

        def place(j, carry):
            placed[EDGE + j] = returned[pad + j - first]
            return carry

        lax.fori_loop(0, ocean_rows, place, 0)

        def send_placed(j, carry):
            target = lax.rem(me + j, n)
            pltpu.make_async_remote_copy(
                placed.at[pl.ds(EDGE + target * P_ROWS - 2, 8)],
                back_out.at[me - BACK_FIRST],
                t_send.at[4],
                t_recv.at[4],
                device_id=(target,),
                device_id_type=MESH,
            ).start()
            return carry

        lax.fori_loop(1, n, send_placed, 0)
        pltpu.make_async_copy(
            placed.at[pl.ds(EDGE + me * P_ROWS - 2, 8)], back_out.at[me - BACK_FIRST], t_recv.at[4]
        ).start()

    ocean_up = pltpu.make_async_remote_copy(
        halo_hbm.at[1], halo_out.at[0], load_sem.at[7], load_sem.at[8], device_id=(up,), device_id_type=MESH
    )
    ocean_down = pltpu.make_async_remote_copy(
        halo_hbm.at[0], halo_out.at[1], load_sem.at[9], load_sem.at[10], device_id=(down,), device_id_type=MESH
    )
    ocean_up.start()
    ocean_down.start()

    def stage_e(nested, carry):
        halo_wait(3, nested)

        def target(inner, plain, j, grads):
            for part in range(3):
                end[nested, part, :, plain] = end[nested, part, :, plain] + grads[part]

        adjoint(3, nested, now, a1, slopes1, target)
        return carry

    lax.fori_loop(0, NCHILD, stage_e, 0)
    store_gnow = pltpu.make_async_copy(end, gnow_out, store_sem.at[2])
    store_gnow.start()

    all_edges = edges.at[pl.ds(0, n - 1)]
    pltpu.make_async_copy(all_edges, all_edges, ag_recv.at[1]).wait()
    store_edges = pltpu.make_async_copy(edges, edge_out, store_sem.at[3])
    store_edges.start()

    ocean_up.wait()
    ocean_down.wait()
    pltpu.make_async_copy(back_out, back_out, t_recv.at[4]).wait()
    for store in (store_next, store_gold, store_gnow, store_edges):
        store.wait()

    pltpu.make_async_copy(all_but, all_but, ag_send.at[0]).wait()
    pltpu.make_async_copy(all_edges, all_edges, ag_send.at[1]).wait()

    def drain_halo(nested, carry):
        for stage in range(4):
            for copy in halo_copies(stage, nested):
                copy.wait_send()
        return carry

    lax.fori_loop(0, NCHILD, drain_halo, 0)

    @pl.when(me < UNITS)
    def _():
        sent = win.at[pl.ds(0, UNITS - 1)]
        pltpu.make_async_copy(sent, sent, t_send.at[0]).wait()
        for target in (0, n - 1):

            @pl.when(me != target)
            def _():
                one = special.at[pl.ds(0, 3)]
                pltpu.make_async_copy(one, one, t_send.at[1]).wait()

    @pl.when(me >= UNITS)
    def _():
        pltpu.make_async_copy(win, win, t_send.at[0]).wait()

    @pl.when(me < ROW_UNITS)
    def _():
        sent = picked.at[pl.ds(0, n - 1)]
        pltpu.make_async_copy(sent, sent, t_send.at[2]).wait()

    @pl.when(me >= BACK_FIRST)
    def _():
        sent = pairs.at[pl.ds(0, BACK - 1)]
        pltpu.make_async_copy(sent, sent, t_send.at[3]).wait()
        gone = returned.at[pl.ds(0, (n - 1) * 8)]
        pltpu.make_async_copy(gone, gone, t_send.at[4]).wait()

    @pl.when(me < BACK_FIRST)
    def _():
        pltpu.make_async_copy(pairs, pairs, t_send.at[3]).wait()


def coastal(n, child_rows, win, frame, halo, old, now, depth, mid, end):
    f32 = jnp.float32
    anywhere = pl.BlockSpec(memory_space=pl.ANY)
    grid_shape = (NCHILD, 3, C_ROWS, C_COLS)
    wide_shape = (NCHILD, 3, C_ROWS, PADDED)
    ocean_rows = n * P_ROWS
    dma = pltpu.SemaphoreType.DMA
    return pl.pallas_call(
        functools.partial(coastal_kernel, n),
        out_shape=[jax.ShapeDtypeStruct(grid_shape, f32)] * 3
        + [
            jax.ShapeDtypeStruct((n, 1, TILE), f32),
            jax.ShapeDtypeStruct((BACK, 8, 2, TILE), f32),
            jax.ShapeDtypeStruct(halo.shape, f32),
        ],
        in_specs=[pl.BlockSpec(memory_space=pltpu.SMEM)] + [anywhere] * 8,
        out_specs=[anywhere] * 6,
        scratch_shapes=[
            pltpu.VMEM(grid_shape, f32),
            pltpu.VMEM(wide_shape, f32),
            pltpu.VMEM(wide_shape, f32),
            pltpu.VMEM((NCHILD, C_ROWS, PADDED), f32),
            pltpu.VMEM(grid_shape, f32),
            pltpu.VMEM(grid_shape, f32),
            pltpu.VMEM(wide_shape, f32),
            pltpu.VMEM(wide_shape, f32),
            pltpu.VMEM((4, NCHILD, C_ROWS, C_COLS), f32),
            pltpu.VMEM((4, NCHILD, C_ROWS, C_COLS), f32),
            pltpu.VMEM((4, NCHILD, 2, 4, C_COLS), f32),
            pltpu.VMEM((4, NCHILD, 2, 4, C_COLS), f32),
            pltpu.VMEM(win.shape, f32),
            pltpu.VMEM((P_ROWS, 1, TILE), f32),
            pltpu.VMEM((ocean_rows + 2 * EDGE, 1, TILE), f32),
            pltpu.VMEM((16, TILE), f32),
            pltpu.VMEM((ocean_rows + 2 * EDGE, 1, UNIT), f32),
            pltpu.VMEM((FOOT_ROWS, 1, UNIT), f32),
            pltpu.VMEM((6, 1, UNIT), f32),
            pltpu.VMEM((ROW_UNITS, 1, UNIT), f32),
            pltpu.VMEM((UNITS, 3, 1, UNIT), f32),
            pltpu.VMEM((2, BACK, TILE), f32),
            pltpu.VMEM((2, BACK, RATIO * TILE), f32),
            pltpu.VMEM((2, BACK, RATIO * TILE), f32),
            pltpu.VMEM((2, BACK, TILE), f32),
            pltpu.VMEM((BACK, 2, TILE), f32),
            pltpu.VMEM((2 * ocean_rows + FOOT_ROWS, 2, TILE), f32),
            pltpu.VMEM((ocean_rows + 2 * EDGE, 2, TILE), f32),
            pltpu.VMEM((NCHILD, 8, FOOT_COLS), f32),
            pltpu.VMEM((n, 1, TILE), f32),
            pltpu.VMEM((1, TILE), f32),
            dma((11,)),
            dma((4,)),
            dma((4, NCHILD, 2)),
            dma((4, NCHILD, 2)),
            dma((2,)),
            dma((2,)),
            dma((5,)),
            dma((5,)),
        ],
        compiler_params=pltpu.CompilerParams(
            collective_id=0, has_side_effects=True, vmem_limit_bytes=48 * 1024 * 1024
        ),
    )(child_rows, win, frame, halo, old, now, depth, mid, end)


def windows(parent_old, parent_now, parent_depth, cot_mid, cot_end, child_cols):
    fields = jnp.concatenate(
        [cot_end, cot_mid, parent_now, parent_old[2:], parent_depth[None]], axis=0
    )
    parts = []
    for nested in range(NCHILD):
        parts.append(lax.dynamic_slice_in_dim(fields, child_cols[nested], FOOT_COLS, 2))
    win = jnp.stack(parts, axis=1)
    win = win.reshape(FIELDS, NCHILD, P_ROWS, FOOT_COLS // UNIT, UNIT)
    win = jnp.transpose(win, (0, 1, 3, 2, 4)).reshape(UNITS, P_ROWS, 1, UNIT)
    padded = jnp.pad(parent_now, ((0, 0), (0, 0), (1, 1)))
    packet = []
    for nested in range(NCHILD):
        for column in (child_cols[nested] - 1, child_cols[nested] + FOOT_COLS):
            around = lax.dynamic_slice_in_dim(padded, column, 3, 2)
            packet.append(jnp.transpose(around, (1, 0, 2)).reshape(P_ROWS, 9))
            for array in (parent_old, parent_depth[None], cot_end):
                packet.append(jnp.transpose(lax.dynamic_slice_in_dim(array, column, 1, 2)[..., 0]))
    return win, jnp.concatenate(packet, axis=1).reshape(P_ROWS, 1, TILE)


def dx(field):
    padded = jnp.pad(field, [(0, 0)] * (field.ndim - 1) + [(1, 1)])
    return padded[..., 2:] - padded[..., :-2]


def dy(field):
    padded = jnp.pad(field, [(0, 0)] * (field.ndim - 2) + [(1, 1), (0, 0)])
    return padded[..., 2:, :] - padded[..., :-2, :]


def step(old, state, depth):
    e, u, v = state
    return jnp.stack(
        [
            old[0] - HALF * (depth * (dx(u) + dy(v)) + dx(e * u) + dy(e * v)),
            old[1] - HALF * (u * dx(u) + v * dy(u) + dx(e)) - DRAG * u,
            old[2] - HALF * (u * dx(v) + v * dy(v) + dy(e)) - DRAG * v,
        ]
    )


def pull(state, cots, depth):
    e, u, v = state
    ae, au, av = [HALF * cots[i] for i in range(3)]
    xe, ye = dx(ae), dy(ae)
    return jnp.stack(
        [
            u * xe + v * ye + dx(au) + dy(av),
            dx(depth * ae + u * au) + dy(v * au) + e * xe - dx(u) * au - dx(v) * av - 0.1 * au,
            dy(depth * ae + v * av) + dx(u * av) + e * ye - dy(u) * au - dy(v) * av - 0.1 * av,
        ]
    )


def ocean(n, halo, own, edges, back, child_rows, child_cols):
    me = lax.axis_index("rows")
    before = jnp.where(me > 0, halo[0], 0.0).reshape(13, 3, P_COLS)
    after = jnp.where(me < n - 1, halo[1], 0.0).reshape(13, 3, P_COLS)
    tall = jnp.concatenate([before, own, after], axis=1)
    old, now, depth, mid, end = tall[0:3], tall[3:6], tall[6], tall[7:10], tall[10:13]
    row = me * P_ROWS - 3 + jnp.arange(10)
    inside = ((row >= 0) & (row < n * P_ROWS))[:, None]
    column = jnp.arange(P_COLS)[None, :]
    back = jnp.transpose(back.reshape(NCHILD, 3, 4, 8, 2, TILE), (4, 0, 1, 3, 2, 5)).reshape(
        2, NCHILD, 3, 8, FOOT_COLS
    )
    back = jnp.pad(back, ((0, 0), (0, 0), (0, 0), (1, 1), (0, 0)))
    covered = jnp.zeros((10, P_COLS), bool)
    means = [jnp.zeros((3, 10, P_COLS), jnp.float32) for _ in range(2)]
    extra = [jnp.zeros((3, 10, P_COLS), jnp.float32) for _ in range(2)]
    for nested in range(NCHILD):
        foot = row - child_rows[nested]
        in_rows = ((foot >= 0) & (foot < FOOT_ROWS))[:, None]
        left = child_cols[nested]
        covered = covered | (in_rows & (column >= left) & (column < left + FOOT_COLS))
        for which in range(2):
            means[which] = lax.dynamic_update_slice_in_dim(means[which], back[which, nested], left, 2)
        line = edges[jnp.clip(foot, 0, FOOT_ROWS - 1), 0]
        line = jnp.where(in_rows, line, 0.0)
        for side, at in ((0, left - 1), (1, left + FOOT_COLS)):
            for which in range(2):
                first = nested * 16 + side * 8 + 3 * which
                cells = jnp.transpose(line[:, first : first + 3])[:, :, None]
                extra[which] = jnp.where(column == at, cells, extra[which])
    raw2 = jnp.where(inside, step(old, now, depth), 0.0)
    state2 = jnp.where(covered, means[0], raw2)
    state3 = jnp.where(covered, means[1], step(now, state2, depth))
    cot3 = jnp.where(covered, 0.0, end)
    cot2 = mid + pull(state2, cot3, depth) + extra[0]
    cot2 = jnp.where(covered | ~inside, 0.0, cot2)
    cot1 = cot3 + pull(now, cot2, depth) + extra[1]
    mine = slice(3, 3 + P_ROWS)
    return state3[:, mine], cot2[:, mine], cot1[:, mine]


def shards(
    n,
    parent_old,
    parent_now,
    child_old,
    child_now,
    parent_depth,
    child_depth,
    child_rows,
    child_cols,
    parent_cot_mid,
    parent_cot_end,
    child_cot_mid,
    child_cot_end,
):
    win, frame = windows(parent_old, parent_now, parent_depth, parent_cot_mid, parent_cot_end, child_cols)
    own = jnp.concatenate(
        [parent_old, parent_now, parent_depth[None], parent_cot_mid, parent_cot_end], axis=0
    )
    halo = jnp.stack([own[:, 0:3], own[:, 1:4]]).reshape(2, 39, P_COLS)
    child_end, child_gold, child_gnow, edges, back, halos = coastal(
        n, child_rows, win, frame, halo, child_old, child_now, child_depth, child_cot_mid, child_cot_end
    )
    parent_end, parent_gold, parent_gnow = ocean(n, halos, own, edges, back, child_rows, child_cols)
    return (parent_end, child_end, parent_gold, parent_gnow, child_gold, child_gnow)


def solution(mesh):
    ocean_spec = P(None, "rows", None)
    coast_spec = P(None, None, "rows", None)
    return jax.shard_map(
        functools.partial(shards, mesh.shape["rows"]),
        mesh=mesh,
        in_specs=(
            ocean_spec,
            ocean_spec,
            coast_spec,
            coast_spec,
            P("rows", None),
            P(None, "rows", None),
            P(),
            P(),
            ocean_spec,
            ocean_spec,
            coast_spec,
            coast_spec,
        ),
        out_specs=(ocean_spec, coast_spec, ocean_spec, ocean_spec, coast_spec, coast_spec),
        check_vma=False,
    )
```

```python
import functools

import jax
import jax.numpy as jnp
from jax import lax
from jax.experimental import pallas as pl
from jax.experimental.pallas import tpu as pltpu
from jax.sharding import PartitionSpec as P

MESH = pl.DeviceIdType.MESH
P_ROWS = 4
P_COLS = 8192
C_ROWS = 8
C_COLS = 4096
NCHILD = 4
RATIO = 8
FOOT_ROWS = 128
FOOT_COLS = 512
BAND = 2048
TILE = 128
PADDED = C_COLS + 2 * TILE
CHUNK = 512
HALF = 0.15
DRAG = 0.015
FIELDS = 11
UNIT = 256
UNITS = FIELDS * NCHILD * (FOOT_COLS // UNIT)
ROW_UNITS = 6 * NCHILD * (FOOT_COLS // UNIT)
BACK = 3 * NCHILD * (FOOT_COLS // TILE)
BACK_FIRST = 80
EDGE = 8


def column_shifts(wide, width):
    ahead = pltpu.roll(wide, wide.shape[1] - 1, 1)[:, TILE : TILE + width]
    behind = pltpu.roll(wide, 1, 1)[:, TILE : TILE + width]
    return ahead, behind


def row_shifts(block, before, after):
    row = lax.broadcasted_iota(jnp.int32, block.shape, 0)
    ahead = jnp.where(row == C_ROWS - 1, after, pltpu.roll(block, C_ROWS - 1, 0))
    behind = jnp.where(row == 0, before, pltpu.roll(block, 1, 0))
    return ahead, behind


def rates(shifted, bed):
    (e, ee, ew, en, es), (u, ue, uw, un, us), (v, ve, vw, vn, vs) = shifted
    ux, uy, vx, vy = ue - uw, un - us, ve - vw, vn - vs
    changes = (
        HALF * (bed * (ux + vy) + (ee * ue - ew * uw) + (en * vn - es * vs)),
        HALF * (u * ux + v * uy + (ee - ew)) + DRAG * u,
        HALF * (u * vx + v * vy + (en - es)) + DRAG * v,
    )
    return changes, (ux, uy, vx, vy)


def pulled(wides, e, v, dy, slopes):
    wae, wau, wav, wu, wbed = wides
    width = wae.shape[1] - 2 * TILE
    ae, au, av, u, bed = [wide[:, TILE : TILE + width] for wide in wides]
    ux, uy, vx, vy = slopes

    def dx(field):
        ahead, behind = column_shifts(field, width)
        return ahead - behind

    xe, ye = dx(wae), dy(ae, 0)
    ge = u * xe + v * ye + dx(wau) + dy(av, 1)
    gu = dx(wbed * wae + wu * wau) + dy(v * au, 2) + e * xe - ux * au - vx * av - 0.1 * au
    gv = dy(bed * ae + v * av, 3) + dx(wu * wav) + e * ye - uy * au - vy * av - 0.1 * av
    return ge, gu, gv


def split3(value):
    high = value.astype(jnp.bfloat16)
    rest = value - high.astype(jnp.float32)
    mid = rest.astype(jnp.bfloat16)
    low = (rest - mid.astype(jnp.float32)).astype(jnp.bfloat16)
    return high, mid, low


def exact_dot(rows, matrix):
    return sum(jnp.dot(part, matrix, preferred_element_type=jnp.float32) for part in split3(rows))


def coastal_kernel(
    n,
    rows_smem,
    win_hbm,
    frame_hbm,
    strip0,
    strip1,
    strip2,
    strip3,
    strip4,
    old_hbm,
    now_hbm,
    depth_hbm,
    mid_hbm,
    end_hbm,
    next_out,
    gold_out,
    gnow_out,
    edge_out,
    back_out,
    halo0,
    halo1,
    halo2,
    halo3,
    halo4,
    old,
    now,
    nxt,
    depth,
    mid,
    end,
    a2,
    a1,
    slopes1,
    slopes2,
    send_rows,
    halo_rows,
    win,
    frame,
    frames,
    fvals,
    gathered,
    picked,
    special,
    rowbuf,
    specbuf,
    lhs,
    spread,
    sums,
    rest,
    pairs,
    returned,
    placed,
    qrow,
    edges,
    packet,
    load_sem,
    store_sem,
    halo_send,
    halo_recv,
    ag_send,
    ag_recv,
    t_send,
    t_recv,
    strip_send,
    strip_recv,
):
    me = lax.axis_index("rows")
    up = lax.rem(me + 1, n)
    down = lax.rem(me + n - 1, n)
    has_before = jnp.where(me > 0, 1.0, 0.0)
    has_after = jnp.where(me < n - 1, 1.0, 0.0)
    centre = pl.ds(TILE, C_COLS)

    barrier = pltpu.get_barrier_semaphore()

    def greet(j, carry):
        pl.semaphore_signal(barrier, inc=1, device_id=(lax.rem(me + j, n),), device_id_type=MESH)
        return carry

    lax.fori_loop(1, n, greet, 0)

    loads = [
        pltpu.make_async_copy(now_hbm, now.at[:, :, :, centre], load_sem.at[0]),
        pltpu.make_async_copy(old_hbm, old, load_sem.at[1]),
        pltpu.make_async_copy(depth_hbm, depth.at[:, :, centre], load_sem.at[2]),
        pltpu.make_async_copy(mid_hbm, mid, load_sem.at[3]),
        pltpu.make_async_copy(end_hbm, end, load_sem.at[4]),
        pltpu.make_async_copy(win_hbm, win, load_sem.at[5]),
        pltpu.make_async_copy(frame_hbm, frame, load_sem.at[6]),
    ]
    for load in loads:
        load.start()

    for array in (a2, a1):
        array[:, :, :, 0:TILE] = jnp.zeros((NCHILD, 3, C_ROWS, TILE), jnp.float32)
        array[:, :, :, TILE + C_COLS :] = jnp.zeros((NCHILD, 3, C_ROWS, TILE), jnp.float32)
    depth[:, :, 0:TILE] = jnp.zeros((NCHILD, C_ROWS, TILE), jnp.float32)
    depth[:, :, TILE + C_COLS :] = jnp.zeros((NCHILD, C_ROWS, TILE), jnp.float32)
    ocean_rows = n * P_ROWS
    frames[0:EDGE] = jnp.zeros((EDGE, 1, TILE), jnp.float32)
    frames[pl.ds(EDGE + ocean_rows, EDGE)] = jnp.zeros((EDGE, 1, TILE), jnp.float32)
    gathered[0:EDGE] = jnp.zeros((EDGE, 1, UNIT), jnp.float32)
    gathered[pl.ds(EDGE + ocean_rows, EDGE)] = jnp.zeros((EDGE, 1, UNIT), jnp.float32)
    qrow[...] = jnp.zeros_like(qrow)
    packet[...] = jnp.zeros_like(packet)

    loads[0].wait()
    loads[6].wait()
    for nested in range(NCHILD):
        for part in range(3):
            send_rows[0, nested, 0, part : part + 1, :] = now[nested, part, 0:1, centre]
            send_rows[0, nested, 1, part : part + 1, :] = now[nested, part, C_ROWS - 1 : C_ROWS, centre]

    pl.semaphore_wait(barrier, n - 1)

    def halo_copies(stage, nested):
        return (
            pltpu.make_async_remote_copy(
                send_rows.at[stage, nested, 0],
                halo_rows.at[stage, nested, 1],
                halo_send.at[stage, nested, 0],
                halo_recv.at[stage, nested, 1],
                device_id=(down,),
                device_id_type=MESH,
            ),
            pltpu.make_async_remote_copy(
                send_rows.at[stage, nested, 1],
                halo_rows.at[stage, nested, 0],
                halo_send.at[stage, nested, 1],
                halo_recv.at[stage, nested, 0],
                device_id=(up,),
                device_id_type=MESH,
            ),
        )

    def halo_start(stage, nested):
        for copy in halo_copies(stage, nested):
            copy.start()

    def halo_wait(stage, nested):
        for copy in halo_copies(stage, nested):
            copy.wait_recv()

    mine = pl.ds(EDGE + me * P_ROWS, P_ROWS)
    frames[mine] = frame[...]

    def send_frame(j, carry):
        pltpu.make_async_remote_copy(
            frame,
            frames.at[mine],
            ag_send.at[0],
            ag_recv.at[0],
            device_id=(lax.rem(me + j, n),),
            device_id_type=MESH,
        ).start()
        return carry

    lax.fori_loop(1, n, send_frame, 0)
    for nested in range(NCHILD):
        halo_start(0, nested)

    loads[5].wait()

    def send_unit(j, carry):
        unit = lax.rem(me + j, UNITS)

        @pl.when(unit != me)
        def _():
            pltpu.make_async_remote_copy(
                win.at[unit],
                gathered.at[mine],
                t_send.at[0],
                t_recv.at[0],
                device_id=(unit,),
                device_id_type=MESH,
            ).start()

        @pl.when(unit == me)
        def _():
            pltpu.make_async_copy(win.at[unit], gathered.at[mine], t_recv.at[0]).start()

        return carry

    lax.fori_loop(0, UNITS, send_unit, 0)

    @pl.when(me < UNITS)
    def _():
        whole = gathered.at[pl.ds(EDGE, ocean_rows)]
        pltpu.make_async_copy(whole, whole, t_recv.at[0]).wait()
        grid_index = lax.rem(me // (FOOT_COLS // UNIT), NCHILD)
        first = rows_smem[0]
        for nested in range(1, NCHILD):
            first = jnp.where(grid_index == nested, rows_smem[nested], first)
        special[0:3] = gathered[pl.ds(EDGE + first - 2, 3)]
        special[3:6] = gathered[pl.ds(EDGE + first + FOOT_ROWS - 1, 3)]

        def pick(j, carry):
            picked[j] = gathered[EDGE + first + j]
            return carry

        lax.fori_loop(0, FOOT_ROWS, pick, 0)

        for side, target in ((0, 0), (1, n - 1)):
            source = special.at[pl.ds(3 * side, 3)]

            @pl.when(me != target)
            def _():
                pltpu.make_async_remote_copy(
                    source,
                    specbuf.at[me],
                    t_send.at[1],
                    t_recv.at[1],
                    device_id=(target,),
                    device_id_type=MESH,
                ).start()

            @pl.when(me == target)
            def _():
                pltpu.make_async_copy(source, specbuf.at[me], t_recv.at[1]).start()

        @pl.when(me < ROW_UNITS)
        def _():
            def send_row(j, carry):
                target = lax.rem(me + j, n)
                pltpu.make_async_remote_copy(
                    picked.at[target],
                    rowbuf.at[me],
                    t_send.at[2],
                    t_recv.at[2],
                    device_id=(target,),
                    device_id_type=MESH,
                ).start()
                return carry

            lax.fori_loop(1, n, send_row, 0)
            pltpu.make_async_copy(picked.at[me], rowbuf.at[me], t_recv.at[2]).start()

    all_but = frames.at[pl.ds(0, (n - 1) * P_ROWS)]
    pltpu.make_async_copy(all_but, all_but, ag_recv.at[0]).wait()
    lane = lax.broadcasted_iota(jnp.int32, (1, TILE), 1)

    def lanes_of(offset):
        value = frames[EDGE + rows_smem[0] + me + offset]
        for nested in range(1, NCHILD):
            other = frames[EDGE + rows_smem[nested] + me + offset]
            value = jnp.where(lane >= 32 * nested, other, value)
        return value

    south, middle, north = lanes_of(-1), lanes_of(0), lanes_of(1)

    def lane_field(row, index):
        return row if index == 0 else pltpu.roll(row, TILE - index, 1)

    e_w, e_c, e_e = [lane_field(middle, i) for i in (0, 1, 2)]
    u_w, u_c, u_e = [lane_field(middle, i) for i in (3, 4, 5)]
    v_w, v_c, v_e = [lane_field(middle, i) for i in (6, 7, 8)]
    e_s, u_s, v_s = [lane_field(south, i) for i in (1, 4, 7)]
    e_n, u_n, v_n = [lane_field(north, i) for i in (1, 4, 7)]
    e_o, u_o, v_o, b_c, ce_c, cu_c, cv_c = [lane_field(middle, i) for i in range(9, 16)]
    e_2 = e_o - HALF * (
        b_c * ((u_e - u_w) + (v_n - v_s)) + (e_e * u_e - e_w * u_w) + (e_n * v_n - e_s * v_s)
    )
    u_2 = u_o - HALF * (u_c * (u_e - u_w) + v_c * (u_n - u_s) + (e_e - e_w)) - DRAG * u_c
    v_2 = v_o - HALF * (u_c * (v_e - v_w) + v_c * (v_n - v_s) + (e_n - e_s)) - DRAG * v_c
    for index, value in enumerate((e_c, u_c, v_c, e_2, u_2, v_2, b_c, ce_c, cu_c, cv_c)):
        fvals[index : index + 1, :] = value
    for nested in range(NCHILD):
        for side in range(2):
            where = 32 * nested + 16 * side
            lanes = slice(0, TILE) if side == 0 else slice(TILE + C_COLS, PADDED)
            for part in range(3):
                for base, array in ((0, now), (3, nxt)):
                    cell = fvals[base + part : base + part + 1, where : where + 1]
                    array[nested, part, :, lanes] = jnp.broadcast_to(cell, (C_ROWS, TILE))

    def forward(stage, nested, state, base, target, slopes):
        def chunk(j, carry):
            here = pl.multiple_of(j * CHUNK, CHUNK)
            wide = pl.ds(here, CHUNK + 2 * TILE)
            plain = pl.ds(here, CHUNK)
            inner = pl.ds(here + TILE, CHUNK)
            shifted = []
            for part in range(3):
                block = state[nested, part, :, wide]
                mid_block = block[:, TILE : TILE + CHUNK]
                before = halo_rows[stage, nested, 0, part : part + 1, plain] * has_before
                after = halo_rows[stage, nested, 1, part : part + 1, plain] * has_after
                shifted.append(
                    (mid_block,) + column_shifts(block, CHUNK) + row_shifts(mid_block, before, after)
                )
            changes, found = rates(shifted, depth[nested, :, inner])
            for index, slope in enumerate(found):
                slopes[index, nested, :, plain] = slope
            bases = [base(part, inner, plain) for part in range(3)]
            news = [start - change for start, change in zip(bases, changes)]
            for part in range(3):
                target(part, inner, plain, news[part], j)
            return carry

        lax.fori_loop(0, C_COLS // CHUNK, chunk, 0)

    def add_sums(which, nested, part, value, j):
        row = (nested * 3 + part) * 4 + j // 2
        sums[which, pl.ds(row, 1), pl.ds(pl.multiple_of(lax.rem(j, 2) * CHUNK, CHUNK), CHUNK)] = (
            jnp.sum(value, axis=0, keepdims=True)
        )

    def stage_a(nested, carry):
        halo_wait(0, nested)

        def target(part, inner, plain, value, j):
            nxt[nested, part, :, inner] = value
            send_rows[1, nested, 0, part : part + 1, plain] = value[0:1]
            send_rows[1, nested, 1, part : part + 1, plain] = value[C_ROWS - 1 :]
            add_sums(0, nested, part, value, j)

        forward(0, nested, now, lambda part, inner, plain: old[nested, part, :, plain], target, slopes1)
        halo_start(1, nested)
        return carry

    for index in (1, 2, 3, 4):
        loads[index].wait()
    lax.fori_loop(0, NCHILD, stage_a, 0)

    def stage_b(nested, carry):
        halo_wait(1, nested)

        def target(part, inner, plain, value, j):
            old[nested, part, :, plain] = value
            add_sums(1, nested, part, value, j)

        forward(1, nested, nxt, lambda part, inner, plain: now[nested, part, :, inner], target, slopes2)
        return carry

    lax.fori_loop(0, NCHILD, stage_b, 0)
    store_next = pltpu.make_async_copy(old, next_out, store_sem.at[0])
    store_next.start()

    fine = lax.broadcasted_iota(jnp.int32, (RATIO * TILE, TILE), 0) // RATIO
    coarse = lax.broadcasted_iota(jnp.int32, (RATIO * TILE, TILE), 1)
    gather_matrix = jnp.where(fine == coarse, 1.0 / (RATIO * RATIO), 0.0).astype(jnp.bfloat16)
    fine_t = lax.broadcasted_iota(jnp.int32, (TILE, RATIO * TILE), 1) // RATIO
    coarse_t = lax.broadcasted_iota(jnp.int32, (TILE, RATIO * TILE), 0)
    spread_matrix = jnp.where(fine_t == coarse_t, 1.0 / (RATIO * RATIO), 0.0).astype(jnp.bfloat16)
    for which in range(2):
        rest[which] = exact_dot(sums[which], gather_matrix)
    for unit in range(BACK):
        for which in range(2):
            pairs[unit, which : which + 1, :] = rest[which, unit : unit + 1, :]

    span = FOOT_ROWS
    pad = ocean_rows
    returned[0:pad] = jnp.zeros((pad, 2, TILE), jnp.float32)
    returned[pl.ds(pad + span, pad)] = jnp.zeros((pad, 2, TILE), jnp.float32)

    def send_back(j, carry):
        unit = lax.rem(me + j, BACK)
        owner = unit + BACK_FIRST

        @pl.when(owner != me)
        def _():
            pltpu.make_async_remote_copy(
                pairs.at[unit],
                returned.at[pad + me],
                t_send.at[3],
                t_recv.at[3],
                device_id=(owner,),
                device_id_type=MESH,
            ).start()

        @pl.when(owner == me)
        def _():
            pltpu.make_async_copy(pairs.at[unit], returned.at[pad + me], t_recv.at[3]).start()

        return carry

    lax.fori_loop(0, BACK, send_back, 0)

    all_rows = rowbuf.at[pl.ds(0, ROW_UNITS)]
    pltpu.make_async_copy(all_rows, all_rows, t_recv.at[2]).wait()
    parts_of = FOOT_COLS // UNIT
    for which in range(2):
        for nested in range(NCHILD):
            for part in range(3):
                for half in range(parts_of):
                    unit = ((3 * which + part) * NCHILD + nested) * parts_of + half
                    for piece in range(UNIT // TILE):
                        row = (nested * 3 + part) * 4 + half * (UNIT // TILE) + piece
                        lhs[which, row : row + 1, :] = rowbuf[unit, :, TILE * piece : TILE * (piece + 1)]
    spread[0] = exact_dot(lhs[0], spread_matrix)

    def spread_at(which, nested, part, j):
        row = (nested * 3 + part) * 4 + j // 2
        return spread[which, pl.ds(row, 1), pl.ds(pl.multiple_of(lax.rem(j, 2) * CHUNK, CHUNK), CHUNK)]

    def put_products(stage, nested, plain, bed, v, ae, au, av):
        for index, value in enumerate((ae, av, v * au, bed * ae + v * av)):
            send_rows[stage, nested, 0, index : index + 1, plain] = value[0:1]
            send_rows[stage, nested, 1, index : index + 1, plain] = value[C_ROWS - 1 :]

    def stage_c(nested, carry):
        def chunk(j, inner_carry):
            here = pl.multiple_of(j * CHUNK, CHUNK)
            plain = pl.ds(here, CHUNK)
            inner = pl.ds(here + TILE, CHUNK)
            scaled = []
            for part in range(3):
                total = end[nested, part, :, plain] + spread_at(0, nested, part, j)
                end[nested, part, :, plain] = total
                scaled.append(HALF * total)
                a2[nested, part, :, inner] = scaled[-1]
            put_products(2, nested, plain, depth[nested, :, inner], nxt[nested, 2, :, inner], *scaled)
            return inner_carry

        lax.fori_loop(0, C_COLS // CHUNK, chunk, 0)
        halo_start(2, nested)
        return carry

    lax.fori_loop(0, NCHILD, stage_c, 0)

    @pl.when((me == 0) | (me == n - 1))
    def _():
        all_special = specbuf.at[pl.ds(0, UNITS)]
        pltpu.make_async_copy(all_special, all_special, t_recv.at[1]).wait()
        sign = jnp.where(me == 0, -1.0, 1.0)
        offset = jnp.where(me == 0, -1, 1)
        wide_lane = lax.broadcasted_iota(jnp.int32, (1, FOOT_COLS), 1)
        for nested in range(NCHILD):

            def line(field, row):
                unit = (field * NCHILD + nested) * parts_of
                return jnp.concatenate([specbuf[unit + half, row] for half in range(parts_of)], axis=1)

            ce, cu, cv = [HALF * line(field, 1) for field in range(3)]
            u1, v1 = line(7, 1), line(8, 1)
            side_row = frames[EDGE + rows_smem[nested] + me + offset]
            west = side_row[:, 32 * nested + 7 : 32 * nested + 8]
            east = side_row[:, 32 * nested + 23 : 32 * nested + 24]
            v_east = jnp.where(
                wide_lane == FOOT_COLS - 1, east, pltpu.roll(v1, FOOT_COLS - 1, 1)
            )
            v_west = jnp.where(wide_lane == 0, west, pltpu.roll(v1, 1, 1))
            v2 = (
                line(9, 1)
                - HALF
                * (
                    u1 * (v_east - v_west)
                    + v1 * (line(8, 2) - line(8, 0))
                    + (line(6, 2) - line(6, 0))
                )
                - DRAG * v1
            )
            e_q, v_q = [
                jnp.concatenate(
                    [rest[0, (nested * 3 + part) * 4 + q : (nested * 3 + part) * 4 + q + 1, :] for q in range(4)],
                    axis=1,
                )
                for part in (0, 2)
            ]
            qrow[nested, 0:1, :] = sign * (v_q * ce + cv)
            qrow[nested, 1:2, :] = sign * (v2 * cu)
            qrow[nested, 2:3, :] = sign * (line(10, 1) * ce + v2 * cv + e_q * ce)

    for nested in range(NCHILD):
        row0 = nested * 12
        for side in range(2):
            sign = -1.0 if side == 0 else 1.0
            where = 32 * nested + 16 * side
            cell = 0 if side == 0 else TILE - 1
            chunk_row = 0 if side == 0 else 3
            u2, bed, ce, cu, cv = [fvals[i : i + 1, where : where + 1] for i in (4, 6, 7, 8, 9)]
            ce, cu, cv = HALF * ce, HALF * cu, HALF * cv
            e_q = rest[0, row0 + chunk_row : row0 + chunk_row + 1, cell : cell + 1]
            u_q = rest[0, row0 + 4 + chunk_row : row0 + 5 + chunk_row, cell : cell + 1]
            adds = (
                sign * (u_q * ce + cu),
                sign * (bed * ce + u2 * cu + e_q * ce),
                sign * (u2 * cv),
            )
            for part in range(3):
                row = row0 + 4 * part + chunk_row
                lhs[1, row : row + 1, :] += jnp.where(lane == cell, adds[part], 0.0)
        for part in range(3):
            for q in range(4):
                row = row0 + 4 * part + q
                lhs[1, row : row + 1, :] += qrow[nested, part : part + 1, TILE * q : TILE * (q + 1)]
    spread[1] = exact_dot(lhs[1], spread_matrix)

    def adjoint(stage, nested, state, cots, slopes, target):
        def chunk(j, carry):
            here = pl.multiple_of(j * CHUNK, CHUNK)
            wide = pl.ds(here, CHUNK + 2 * TILE)
            plain = pl.ds(here, CHUNK)
            inner = pl.ds(here + TILE, CHUNK)
            wides = [cots[nested, part, :, wide] for part in range(3)]
            wides += [state[nested, 1, :, wide], depth[nested, :, wide]]
            e, v = state[nested, 0, :, inner], state[nested, 2, :, inner]

            def dy(field, index):
                before = halo_rows[stage, nested, 0, index : index + 1, plain] * has_before
                after = halo_rows[stage, nested, 1, index : index + 1, plain] * has_after
                ahead, behind = row_shifts(field, before, after)
                return ahead - behind

            grads = pulled(wides, e, v, dy, [slopes[i, nested, :, plain] for i in range(4)])
            target(inner, plain, j, grads)
            return carry

        lax.fori_loop(0, C_COLS // CHUNK, chunk, 0)

    def frame_cots(nested, state, cots, first):
        for side in range(2):
            near = pl.ds(TILE, TILE) if side == 0 else pl.ds(C_COLS, TILE)
            far = pl.ds(0, TILE) if side == 0 else pl.ds(TILE + C_COLS, TILE)
            cell = 0 if side == 0 else TILE - 1
            sign = 1.0 if side == 0 else -1.0
            ae, au, av = [cots[nested, part, :, near] for part in range(3)]
            u, bed = state[nested, 1, :, near], depth[nested, :, near]
            ef, uf = state[nested, 0, :, far], state[nested, 1, :, far]
            values = (uf * ae + au, bed * ae + u * au + ef * ae, u * av)
            for part in range(3):
                column = sign * jnp.sum(values[part], axis=0, keepdims=True)[:, cell : cell + 1]
                packet[...] = jnp.where(
                    lane == nested * 16 + side * 8 + first + part, column, packet[...]
                )

    def stage_d(nested, carry):
        halo_wait(2, nested)

        def target(inner, plain, j, grads):
            scaled = []
            for part in range(3):
                total = mid[nested, part, :, plain] + grads[part] + spread_at(1, nested, part, j)
                mid[nested, part, :, plain] = total
                scaled.append(HALF * total)
                a1[nested, part, :, inner] = scaled[-1]
            put_products(3, nested, plain, depth[nested, :, inner], now[nested, 2, :, inner], *scaled)

        adjoint(2, nested, nxt, a2, slopes2, target)
        halo_start(3, nested)
        frame_cots(nested, nxt, a2, 0)
        return carry

    lax.fori_loop(0, NCHILD, stage_d, 0)
    store_gold = pltpu.make_async_copy(mid, gold_out, store_sem.at[1])
    store_gold.start()

    def stage_e1(nested, carry):
        frame_cots(nested, now, a1, 3)
        return carry

    lax.fori_loop(0, NCHILD, stage_e1, 0)

    edges[me] = packet[...]

    def send_edge(j, carry):
        pltpu.make_async_remote_copy(
            packet,
            edges.at[me],
            ag_send.at[1],
            ag_recv.at[1],
            device_id=(lax.rem(me + j, n),),
            device_id_type=MESH,
        ).start()
        return carry

    lax.fori_loop(1, n, send_edge, 0)

    @pl.when(me >= BACK_FIRST)
    def _():
        all_back = returned.at[pl.ds(pad, span)]
        pltpu.make_async_copy(all_back, all_back, t_recv.at[3]).wait()
        grid_index = (me - BACK_FIRST) // 12
        first = rows_smem[0]
        for nested in range(1, NCHILD):
            first = jnp.where(grid_index == nested, rows_smem[nested], first)
        placed[0:EDGE] = jnp.zeros((EDGE, 2, TILE), jnp.float32)
        placed[pl.ds(EDGE + ocean_rows, EDGE)] = jnp.zeros((EDGE, 2, TILE), jnp.float32)

        def place(j, carry):
            placed[EDGE + j] = returned[pad + j - first]
            return carry

        lax.fori_loop(0, ocean_rows, place, 0)

        def send_placed(j, carry):
            target = lax.rem(me + j, n)
            pltpu.make_async_remote_copy(
                placed.at[pl.ds(EDGE + target * P_ROWS - 2, 8)],
                back_out.at[me - BACK_FIRST],
                t_send.at[4],
                t_recv.at[4],
                device_id=(target,),
                device_id_type=MESH,
            ).start()
            return carry

        lax.fori_loop(1, n, send_placed, 0)
        pltpu.make_async_copy(
            placed.at[pl.ds(EDGE + me * P_ROWS - 2, 8)], back_out.at[me - BACK_FIRST], t_recv.at[4]
        ).start()

    ocean_copies = []
    for index, (strip, halo) in enumerate(
        zip((strip0, strip1, strip2, strip3, strip4), (halo0, halo1, halo2, halo3, halo4))
    ):
        for side, target in ((0, up), (1, down)):
            ocean_copies.append(
                pltpu.make_async_remote_copy(
                    strip,
                    halo.at[side],
                    strip_send.at[index, side],
                    strip_recv.at[index, side],
                    device_id=(target,),
                    device_id_type=MESH,
                )
            )
            ocean_copies[-1].start()

    def stage_e(nested, carry):
        halo_wait(3, nested)

        def target(inner, plain, j, grads):
            for part in range(3):
                end[nested, part, :, plain] = end[nested, part, :, plain] + grads[part]

        adjoint(3, nested, now, a1, slopes1, target)
        return carry

    lax.fori_loop(0, NCHILD, stage_e, 0)
    store_gnow = pltpu.make_async_copy(end, gnow_out, store_sem.at[2])
    store_gnow.start()

    all_edges = edges.at[pl.ds(0, n - 1)]
    pltpu.make_async_copy(all_edges, all_edges, ag_recv.at[1]).wait()
    store_edges = pltpu.make_async_copy(edges, edge_out, store_sem.at[3])
    store_edges.start()

    for copy in ocean_copies:
        copy.wait()
    pltpu.make_async_copy(back_out, back_out, t_recv.at[4]).wait()
    for store in (store_next, store_gold, store_gnow, store_edges):
        store.wait()

    pltpu.make_async_copy(all_but, all_but, ag_send.at[0]).wait()
    pltpu.make_async_copy(all_edges, all_edges, ag_send.at[1]).wait()

    def drain_halo(nested, carry):
        for stage in range(4):
            for copy in halo_copies(stage, nested):
                copy.wait_send()
        return carry

    lax.fori_loop(0, NCHILD, drain_halo, 0)

    @pl.when(me < UNITS)
    def _():
        sent = win.at[pl.ds(0, UNITS - 1)]
        pltpu.make_async_copy(sent, sent, t_send.at[0]).wait()
        for target in (0, n - 1):

            @pl.when(me != target)
            def _():
                one = special.at[pl.ds(0, 3)]
                pltpu.make_async_copy(one, one, t_send.at[1]).wait()

    @pl.when(me >= UNITS)
    def _():
        pltpu.make_async_copy(win, win, t_send.at[0]).wait()

    @pl.when(me < ROW_UNITS)
    def _():
        sent = picked.at[pl.ds(0, n - 1)]
        pltpu.make_async_copy(sent, sent, t_send.at[2]).wait()

    @pl.when(me >= BACK_FIRST)
    def _():
        sent = pairs.at[pl.ds(0, BACK - 1)]
        pltpu.make_async_copy(sent, sent, t_send.at[3]).wait()
        gone = returned.at[pl.ds(0, (n - 1) * 8)]
        pltpu.make_async_copy(gone, gone, t_send.at[4]).wait()

    @pl.when(me < BACK_FIRST)
    def _():
        pltpu.make_async_copy(pairs, pairs, t_send.at[3]).wait()


def coastal(n, child_rows, win, frame, strips, old, now, depth, mid, end):
    f32 = jnp.float32
    anywhere = pl.BlockSpec(memory_space=pl.ANY)
    grid_shape = (NCHILD, 3, C_ROWS, C_COLS)
    wide_shape = (NCHILD, 3, C_ROWS, PADDED)
    ocean_rows = n * P_ROWS
    dma = pltpu.SemaphoreType.DMA
    return pl.pallas_call(
        functools.partial(coastal_kernel, n),
        out_shape=[jax.ShapeDtypeStruct(grid_shape, f32)] * 3
        + [
            jax.ShapeDtypeStruct((n, 1, TILE), f32),
            jax.ShapeDtypeStruct((BACK, 8, 2, TILE), f32),
        ]
        + [jax.ShapeDtypeStruct((2,) + strip.shape, f32) for strip in strips],
        in_specs=[pl.BlockSpec(memory_space=pltpu.SMEM)] + [anywhere] * 12,
        out_specs=[anywhere] * 10,
        scratch_shapes=[
            pltpu.VMEM(grid_shape, f32),
            pltpu.VMEM(wide_shape, f32),
            pltpu.VMEM(wide_shape, f32),
            pltpu.VMEM((NCHILD, C_ROWS, PADDED), f32),
            pltpu.VMEM(grid_shape, f32),
            pltpu.VMEM(grid_shape, f32),
            pltpu.VMEM(wide_shape, f32),
            pltpu.VMEM(wide_shape, f32),
            pltpu.VMEM((4, NCHILD, C_ROWS, C_COLS), f32),
            pltpu.VMEM((4, NCHILD, C_ROWS, C_COLS), f32),
            pltpu.VMEM((4, NCHILD, 2, 4, C_COLS), f32),
            pltpu.VMEM((4, NCHILD, 2, 4, C_COLS), f32),
            pltpu.VMEM(win.shape, f32),
            pltpu.VMEM((P_ROWS, 1, TILE), f32),
            pltpu.VMEM((ocean_rows + 2 * EDGE, 1, TILE), f32),
            pltpu.VMEM((16, TILE), f32),
            pltpu.VMEM((ocean_rows + 2 * EDGE, 1, UNIT), f32),
            pltpu.VMEM((FOOT_ROWS, 1, UNIT), f32),
            pltpu.VMEM((6, 1, UNIT), f32),
            pltpu.VMEM((ROW_UNITS, 1, UNIT), f32),
            pltpu.VMEM((UNITS, 3, 1, UNIT), f32),
            pltpu.VMEM((2, BACK, TILE), f32),
            pltpu.VMEM((2, BACK, RATIO * TILE), f32),
            pltpu.VMEM((2, BACK, RATIO * TILE), f32),
            pltpu.VMEM((2, BACK, TILE), f32),
            pltpu.VMEM((BACK, 2, TILE), f32),
            pltpu.VMEM((2 * ocean_rows + FOOT_ROWS, 2, TILE), f32),
            pltpu.VMEM((ocean_rows + 2 * EDGE, 2, TILE), f32),
            pltpu.VMEM((NCHILD, 8, FOOT_COLS), f32),
            pltpu.VMEM((n, 1, TILE), f32),
            pltpu.VMEM((1, TILE), f32),
            dma((7,)),
            dma((4,)),
            dma((4, NCHILD, 2)),
            dma((4, NCHILD, 2)),
            dma((2,)),
            dma((2,)),
            dma((5,)),
            dma((5,)),
            dma((5, 2)),
            dma((5, 2)),
        ],
        compiler_params=pltpu.CompilerParams(
            collective_id=0, has_side_effects=True, vmem_limit_bytes=48 * 1024 * 1024
        ),
    )(child_rows, win, frame, *strips, old, now, depth, mid, end)


def window_kernel(cols, old, now, depth, mid, end, win, frame):
    lane = lax.broadcasted_iota(jnp.int32, (P_ROWS, TILE), 1)
    packet = jnp.zeros((P_ROWS, TILE), jnp.float32)
    reach = FOOT_COLS + 2 * TILE
    halves = FOOT_COLS // UNIT
    for nested in range(NCHILD):
        left = cols[nested]
        start = jnp.clip((left - 2) // TILE * TILE, 0, P_COLS - reach)
        start = pl.multiple_of(start, TILE)
        shift = reach - (left - start)

        def turned(ref, part):
            if part is None:
                block = ref[:, pl.ds(start, reach)]
            else:
                block = ref[part, :, pl.ds(start, reach)]
            return pltpu.roll(block, shift, 1)

        lists = [(end, i) for i in range(3)] + [(mid, i) for i in range(3)]
        lists += [(now, i) for i in range(3)] + [(old, 2), (depth, None), (old, 0), (old, 1)]
        blocks = [turned(*item) for item in lists]
        for field in range(FIELDS):
            for half in range(halves):
                unit = (field * NCHILD + nested) * halves + half
                for row in range(P_ROWS):
                    win[unit, row] = blocks[field][row : row + 1, half * UNIT : (half + 1) * UNIT]
        first_ok = jnp.where(left >= 2, 1.0, 0.0)
        last_ok = jnp.where(left + FOOT_COLS + 1 < P_COLS, 1.0, 0.0)
        for side, lanes in enumerate(((reach - 2, reach - 1, 0), (FOOT_COLS - 1, FOOT_COLS, FOOT_COLS + 1))):
            cells = []
            for part in range(3):
                for which, at in enumerate(lanes):
                    cell = blocks[6 + part][:, at : at + 1]
                    if side == 0 and which == 0:
                        cell = cell * first_ok
                    if side == 1 and which == 2:
                        cell = cell * last_ok
                    cells.append(cell)
            at = lanes[1]
            for index in (11, 12, 9, 10, 0, 1, 2):
                cells.append(blocks[index][:, at : at + 1])
            for index, cell in enumerate(cells):
                packet = jnp.where(lane == 32 * nested + 16 * side + index, cell, packet)
    for row in range(P_ROWS):
        frame[row] = packet[row : row + 1]


def windows(old, now, depth, mid, end, child_cols):
    f32 = jnp.float32
    return pl.pallas_call(
        window_kernel,
        out_shape=[
            jax.ShapeDtypeStruct((UNITS, P_ROWS, 1, UNIT), f32),
            jax.ShapeDtypeStruct((P_ROWS, 1, TILE), f32),
        ],
        in_specs=[pl.BlockSpec(memory_space=pltpu.SMEM)] + [pl.BlockSpec(memory_space=pltpu.VMEM)] * 5,
        out_specs=[pl.BlockSpec(memory_space=pltpu.VMEM)] * 2,
        compiler_params=pltpu.CompilerParams(vmem_limit_bytes=32 * 1024 * 1024),
    )(child_cols, old, now, depth, mid, end)


def ocean_kernel(
    n,
    rows,
    cols,
    edges,
    back,
    old,
    now,
    depth,
    mid,
    end,
    old_halo,
    now_halo,
    depth_halo,
    mid_halo,
    end_halo,
    state3,
    cot2,
    cot1,
    now8,
    depth8,
    second,
    a2,
    a1,
    slopes1,
    means,
    cells,
):
    me = lax.axis_index("rows")
    has_before = jnp.where(me > 0, 1.0, 0.0)
    has_after = jnp.where(me < n - 1, 1.0, 0.0)
    ends = (slice(0, TILE), slice(TILE + P_COLS, P_COLS + 2 * TILE))
    for array in (now8, second, a2, a1):
        for lanes in ends:
            array[:, :, lanes] = jnp.zeros((3, 8, TILE), jnp.float32)
    for lanes in ends:
        depth8[:, lanes] = jnp.zeros((8, TILE), jnp.float32)

    def tall(own, halo, part, plain):
        index = () if part is None else (part,)
        below = halo[(0,) + index + (slice(2, 4), plain)] * has_before
        above = halo[(1,) + index + (slice(0, 2), plain)] * has_after
        return jnp.concatenate([below, own[index + (slice(None), plain)], above], axis=0)

    row8 = me * P_ROWS - 2 + lax.broadcasted_iota(jnp.int32, (8, 1), 0)
    for nested in range(NCHILD):
        foot = row8 - rows[nested]
        in_rows = (foot >= 0) & (foot < FOOT_ROWS)
        lines = jnp.concatenate(
            [
                edges[jnp.clip(me * P_ROWS - 2 + t - rows[nested], 0, FOOT_ROWS - 1)]
                for t in range(8)
            ],
            axis=0,
        )
        lines = jnp.where(in_rows, lines, 0.0)
        for side in range(2):
            for which in range(2):
                for part in range(3):
                    at = nested * 16 + side * 8 + 3 * which + part
                    cells[nested, side, which, part] = jnp.broadcast_to(lines[:, at : at + 1], (8, TILE))
        shift = cols[nested] - nested * BAND
        band = slice(nested * BAND, (nested + 1) * BAND)
        for which in range(2):
            for part in range(3):
                pieces = [back[(nested * 3 + part) * 4 + q, :, which, :] for q in range(4)]
                pieces.append(jnp.zeros((8, BAND - FOOT_COLS), jnp.float32))
                means[which, part, :, band] = pltpu.roll(jnp.concatenate(pieces, axis=1), shift, 1)

    def lanes_at(j):
        here = pl.multiple_of(j * CHUNK, CHUNK)
        return pl.ds(here, CHUNK), pl.ds(here + TILE, CHUNK), pl.ds(here, CHUNK + 2 * TILE)

    def masks(j):
        nested = j // (BAND // CHUNK)
        column = j * CHUNK + lax.broadcasted_iota(jnp.int32, (8, CHUNK), 1)
        row = me * P_ROWS - 2 + lax.broadcasted_iota(jnp.int32, (8, CHUNK), 0)
        foot = row - rows[nested]
        left = cols[nested]
        covered = (foot >= 0) & (foot < FOOT_ROWS) & (column >= left) & (column < left + FOOT_COLS)
        inside = (row >= 0) & (row < n * P_ROWS)
        return covered, inside, nested, column, left

    def assemble(j, carry):
        plain, inner, wide = lanes_at(j)
        for part in range(3):
            now8[part, :, inner] = tall(now, now_halo, part, plain)
        depth8[:, inner] = tall(depth, depth_halo, None, plain)
        return carry

    chunks = P_COLS // CHUNK
    lax.fori_loop(0, chunks, assemble, 0)

    def first_step(j, carry):
        plain, inner, wide = lanes_at(j)
        covered, inside, nested, column, left = masks(j)
        shifted = []
        for part in range(3):
            block = now8[part, :, wide]
            middle = block[:, TILE : TILE + CHUNK]
            before = now_halo[0, part, 1:2, plain] * has_before
            after = now_halo[1, part, 2:3, plain] * has_after
            shifted.append((middle,) + column_shifts(block, CHUNK) + row_shifts(middle, before, after))
        changes, found = rates(shifted, depth8[:, inner])
        for index, slope in enumerate(found):
            slopes1[index, :, plain] = slope
        for part in range(3):
            raw = jnp.where(inside, tall(old, old_halo, part, plain) - changes[part], 0.0)
            second[part, :, inner] = jnp.where(covered, means[0, part, :, plain], raw)
            a2[part, :, inner] = jnp.where(covered, 0.0, HALF * tall(end, end_halo, part, plain))
        return carry

    lax.fori_loop(0, chunks, first_step, 0)

    def turn(field):
        return pltpu.roll(field, 7, 0), pltpu.roll(field, 1, 0)

    def second_step(j, carry):
        plain, inner, wide = lanes_at(j)
        covered, inside, nested, column, left = masks(j)
        shifted = []
        for part in range(3):
            block = second[part, :, wide]
            middle = block[:, TILE : TILE + CHUNK]
            shifted.append((middle,) + column_shifts(block, CHUNK) + turn(middle))
        changes, found = rates(shifted, depth8[:, inner])
        for part in range(3):
            value = jnp.where(covered, means[1, part, :, plain], now8[part, :, inner] - changes[part])
            state3[part, :, plain] = value[2:6]
        add_cots(j, second, a2, found, 0)
        return carry

    def dy(field, index):
        ahead, behind = turn(field)
        return ahead - behind

    def add_cots(j, state, cots, slopes, which):
        plain, inner, wide = lanes_at(j)
        covered, inside, nested, column, left = masks(j)
        wides = [cots[part, :, wide] for part in range(3)] + [state[1, :, wide], depth8[:, wide]]
        grads = pulled(wides, state[0, :, inner], state[2, :, inner], dy, slopes)
        for part in range(3):
            extra = jnp.where(column == left - 1, jnp.concatenate([cells[nested, 0, which, part]] * 4, axis=1), 0.0)
            extra += jnp.where(
                column == left + FOOT_COLS, jnp.concatenate([cells[nested, 1, which, part]] * 4, axis=1), 0.0
            )
            value = grads[part] + extra
            if which == 0:
                value = jnp.where(covered | ~inside, 0.0, tall(mid, mid_halo, part, plain) + value)
                cot2[part, :, plain] = value[2:6]
                a1[part, :, inner] = HALF * value
            else:
                kept = jnp.where(covered, 0.0, tall(end, end_halo, part, plain))
                cot1[part, :, plain] = (kept + value)[2:6]

    lax.fori_loop(0, chunks, second_step, 0)

    def last_step(j, carry):
        plain, inner, wide = lanes_at(j)
        add_cots(j, now8, a1, [slopes1[i, :, plain] for i in range(4)], 1)
        return carry

    lax.fori_loop(0, chunks, last_step, 0)


def ocean(n, child_rows, child_cols, edges, back, strips, halos):
    f32 = jnp.float32
    smem = pl.BlockSpec(memory_space=pltpu.SMEM)
    vmem = pl.BlockSpec(memory_space=pltpu.VMEM)
    wide = P_COLS + 2 * TILE
    return pl.pallas_call(
        functools.partial(ocean_kernel, n),
        out_shape=[jax.ShapeDtypeStruct((3, P_ROWS, P_COLS), f32)] * 3,
        in_specs=[smem] * 2 + [vmem] * 12,
        out_specs=[vmem] * 3,
        scratch_shapes=[
            pltpu.VMEM((3, 8, wide), f32),
            pltpu.VMEM((8, wide), f32),
            pltpu.VMEM((3, 8, wide), f32),
            pltpu.VMEM((3, 8, wide), f32),
            pltpu.VMEM((3, 8, wide), f32),
            pltpu.VMEM((4, 8, P_COLS), f32),
            pltpu.VMEM((2, 3, 8, P_COLS), f32),
            pltpu.VMEM((NCHILD, 2, 2, 3, 8, TILE), f32),
        ],
        compiler_params=pltpu.CompilerParams(vmem_limit_bytes=48 * 1024 * 1024),
    )(child_rows, child_cols, edges, back, *strips, *halos)


def shards(
    n,
    parent_old,
    parent_now,
    child_old,
    child_now,
    parent_depth,
    child_depth,
    child_rows,
    child_cols,
    parent_cot_mid,
    parent_cot_end,
    child_cot_mid,
    child_cot_end,
):
    strips = (parent_old, parent_now, parent_depth, parent_cot_mid, parent_cot_end)
    win, frame = windows(*strips, child_cols)
    child_end, child_gold, child_gnow, edges, back, *halos = coastal(
        n, child_rows, win, frame, strips, child_old, child_now, child_depth, child_cot_mid, child_cot_end
    )
    parent_end, parent_gold, parent_gnow = ocean(n, child_rows, child_cols, edges, back, strips, halos)
    return (parent_end, child_end, parent_gold, parent_gnow, child_gold, child_gnow)


def solution(mesh):
    ocean_spec = P(None, "rows", None)
    coast_spec = P(None, None, "rows", None)
    return jax.shard_map(
        functools.partial(shards, mesh.shape["rows"]),
        mesh=mesh,
        in_specs=(
            ocean_spec,
            ocean_spec,
            coast_spec,
            coast_spec,
            P("rows", None),
            P(None, "rows", None),
            P(),
            P(),
            ocean_spec,
            ocean_spec,
            coast_spec,
            coast_spec,
        ),
        out_specs=(ocean_spec, coast_spec, ocean_spec, ocean_spec, coast_spec, coast_spec),
        check_vma=False,
    )
```

```python
import functools

import jax
import jax.numpy as jnp
from jax import lax
from jax.experimental import pallas as pl
from jax.experimental.pallas import tpu as pltpu
from jax.sharding import PartitionSpec as P

MESH = pl.DeviceIdType.MESH
P_ROWS = 4
P_COLS = 8192
C_ROWS = 8
C_COLS = 4096
NCHILD = 4
RATIO = 8
FOOT_ROWS = 128
FOOT_COLS = 512
BAND = 2048
TILE = 128
PADDED = C_COLS + 2 * TILE
CHUNK = 512
HALF = 0.15
DRAG = 0.015
PARTS = FOOT_COLS // TILE
ROW_UNITS = 6 * NCHILD * PARTS
SIDE_UNITS = 2 * NCHILD * PARTS
SIDE_FIRST = 96
BACK = 3 * NCHILD * PARTS
BACK_FIRST = 80
EDGE = 8


def column_shifts(wide, width):
    ahead = pltpu.roll(wide, wide.shape[1] - 1, 1)[:, TILE : TILE + width]
    behind = pltpu.roll(wide, 1, 1)[:, TILE : TILE + width]
    return ahead, behind


def row_shifts(block, before, after):
    row = lax.broadcasted_iota(jnp.int32, block.shape, 0)
    ahead = jnp.where(row == C_ROWS - 1, after, pltpu.roll(block, C_ROWS - 1, 0))
    behind = jnp.where(row == 0, before, pltpu.roll(block, 1, 0))
    return ahead, behind


def moved_left(block, amount, bits):
    width = block.shape[1]
    amounts = jnp.full(block.shape, amount, jnp.int32)
    for bit in range(bits):
        block = jnp.where((amounts >> bit) & 1 == 1, pltpu.roll(block, width - (1 << bit), 1), block)
    return block


def cut_window(tiles, amount):
    shape = tiles[0].shape
    amounts = jnp.full(shape, amount, jnp.int32)
    blank = jnp.zeros(shape, jnp.float32)
    wanted = PARTS + 3
    for bit, count in ((10, wanted + 7), (9, wanted + 3), (8, wanted + 1), (7, wanted)):
        step = 1 << (bit - 7)
        chosen = (amounts >> bit) & 1 == 1
        tiles = [
            jnp.where(chosen, tiles[q + step] if q + step < len(tiles) else blank, tiles[q])
            for q in range(count)
        ]
    return moved_left(jnp.concatenate(tiles, axis=1), amount, 7)


def rates(shifted, bed):
    (e, ee, ew, en, es), (u, ue, uw, un, us), (v, ve, vw, vn, vs) = shifted
    ux, uy, vx, vy = ue - uw, un - us, ve - vw, vn - vs
    changes = (
        HALF * (bed * (ux + vy) + (ee * ue - ew * uw) + (en * vn - es * vs)),
        HALF * (u * ux + v * uy + (ee - ew)) + DRAG * u,
        HALF * (u * vx + v * vy + (en - es)) + DRAG * v,
    )
    return changes, (ux, uy, vx, vy)


def pulled(wides, e, v, dy, slopes):
    wae, wau, wav, wu, wbed = wides
    width = wae.shape[1] - 2 * TILE
    ae, au, av, u, bed = [wide[:, TILE : TILE + width] for wide in wides]
    ux, uy, vx, vy = slopes

    def dx(field):
        ahead, behind = column_shifts(field, width)
        return ahead - behind

    xe, ye = dx(wae), dy(ae, 0)
    ge = u * xe + v * ye + dx(wau) + dy(av, 1)
    gu = dx(wbed * wae + wu * wau) + dy(v * au, 2) + e * xe - ux * au - vx * av - 0.1 * au
    gv = dy(bed * ae + v * av, 3) + dx(wu * wav) + e * ye - uy * au - vy * av - 0.1 * av
    return ge, gu, gv


def split3(value):
    high = value.astype(jnp.bfloat16)
    rest = value - high.astype(jnp.float32)
    mid = rest.astype(jnp.bfloat16)
    low = (rest - mid.astype(jnp.float32)).astype(jnp.bfloat16)
    return high, mid, low


def exact_dot(rows, matrix):
    return sum(jnp.dot(part, matrix, preferred_element_type=jnp.float32) for part in split3(rows))


def coastal_kernel(n, rows_smem, cols_smem, *refs):
    strips_hbm, refs = refs[:5], refs[5:]
    old_hbm, now_hbm, depth_hbm, mid_hbm, end_hbm = refs[:5]
    next_out, gold_out, gnow_out, pend_out, pgold_out, pgnow_out = refs[5:11]
    (
        old,
        now,
        nxt,
        depth,
        mid,
        end,
        a2,
        a1,
        slopes1,
        slopes2,
        first_send,
        first_halo,
        send_rows,
        halo_rows,
        win,
        side_win,
        frame,
        frames,
        fvals,
        gathered,
        side_gathered,
        picked,
        beside,
        side_picked,
        rowbuf,
        besides,
        side_rows,
        lhs,
        spread,
        sums,
        rest,
        pairs,
        returned,
        placed,
        qrow,
        edges,
        packet,
        p_old,
        p_now,
        p_depth,
        p_mid,
        p_end,
        now8,
        depth8,
        second8,
        a28,
        a18,
        pslopes,
        means,
        cells,
        back,
        pend,
        pgold,
        pgnow,
        ocean_send,
        ocean_halo,
        load_sem,
        store_sem,
        halo_send,
        halo_recv,
        ag_send,
        ag_recv,
        t_send,
        t_recv,
        ocean_send_sem,
        ocean_recv_sem,
    ) = refs[11:]
    me = lax.axis_index("rows")
    up = lax.rem(me + 1, n)
    down = lax.rem(me + n - 1, n)
    has_before = jnp.where(me > 0, 1.0, 0.0)
    has_after = jnp.where(me < n - 1, 1.0, 0.0)
    centre = pl.ds(TILE, C_COLS)

    barrier = pltpu.get_barrier_semaphore()

    def greet(j, carry):
        pl.semaphore_signal(barrier, inc=1, device_id=(lax.rem(me + j, n),), device_id_type=MESH)
        return carry

    lax.fori_loop(1, n, greet, 0)

    strips = (p_old, p_now, p_depth, p_mid, p_end)
    loads = [
        pltpu.make_async_copy(source, target, load_sem.at[index])
        for index, (source, target) in enumerate(
            zip(
                strips_hbm + (now_hbm, depth_hbm, old_hbm, end_hbm, mid_hbm),
                strips + (now.at[:, :, :, centre], depth.at[:, :, centre], old, end, mid),
            )
        )
    ]
    for load in loads:
        load.start()

    for array in (a2, a1):
        array[:, :, :, 0:TILE] = jnp.zeros((NCHILD, 3, C_ROWS, TILE), jnp.float32)
        array[:, :, :, TILE + C_COLS :] = jnp.zeros((NCHILD, 3, C_ROWS, TILE), jnp.float32)
    depth[:, :, 0:TILE] = jnp.zeros((NCHILD, C_ROWS, TILE), jnp.float32)
    depth[:, :, TILE + C_COLS :] = jnp.zeros((NCHILD, C_ROWS, TILE), jnp.float32)
    ocean_rows = n * P_ROWS
    frames[0:EDGE] = jnp.zeros((EDGE, 1, TILE), jnp.float32)
    frames[pl.ds(EDGE + ocean_rows, EDGE)] = jnp.zeros((EDGE, 1, TILE), jnp.float32)
    for array in (gathered, side_gathered):
        array[0:EDGE] = jnp.zeros((EDGE, 1, TILE), jnp.float32)
        array[pl.ds(EDGE + ocean_rows, EDGE)] = jnp.zeros((EDGE, 1, TILE), jnp.float32)
    pad = ocean_rows
    span = FOOT_ROWS
    returned[0:pad] = jnp.zeros((pad, 2, TILE), jnp.float32)
    returned[pl.ds(pad + span, pad)] = jnp.zeros((pad, 2, TILE), jnp.float32)
    for array in (now8, second8, a28, a18):
        for lanes in (slice(0, TILE), slice(TILE + P_COLS, P_COLS + 2 * TILE)):
            array[:, :, lanes] = jnp.zeros((3, 8, TILE), jnp.float32)
        array[:, 6:8, :] = jnp.zeros((3, 2, P_COLS + 2 * TILE), jnp.float32)
    depth8[:, 0:TILE] = jnp.zeros((8, TILE), jnp.float32)
    depth8[:, TILE + P_COLS :] = jnp.zeros((8, TILE), jnp.float32)
    depth8[6:8, :] = jnp.zeros((2, P_COLS + 2 * TILE), jnp.float32)
    qrow[...] = jnp.zeros_like(qrow)
    packet[...] = jnp.zeros_like(packet)

    lane = lax.broadcasted_iota(jnp.int32, (1, TILE), 1)
    whole_ocean = pl.ds(TILE, P_COLS)

    for index in range(5):
        loads[index].wait()

    def band_tiles(nested, blocks):
        first = nested * (BAND // TILE) - 1
        tiles = []
        for q in range(first, first + BAND // TILE + 2):
            if q < 0 or q >= P_COLS // TILE:
                tiles.append(jnp.zeros((P_ROWS * len(blocks), TILE), jnp.float32))
            else:
                tiles.append(jnp.concatenate([block(q) for block in blocks], axis=0))
        return cut_window(tiles, cols_smem[nested] - nested * BAND)

    lane4 = lax.broadcasted_iota(jnp.int32, (P_ROWS, TILE), 1)
    raw_cells = jnp.zeros((P_ROWS, TILE), jnp.float32)
    for nested in range(NCHILD):
        def block_of(ref, part):
            if part is None:
                return lambda q: ref[:, TILE * q : TILE * (q + 1)]
            return lambda q: ref[part, :, TILE * q : TILE * (q + 1)]

        sources = [(p_end, 0), (p_end, 1), (p_end, 2), (p_mid, 0), (p_mid, 1), (p_mid, 2)]
        sources += [(p_now, 0), (p_now, 1), (p_now, 2), (p_old, 0), (p_old, 1), (p_old, 2), (p_depth, None)]
        blocks = []
        for first in range(0, len(sources), 2):
            pair = [block_of(*source) for source in sources[first : first + 2]]
            both = band_tiles(nested, pair)
            blocks += [both[P_ROWS * i : P_ROWS * (i + 1)] for i in range(len(pair))]
        for field in range(6):
            for piece in range(PARTS):
                unit = (field * NCHILD + nested) * PARTS + piece
                for row in range(P_ROWS):
                    win[unit, row] = blocks[field][row : row + 1, (piece + 1) * TILE : (piece + 2) * TILE]
        foot_end = TILE + FOOT_COLS
        for side, lanes in enumerate(
            ((TILE - 2, TILE - 1, TILE), (foot_end - 1, foot_end, foot_end + 1))
        ):
            found = [blocks[6 + part][:, at : at + 1] for part in range(3) for at in lanes]
            at = lanes[1]
            for index in (9, 10, 11, 12, 0, 1, 2):
                found.append(blocks[index][:, at : at + 1])
            for index, cell in enumerate(found):
                raw_cells = jnp.where(lane4 == 32 * nested + 16 * side + index, cell, raw_cells)
    for row in range(P_ROWS):
        frame[row] = raw_cells[row : row + 1]

    for side, row in ((0, 0), (1, P_ROWS - 1)):
        for part in range(3):
            ocean_send[side, part] = p_now[part, row : row + 1, :]
        ocean_send[side, 3] = p_depth[row : row + 1, :]
    loads[5].wait()
    loads[6].wait()
    for nested in range(NCHILD):
        for side, row in ((0, 0), (1, C_ROWS - 1)):
            for part in range(3):
                first_send[nested, side, part] = now[nested, part, row : row + 1, centre]
            first_send[nested, side, 3] = depth[nested, row : row + 1, centre]

    pl.semaphore_wait(barrier, n - 1)

    def remote(source, target, send, recv, device):
        return pltpu.make_async_remote_copy(
            source, target, send, recv, device_id=(device,), device_id_type=MESH
        )

    def ocean_copies(first, count, stage):
        fields = pl.ds(first, count)
        return (
            remote(
                ocean_send.at[0, fields],
                ocean_halo.at[1, fields],
                ocean_send_sem.at[stage, 0],
                ocean_recv_sem.at[stage, 1],
                down,
            ),
            remote(
                ocean_send.at[1, fields],
                ocean_halo.at[0, fields],
                ocean_send_sem.at[stage, 1],
                ocean_recv_sem.at[stage, 0],
                up,
            ),
        )

    ocean_stages = ((0, 4, 0), (4, 6, 1), (10, 3, 2))

    def ocean_start(stage):
        for copy in ocean_copies(*ocean_stages[stage]):
            copy.start()

    def ocean_wait(stage):
        for copy in ocean_copies(*ocean_stages[stage]):
            copy.wait_recv()

    def halo_copies(stage, nested):
        if stage == 0:
            sources = (first_send.at[nested, 0], first_send.at[nested, 1])
            targets = (first_halo.at[nested, 1], first_halo.at[nested, 0])
        else:
            sources = (send_rows.at[stage - 1, nested, 0], send_rows.at[stage - 1, nested, 1])
            targets = (halo_rows.at[stage - 1, nested, 1], halo_rows.at[stage - 1, nested, 0])
        return (
            remote(sources[0], targets[0], halo_send.at[stage, nested, 0], halo_recv.at[stage, nested, 1], down),
            remote(sources[1], targets[1], halo_send.at[stage, nested, 1], halo_recv.at[stage, nested, 0], up),
        )

    def halo_row(stage, nested, side, part, plain):
        kept = has_before if side == 0 else has_after
        if stage == 0:
            return first_halo[nested, side, part, :, plain] * kept
        return halo_rows[stage - 1, nested, side, part, :, plain] * kept

    def put_row(stage, nested, part, plain, value):
        send_rows[stage - 1, nested, 0, part, :, plain] = value[0:1]
        send_rows[stage - 1, nested, 1, part, :, plain] = value[C_ROWS - 1 :]

    def halo_start(stage, nested):
        for copy in halo_copies(stage, nested):
            copy.start()

    def halo_wait(stage, nested):
        for copy in halo_copies(stage, nested):
            copy.wait_recv()

    mine = pl.ds(EDGE + me * P_ROWS, P_ROWS)
    frames[mine] = frame[...]
    def deal(count, first, source, target, send, recv):
        own = (me >= first) & (me < first + count)
        place = lax.rem(me + (n // count + 1) * count - first, count)

        def one(j, carry):
            unit = lax.rem(place + j, count)
            remote(source(unit), target, send, recv, first + unit).start()
            return carry

        lax.fori_loop(jnp.where(own, 1, 0), count, one, 0)

        @pl.when(own)
        def _():
            pltpu.make_async_copy(source(place), target, recv).start()

    def every(source, target, send, recv):
        def one(j, carry):
            other = lax.rem(me + j, n)
            remote(source(other), target, send, recv, other).start()
            return carry

        lax.fori_loop(1, n, one, 0)

    def grid_first(grid_index):
        first = rows_smem[0]
        for nested in range(1, NCHILD):
            first = jnp.where(grid_index == nested, rows_smem[nested], first)
        return first

    deal(ROW_UNITS, 0, lambda unit: win.at[unit], gathered.at[mine], t_send.at[0], t_recv.at[0])
    every(lambda other: frame, frames.at[mine], ag_send.at[0], ag_recv.at[0])
    ocean_start(0)
    for nested in range(NCHILD):
        halo_start(0, nested)

    @pl.when(me < ROW_UNITS)
    def _():
        whole = gathered.at[pl.ds(EDGE, ocean_rows)]
        pltpu.make_async_copy(whole, whole, t_recv.at[0]).wait()
        first = grid_first(lax.rem(me // PARTS, NCHILD))
        picked[...] = gathered[pl.ds(EDGE + first, FOOT_ROWS)]
        every(lambda other: picked.at[other], rowbuf.at[me], t_send.at[2], t_recv.at[2])
        pltpu.make_async_copy(picked.at[me], rowbuf.at[me], t_recv.at[2]).start()

        @pl.when(me < ROW_UNITS // 2)
        def _():
            beside[0:1] = gathered[pl.ds(EDGE + first - 1, 1)]
            beside[1:2] = gathered[pl.ds(EDGE + first + FOOT_ROWS, 1)]
            for side, target in ((0, 0), (1, n - 1)):

                @pl.when(me != target)
                def _():
                    remote(beside.at[side], besides.at[me], t_send.at[1], t_recv.at[1], target).start()

                @pl.when(me == target)
                def _():
                    pltpu.make_async_copy(beside.at[side], besides.at[me], t_recv.at[1]).start()

    def ocean_lanes(j):
        here = pl.multiple_of(j * CHUNK, CHUNK)
        return pl.ds(here, CHUNK), pl.ds(here + TILE, CHUNK), pl.ds(here, CHUNK + 2 * TILE)

    def ocean_edge(side, field, plain):
        return ocean_halo[side, field, :, plain] * (has_before if side == 0 else has_after)

    def put8(array, part, inner, own, field, plain):
        array[part, 1:5, inner] = own
        if field is not None:
            array[part, 0:1, inner] = ocean_edge(0, field, plain)
            array[part, 5:6, inner] = ocean_edge(1, field, plain)

    chunks = P_COLS // CHUNK
    ocean_wait(0)

    def assemble(j, carry):
        plain, inner, wide = ocean_lanes(j)
        for part in range(3):
            put8(now8, part, inner, p_now[part, :, plain], part, plain)
        depth8[1:5, inner] = p_depth[:, plain]
        depth8[0:1, inner] = ocean_edge(0, 3, plain)
        depth8[5:6, inner] = ocean_edge(1, 3, plain)
        return carry

    lax.fori_loop(0, chunks, assemble, 0)

    def turn(field):
        return pltpu.roll(field, 7, 0), pltpu.roll(field, 1, 0)

    def ocean_rates(state, j):
        plain, inner, wide = ocean_lanes(j)
        shifted = []
        for part in range(3):
            block = state[part, :, wide]
            middle = block[:, TILE : TILE + CHUNK]
            shifted.append((middle,) + column_shifts(block, CHUNK) + turn(middle))
        return rates(shifted, depth8[:, inner])

    def ocean_first(j, carry):
        plain, inner, wide = ocean_lanes(j)
        changes, found = ocean_rates(now8, j)
        for index, slope in enumerate(found):
            pslopes[index, :, plain] = slope
        for part in range(3):
            second8[part, 1:5, inner] = p_old[part, :, plain] - changes[part][1:5]
        return carry

    lax.fori_loop(0, chunks, ocean_first, 0)

    for nested in range(NCHILD):
        def first_product(q):
            tile = slice(TILE * q, TILE * (q + 1))
            return second8[2, 1:5, TILE * (q + 1) : TILE * (q + 2)] * p_end[1, :, tile]

        def second_product(q):
            tile = slice(TILE * q, TILE * (q + 1))
            v_2 = second8[2, 1:5, TILE * (q + 1) : TILE * (q + 2)]
            return p_depth[:, tile] * p_end[0, :, tile] + v_2 * p_end[2, :, tile]

        value = band_tiles(nested, (first_product, second_product))
        for which in range(2):
            for piece in range(PARTS):
                unit = (which * NCHILD + nested) * PARTS + piece
                for row in range(P_ROWS):
                    at = which * P_ROWS + row
                    side_win[unit, row] = value[at : at + 1, (piece + 1) * TILE : (piece + 2) * TILE]
    deal(SIDE_UNITS, SIDE_FIRST, lambda unit: side_win.at[unit], side_gathered.at[mine], t_send.at[5], t_recv.at[5])

    all_but = frames.at[pl.ds(0, (n - 1) * P_ROWS)]
    pltpu.make_async_copy(all_but, all_but, ag_recv.at[0]).wait()

    def lanes_of(offset):
        value = frames[EDGE + rows_smem[0] + me + offset]
        for nested in range(1, NCHILD):
            other = frames[EDGE + rows_smem[nested] + me + offset]
            value = jnp.where(lane >= 32 * nested, other, value)
        return value

    south, middle, north = lanes_of(-1), lanes_of(0), lanes_of(1)

    def lane_field(row, index):
        return row if index == 0 else pltpu.roll(row, TILE - index, 1)

    e_w, e_c, e_e = [lane_field(middle, i) for i in (0, 1, 2)]
    u_w, u_c, u_e = [lane_field(middle, i) for i in (3, 4, 5)]
    v_w, v_c, v_e = [lane_field(middle, i) for i in (6, 7, 8)]
    e_s, u_s, v_s = [lane_field(south, i) for i in (1, 4, 7)]
    e_n, u_n, v_n = [lane_field(north, i) for i in (1, 4, 7)]
    e_o, u_o, v_o, b_c, ce_c, cu_c, cv_c = [lane_field(middle, i) for i in range(9, 16)]
    e_2 = e_o - HALF * (
        b_c * ((u_e - u_w) + (v_n - v_s)) + (e_e * u_e - e_w * u_w) + (e_n * v_n - e_s * v_s)
    )
    u_2 = u_o - HALF * (u_c * (u_e - u_w) + v_c * (u_n - u_s) + (e_e - e_w)) - DRAG * u_c
    v_2 = v_o - HALF * (u_c * (v_e - v_w) + v_c * (v_n - v_s) + (e_n - e_s)) - DRAG * v_c
    for index, value in enumerate((e_c, u_c, v_c, e_2, u_2, v_2, b_c, ce_c, cu_c, cv_c)):
        fvals[index : index + 1, :] = value
    for nested in range(NCHILD):
        for side in range(2):
            where = 32 * nested + 16 * side
            lanes = slice(0, TILE) if side == 0 else slice(TILE + C_COLS, PADDED)
            for part in range(3):
                for base, array in ((0, now), (3, nxt)):
                    cell = fvals[base + part : base + part + 1, where : where + 1]
                    array[nested, part, :, lanes] = jnp.broadcast_to(cell, (C_ROWS, TILE))

    def forward(stage, nested, state, base, target, slopes):
        def chunk(j, carry):
            here = pl.multiple_of(j * CHUNK, CHUNK)
            wide = pl.ds(here, CHUNK + 2 * TILE)
            plain = pl.ds(here, CHUNK)
            inner = pl.ds(here + TILE, CHUNK)
            shifted = []
            for part in range(3):
                block = state[nested, part, :, wide]
                mid_block = block[:, TILE : TILE + CHUNK]
                before = halo_row(stage, nested, 0, part, plain)
                after = halo_row(stage, nested, 1, part, plain)
                shifted.append(
                    (mid_block,) + column_shifts(block, CHUNK) + row_shifts(mid_block, before, after)
                )
            changes, found = rates(shifted, depth[nested, :, inner])
            for index, slope in enumerate(found):
                slopes[index, nested, :, plain] = slope
            bases = [base(part, inner, plain) for part in range(3)]
            news = [start - change for start, change in zip(bases, changes)]
            for part in range(3):
                target(part, inner, plain, news[part], j)
            return carry

        lax.fori_loop(0, C_COLS // CHUNK, chunk, 0)

    def add_sums(which, nested, part, value, j):
        row = (nested * 3 + part) * 4 + j // 2
        sums[which, pl.ds(row, 1), pl.ds(pl.multiple_of(lax.rem(j, 2) * CHUNK, CHUNK), CHUNK)] = (
            jnp.sum(value, axis=0, keepdims=True)
        )

    def stage_a(nested, carry):
        halo_wait(0, nested)

        def target(part, inner, plain, value, j):
            nxt[nested, part, :, inner] = value
            put_row(1, nested, part, plain, value)
            add_sums(0, nested, part, value, j)

        forward(0, nested, now, lambda part, inner, plain: old[nested, part, :, plain], target, slopes1)
        halo_start(1, nested)
        return carry

    for index in (7, 8, 9):
        loads[index].wait()
    lax.fori_loop(0, NCHILD, stage_a, 0)

    def stage_b(nested, carry):
        halo_wait(1, nested)

        def target(part, inner, plain, value, j):
            old[nested, part, :, plain] = value
            add_sums(1, nested, part, value, j)

        forward(1, nested, nxt, lambda part, inner, plain: now[nested, part, :, inner], target, slopes2)
        return carry

    lax.fori_loop(0, NCHILD, stage_b, 0)
    store_next = pltpu.make_async_copy(old, next_out, store_sem.at[0])
    store_next.start()

    fine = lax.broadcasted_iota(jnp.int32, (RATIO * TILE, TILE), 0) // RATIO
    coarse = lax.broadcasted_iota(jnp.int32, (RATIO * TILE, TILE), 1)
    gather_matrix = jnp.where(fine == coarse, 1.0 / (RATIO * RATIO), 0.0).astype(jnp.bfloat16)
    fine_t = lax.broadcasted_iota(jnp.int32, (TILE, RATIO * TILE), 1) // RATIO
    coarse_t = lax.broadcasted_iota(jnp.int32, (TILE, RATIO * TILE), 0)
    spread_matrix = jnp.where(fine_t == coarse_t, 1.0 / (RATIO * RATIO), 0.0).astype(jnp.bfloat16)
    for which in range(2):
        rest[which] = exact_dot(sums[which], gather_matrix)
    for unit in range(BACK):
        for which in range(2):
            pairs[unit, which : which + 1, :] = rest[which, unit : unit + 1, :]

    deal(BACK, BACK_FIRST, lambda unit: pairs.at[unit], returned.at[pad + me], t_send.at[3], t_recv.at[3])

    @pl.when(me >= SIDE_FIRST)
    def _():
        whole = side_gathered.at[pl.ds(EDGE, ocean_rows)]
        pltpu.make_async_copy(whole, whole, t_recv.at[5]).wait()
        first = grid_first(lax.rem((me - SIDE_FIRST) // PARTS, NCHILD))
        side_picked[0:1] = side_gathered[pl.ds(EDGE + first - 1, 1)]
        side_picked[1:2] = side_gathered[pl.ds(EDGE + first + FOOT_ROWS, 1)]
        for side, target in ((0, 0), (1, n - 1)):
            place = side_rows.at[me - SIDE_FIRST]

            @pl.when(me != target)
            def _():
                remote(side_picked.at[side], place, t_send.at[6], t_recv.at[6], target).start()

            @pl.when(me == target)
            def _():
                pltpu.make_async_copy(side_picked.at[side], place, t_recv.at[6]).start()

    pltpu.make_async_copy(rowbuf, rowbuf, t_recv.at[2]).wait()
    for which in range(2):
        for nested in range(NCHILD):
            for part in range(3):
                for piece in range(PARTS):
                    unit = ((3 * which + part) * NCHILD + nested) * PARTS + piece
                    row = (nested * 3 + part) * PARTS + piece
                    lhs[which, row : row + 1, :] = rowbuf[unit]
    spread[0] = exact_dot(lhs[0], spread_matrix)

    def spread_at(which, nested, part, j):
        row = (nested * 3 + part) * 4 + j // 2
        return spread[which, pl.ds(row, 1), pl.ds(pl.multiple_of(lax.rem(j, 2) * CHUNK, CHUNK), CHUNK)]

    def stage_c(nested, carry):
        def chunk(j, inner_carry):
            here = pl.multiple_of(j * CHUNK, CHUNK)
            plain = pl.ds(here, CHUNK)
            inner = pl.ds(here + TILE, CHUNK)
            scaled = []
            for part in range(3):
                total = end[nested, part, :, plain] + spread_at(0, nested, part, j)
                end[nested, part, :, plain] = total
                scaled.append(HALF * total)
                a2[nested, part, :, inner] = scaled[-1]
                put_row(2, nested, part, plain, scaled[-1])
            return inner_carry

        lax.fori_loop(0, C_COLS // CHUNK, chunk, 0)
        halo_start(2, nested)
        return carry

    lax.fori_loop(0, NCHILD, stage_c, 0)

    @pl.when((me == 0) | (me == n - 1))
    def _():
        pltpu.make_async_copy(besides, besides, t_recv.at[1]).wait()
        pltpu.make_async_copy(side_rows, side_rows, t_recv.at[6]).wait()
        sign = jnp.where(me == 0, -1.0, 1.0)
        for nested in range(NCHILD):

            def line(array, field):
                unit = (field * NCHILD + nested) * PARTS
                return HALF * jnp.concatenate([array[unit + piece] for piece in range(PARTS)], axis=1)

            ce, cv = line(besides, 0), line(besides, 2)
            e_q, v_q = [
                jnp.concatenate(
                    [rest[0, (nested * 3 + part) * 4 + q : (nested * 3 + part) * 4 + q + 1, :] for q in range(4)],
                    axis=1,
                )
                for part in (0, 2)
            ]
            qrow[nested, 0:1, :] = sign * (v_q * ce + cv)
            qrow[nested, 1:2, :] = sign * line(side_rows, 0)
            qrow[nested, 2:3, :] = sign * (line(side_rows, 1) + e_q * ce)

    for nested in range(NCHILD):
        row0 = nested * 12
        for side in range(2):
            sign = -1.0 if side == 0 else 1.0
            where = 32 * nested + 16 * side
            cell = 0 if side == 0 else TILE - 1
            chunk_row = 0 if side == 0 else 3
            u2, bed, ce, cu, cv = [fvals[i : i + 1, where : where + 1] for i in (4, 6, 7, 8, 9)]
            ce, cu, cv = HALF * ce, HALF * cu, HALF * cv
            e_q = rest[0, row0 + chunk_row : row0 + chunk_row + 1, cell : cell + 1]
            u_q = rest[0, row0 + 4 + chunk_row : row0 + 5 + chunk_row, cell : cell + 1]
            adds = (
                sign * (u_q * ce + cu),
                sign * (bed * ce + u2 * cu + e_q * ce),
                sign * (u2 * cv),
            )
            for part in range(3):
                row = row0 + 4 * part + chunk_row
                lhs[1, row : row + 1, :] += jnp.where(lane == cell, adds[part], 0.0)
        for part in range(3):
            for q in range(4):
                row = row0 + 4 * part + q
                lhs[1, row : row + 1, :] += qrow[nested, part : part + 1, TILE * q : TILE * (q + 1)]
    spread[1] = exact_dot(lhs[1], spread_matrix)

    def adjoint(stage, nested, state, cots, slopes, target, beside_it):
        def chunk(j, carry):
            beside_it(nested * (C_COLS // CHUNK) + j)
            here = pl.multiple_of(j * CHUNK, CHUNK)
            wide = pl.ds(here, CHUNK + 2 * TILE)
            plain = pl.ds(here, CHUNK)
            inner = pl.ds(here + TILE, CHUNK)
            wides = [cots[nested, part, :, wide] for part in range(3)]
            wides += [state[nested, 1, :, wide], depth[nested, :, wide]]
            e, v = state[nested, 0, :, inner], state[nested, 2, :, inner]

            edge_fields = []
            for side in range(2):
                he, hu, hv = [halo_row(stage, nested, side, part, plain) for part in range(3)]
                sv = halo_row(1 if stage == 2 else 0, nested, side, 2, plain)
                sb = halo_row(0, nested, side, 3, plain)
                edge_fields.append((he, hv, sv * hu, sb * he + sv * hv))

            def dy(field, index):
                ahead, behind = row_shifts(field, edge_fields[0][index], edge_fields[1][index])
                return ahead - behind

            grads = pulled(wides, e, v, dy, [slopes[i, nested, :, plain] for i in range(4)])
            target(inner, plain, j, grads)
            return carry

        lax.fori_loop(0, C_COLS // CHUNK, chunk, 0)

    def frame_cots(nested, state, cots, first):
        for side in range(2):
            near = pl.ds(TILE, TILE) if side == 0 else pl.ds(C_COLS, TILE)
            far = pl.ds(0, TILE) if side == 0 else pl.ds(TILE + C_COLS, TILE)
            cell = 0 if side == 0 else TILE - 1
            sign = 1.0 if side == 0 else -1.0
            ae, au, av = [cots[nested, part, :, near] for part in range(3)]
            u, bed = state[nested, 1, :, near], depth[nested, :, near]
            ef, uf = state[nested, 0, :, far], state[nested, 1, :, far]
            values = (uf * ae + au, bed * ae + u * au + ef * ae, u * av)
            for part in range(3):
                column = sign * jnp.sum(values[part], axis=0, keepdims=True)[:, cell : cell + 1]
                packet[...] = jnp.where(
                    lane == nested * 16 + side * 8 + first + part, column, packet[...]
                )

    steps = NCHILD * (C_COLS // CHUNK)
    each = -(-n // steps)

    @pl.when(me >= BACK_FIRST)
    def _():
        all_back = returned.at[pl.ds(pad, span)]
        pltpu.make_async_copy(all_back, all_back, t_recv.at[3]).wait()
        first = grid_first((me - BACK_FIRST) // (3 * PARTS))
        placed[...] = returned[pl.ds(pad - first, ocean_rows)]
        pltpu.make_async_copy(
            placed.at[pl.ds(me * P_ROWS, P_ROWS)], back.at[me - BACK_FIRST], t_recv.at[4]
        ).start()

    def some_placed(it):
        @pl.when(me >= BACK_FIRST)
        def _():
            for index in range(each):
                j = it * each + index

                @pl.when((j > 0) & (j < n))
                def _():
                    target = lax.rem(me + j, n)
                    remote(
                        placed.at[pl.ds(target * P_ROWS, P_ROWS)],
                        back.at[me - BACK_FIRST],
                        t_send.at[4],
                        t_recv.at[4],
                        target,
                    ).start()

    def some_edges(it):
        for index in range(each):
            j = it * each + index

            @pl.when((j > 0) & (j < n))
            def _():
                target = lax.rem(me + j, n)
                remote(packet, edges.at[me], ag_send.at[1], ag_recv.at[1], target).start()

    def stage_d(nested, carry):
        halo_wait(2, nested)

        def target(inner, plain, j, grads):
            scaled = []
            for part in range(3):
                total = mid[nested, part, :, plain] + grads[part] + spread_at(1, nested, part, j)
                mid[nested, part, :, plain] = total
                scaled.append(HALF * total)
                a1[nested, part, :, inner] = scaled[-1]
                put_row(3, nested, part, plain, scaled[-1])

        adjoint(2, nested, nxt, a2, slopes2, target, some_placed)
        halo_start(3, nested)
        frame_cots(nested, nxt, a2, 0)
        frame_cots(nested, now, a1, 3)
        return carry

    lax.fori_loop(0, NCHILD, stage_d, 0)
    store_gold = pltpu.make_async_copy(mid, gold_out, store_sem.at[1])
    store_gold.start()

    edges[me] = packet[...]

    def stage_e(nested, carry):
        halo_wait(3, nested)

        def target(inner, plain, j, grads):
            for part in range(3):
                end[nested, part, :, plain] = end[nested, part, :, plain] + grads[part]

        adjoint(3, nested, now, a1, slopes1, target, some_edges)
        return carry

    lax.fori_loop(0, NCHILD // 2, stage_e, 0)

    row4 = me * P_ROWS + lax.broadcasted_iota(jnp.int32, (P_ROWS, CHUNK), 0)
    column4 = lax.broadcasted_iota(jnp.int32, (P_ROWS, CHUNK), 1)

    def covered_at(j):
        nested = j // (BAND // CHUNK)
        foot = row4 - rows_smem[nested]
        column = j * CHUNK + column4 - cols_smem[nested]
        return (foot >= 0) & (foot < FOOT_ROWS) & (column >= 0) & (column < FOOT_COLS)

    pltpu.make_async_copy(back, back, t_recv.at[4]).wait()
    for nested in range(NCHILD):
        right = cols_smem[nested] - nested * BAND
        fine_shift = TILE - lax.rem(right, TILE)
        tiles = jnp.full((2 * P_ROWS, TILE), right // TILE, jnp.int32)
        band = nested * BAND
        blank = jnp.zeros((2 * P_ROWS, TILE), jnp.float32)
        for part in range(3):
            rows_of = [
                jnp.concatenate(
                    [back[(nested * 3 + part) * PARTS + q, :, which, :] for q in range(PARTS)], axis=1
                )
                for which in range(2)
            ]
            both = jnp.concatenate([blank, jnp.concatenate(rows_of, axis=0), blank], axis=1)
            both = moved_left(both, fine_shift, 8)
            held = [both[:, TILE * q : TILE * (q + 1)] for q in range(PARTS + 1)]
            held += [blank] * (BAND // TILE - PARTS - 1)
            for bit in range(4):
                step = 1 << bit
                chosen = (tiles >> bit) & 1 == 1
                held = [
                    jnp.where(chosen, held[q - step] if q >= step else blank, held[q])
                    for q in range(len(held))
                ]
            for q, tile in enumerate(held):
                for which in range(2):
                    means[which, part, :, band + TILE * q : band + TILE * (q + 1)] = tile[
                        P_ROWS * which : P_ROWS * (which + 1)
                    ]

    def ocean_second(j, carry):
        plain, inner, wide = ocean_lanes(j)
        covered = covered_at(j)
        for part in range(3):
            state = jnp.where(covered, means[0, part, :, plain], second8[part, 1:5, inner])
            cot = jnp.where(covered, 0.0, HALF * p_end[part, :, plain])
            second8[part, 1:5, inner] = state
            a28[part, 1:5, inner] = cot
            for side, row in ((0, 0), (1, P_ROWS - 1)):
                ocean_send[side, 4 + part, :, plain] = state[row : row + 1]
                ocean_send[side, 7 + part, :, plain] = cot[row : row + 1]
        return carry

    lax.fori_loop(0, chunks, ocean_second, 0)
    ocean_start(1)

    lax.fori_loop(NCHILD // 2, NCHILD, stage_e, 0)
    store_gnow = pltpu.make_async_copy(end, gnow_out, store_sem.at[2])
    store_gnow.start()

    ocean_wait(1)

    def ocean_edges(j, carry):
        plain, inner, wide = ocean_lanes(j)
        for part in range(3):
            for array, first in ((second8, 4), (a28, 7)):
                array[part, 0:1, inner] = ocean_edge(0, first + part, plain)
                array[part, 5:6, inner] = ocean_edge(1, first + part, plain)
        return carry

    lax.fori_loop(0, chunks, ocean_edges, 0)

    def ocean_dy(field, index):
        ahead, behind = turn(field)
        return ahead - behind

    def ocean_pull(j, state, cots, slopes):
        plain, inner, wide = ocean_lanes(j)
        wides = [cots[part, :, wide] for part in range(3)] + [state[1, :, wide], depth8[:, wide]]
        return pulled(wides, state[0, :, inner], state[2, :, inner], ocean_dy, slopes)

    def ocean_third(j, carry):
        plain, inner, wide = ocean_lanes(j)
        covered = covered_at(j)
        changes, found = ocean_rates(second8, j)
        grads = ocean_pull(j, second8, a28, found)
        for part in range(3):
            pend[part, :, plain] = jnp.where(
                covered, means[1, part, :, plain], p_now[part, :, plain] - changes[part][1:5]
            )
            cot = jnp.where(covered, 0.0, p_mid[part, :, plain] + grads[part][1:5])
            pgold[part, :, plain] = cot
            for side, row in ((0, 0), (1, P_ROWS - 1)):
                ocean_send[side, 10 + part, :, plain] = cot[row : row + 1]
        return carry

    lax.fori_loop(0, chunks, ocean_third, 0)
    ocean_start(2)
    store_pend = pltpu.make_async_copy(pend, pend_out, store_sem.at[3])
    store_pend.start()

    all_edges = edges.at[pl.ds(0, n - 1)]
    pltpu.make_async_copy(all_edges, all_edges, ag_recv.at[1]).wait()
    row8 = me * P_ROWS - 1 + lax.broadcasted_iota(jnp.int32, (8, 1), 0)
    for nested in range(NCHILD):
        foot = row8 - rows_smem[nested]
        lines = jnp.concatenate(
            [
                edges[jnp.clip(me * P_ROWS - 1 + t - rows_smem[nested], 0, FOOT_ROWS - 1)]
                for t in range(8)
            ],
            axis=0,
        )
        lines = jnp.where((foot >= 0) & (foot < FOOT_ROWS), lines, 0.0)
        for side in range(2):
            for which in range(2):
                for part in range(3):
                    at = nested * 16 + side * 8 + 3 * which + part
                    cells[nested, side, which, part] = jnp.broadcast_to(lines[:, at : at + 1], (8, TILE))
    ocean_wait(2)
    column8 = lax.broadcasted_iota(jnp.int32, (8, CHUNK), 1)

    def beside_at(j, which, part):
        nested = j // (BAND // CHUNK)
        column = j * CHUNK + column8 - cols_smem[nested]
        west, east = [
            jnp.concatenate([cells[nested, side, which, part]] * (CHUNK // TILE), axis=1) for side in range(2)
        ]
        return jnp.where(column == -1, west, 0.0) + jnp.where(column == FOOT_COLS, east, 0.0)

    def ocean_fourth(j, carry):
        plain, inner, wide = ocean_lanes(j)
        for part in range(3):
            extra = beside_at(j, 0, part)
            cot = pgold[part, :, plain] + extra[1:5]
            pgold[part, :, plain] = cot
            a18[part, 1:5, inner] = HALF * cot
            a18[part, 0:1, inner] = HALF * (ocean_edge(0, 10 + part, plain) + extra[0:1])
            a18[part, 5:6, inner] = HALF * (ocean_edge(1, 10 + part, plain) + extra[5:6])
        return carry

    lax.fori_loop(0, chunks, ocean_fourth, 0)
    store_pgold = pltpu.make_async_copy(pgold, pgold_out, store_sem.at[4])
    store_pgold.start()

    def ocean_last(j, carry):
        plain, inner, wide = ocean_lanes(j)
        covered = covered_at(j)
        grads = ocean_pull(j, now8, a18, [pslopes[i, :, plain] for i in range(4)])
        for part in range(3):
            kept = jnp.where(covered, 0.0, p_end[part, :, plain])
            pgnow[part, :, plain] = kept + (grads[part] + beside_at(j, 1, part))[1:5]
        return carry

    lax.fori_loop(0, chunks, ocean_last, 0)
    store_pgnow = pltpu.make_async_copy(pgnow, pgnow_out, store_sem.at[5])
    store_pgnow.start()
    for store in (store_next, store_gold, store_gnow, store_pend, store_pgold, store_pgnow):
        store.wait()

    pltpu.make_async_copy(all_but, all_but, ag_send.at[0]).wait()
    pltpu.make_async_copy(all_edges, all_edges, ag_send.at[1]).wait()

    def drain_halo(nested, carry):
        for stage in range(4):
            for copy in halo_copies(stage, nested):
                copy.wait_send()
        return carry

    lax.fori_loop(0, NCHILD, drain_halo, 0)
    for stage in range(3):
        for copy in ocean_copies(*ocean_stages[stage]):
            copy.wait_send()

    def drain(count, first, like, send):
        own = (me >= first) & (me < first + count)

        @pl.when(own)
        def _():
            sent = like.at[pl.ds(0, count - 1)]
            pltpu.make_async_copy(sent, sent, send).wait()

        @pl.when(jnp.logical_not(own))
        def _():
            pltpu.make_async_copy(like, like, send).wait()

    drain(ROW_UNITS, 0, win, t_send.at[0])
    drain(SIDE_UNITS, SIDE_FIRST, side_win, t_send.at[5])
    drain(BACK, BACK_FIRST, pairs, t_send.at[3])

    @pl.when(me < ROW_UNITS)
    def _():
        sent = picked.at[pl.ds(0, n - 1)]
        pltpu.make_async_copy(sent, sent, t_send.at[2]).wait()

    for target in (0, n - 1):

        @pl.when((me != target) & (me < ROW_UNITS // 2))
        def _():
            one = beside.at[0]
            pltpu.make_async_copy(one, one, t_send.at[1]).wait()

        @pl.when((me != target) & (me >= SIDE_FIRST))
        def _():
            one = side_picked.at[0]
            pltpu.make_async_copy(one, one, t_send.at[6]).wait()

    @pl.when(me >= BACK_FIRST)
    def _():
        gone = placed.at[pl.ds(0, (n - 1) * P_ROWS)]
        pltpu.make_async_copy(gone, gone, t_send.at[4]).wait()


def everything(n, child_rows, child_cols, strips, coast):
    f32 = jnp.float32
    anywhere = pl.BlockSpec(memory_space=pl.ANY)
    smem = pl.BlockSpec(memory_space=pltpu.SMEM)
    grid_shape = (NCHILD, 3, C_ROWS, C_COLS)
    wide_shape = (NCHILD, 3, C_ROWS, PADDED)
    ocean_shape = (3, P_ROWS, P_COLS)
    tall_shape = (3, 8, P_COLS + 2 * TILE)
    ocean_rows = n * P_ROWS
    dma = pltpu.SemaphoreType.DMA
    shapes = [
        grid_shape,
        wide_shape,
        wide_shape,
        (NCHILD, C_ROWS, PADDED),
        grid_shape,
        grid_shape,
        wide_shape,
        wide_shape,
        (4, NCHILD, C_ROWS, C_COLS),
        (4, NCHILD, C_ROWS, C_COLS),
        (NCHILD, 2, 4, 1, C_COLS),
        (NCHILD, 2, 4, 1, C_COLS),
        (3, NCHILD, 2, 3, 1, C_COLS),
        (3, NCHILD, 2, 3, 1, C_COLS),
        (ROW_UNITS, P_ROWS, 1, TILE),
        (SIDE_UNITS, P_ROWS, 1, TILE),
        (P_ROWS, 1, TILE),
        (ocean_rows + 2 * EDGE, 1, TILE),
        (16, TILE),
        (ocean_rows + 2 * EDGE, 1, TILE),
        (ocean_rows + 2 * EDGE, 1, TILE),
        (FOOT_ROWS, 1, TILE),
        (2, 1, TILE),
        (2, 1, TILE),
        (ROW_UNITS, 1, TILE),
        (ROW_UNITS // 2, 1, TILE),
        (SIDE_UNITS, 1, TILE),
        (2, BACK, TILE),
        (2, BACK, RATIO * TILE),
        (2, BACK, RATIO * TILE),
        (2, BACK, TILE),
        (BACK, 2, TILE),
        (2 * ocean_rows + FOOT_ROWS, 2, TILE),
        (ocean_rows, 2, TILE),
        (NCHILD, 8, FOOT_COLS),
        (n, 1, TILE),
        (1, TILE),
        ocean_shape,
        ocean_shape,
        (P_ROWS, P_COLS),
        ocean_shape,
        ocean_shape,
        tall_shape,
        tall_shape[1:],
        tall_shape,
        tall_shape,
        tall_shape,
        (4, 8, P_COLS),
        (2, 3, P_ROWS, P_COLS),
        (NCHILD, 2, 2, 3, 8, TILE),
        (BACK, P_ROWS, 2, TILE),
        ocean_shape,
        ocean_shape,
        ocean_shape,
        (2, 13, 1, P_COLS),
        (2, 13, 1, P_COLS),
    ]
    return pl.pallas_call(
        functools.partial(coastal_kernel, n),
        out_shape=[jax.ShapeDtypeStruct(grid_shape, f32)] * 3 + [jax.ShapeDtypeStruct(ocean_shape, f32)] * 3,
        in_specs=[smem] * 2 + [anywhere] * 10,
        out_specs=[anywhere] * 6,
        scratch_shapes=[pltpu.VMEM(shape, f32) for shape in shapes]
        + [
            dma((10,)),
            dma((6,)),
            dma((4, NCHILD, 2)),
            dma((4, NCHILD, 2)),
            dma((2,)),
            dma((2,)),
            dma((7,)),
            dma((7,)),
            dma((3, 2)),
            dma((3, 2)),
        ],
        compiler_params=pltpu.CompilerParams(
            collective_id=0, has_side_effects=True, vmem_limit_bytes=56 * 1024 * 1024
        ),
    )(child_rows, child_cols, *strips, *coast)


def bounce_kernel(*refs):
    sources, targets, held, sems = refs[:6], refs[6:12], refs[12:18], refs[18]
    pieces = []
    for index in range(6):
        for part in range(sources[index].shape[0]):
            pieces.append(
                (
                    pltpu.make_async_copy(
                        sources[index].at[part], held[index].at[part], sems.at[0, index, part]
                    ),
                    pltpu.make_async_copy(
                        held[index].at[part], targets[index].at[part], sems.at[1, index, part]
                    ),
                )
            )
    for fetch, store in pieces:
        fetch.start()
    for fetch, store in pieces:
        fetch.wait()
        store.start()
    for fetch, store in pieces:
        store.wait()


def bounce(arrays):
    anywhere = pl.BlockSpec(memory_space=pl.ANY)
    return pl.pallas_call(
        bounce_kernel,
        out_shape=[jax.ShapeDtypeStruct(array.shape, array.dtype) for array in arrays],
        in_specs=[anywhere] * 6,
        out_specs=[anywhere] * 6,
        scratch_shapes=[pltpu.VMEM(array.shape, array.dtype) for array in arrays]
        + [pltpu.SemaphoreType.DMA((2, 6, NCHILD))],
        compiler_params=pltpu.CompilerParams(vmem_limit_bytes=60 * 1024 * 1024),
    )(*arrays)


def shards(
    n,
    parent_old,
    parent_now,
    child_old,
    child_now,
    parent_depth,
    child_depth,
    child_rows,
    child_cols,
    parent_cot_mid,
    parent_cot_end,
    child_cot_mid,
    child_cot_end,
):
    strips = (parent_old, parent_now, parent_depth, parent_cot_mid, parent_cot_end)
    coast = (child_old, child_now, child_depth, child_cot_mid, child_cot_end)
    results = bounce(everything(n, child_rows, child_cols, strips, coast))
    child_end, child_gold, child_gnow, parent_end, parent_gold, parent_gnow = results
    return (parent_end, child_end, parent_gold, parent_gnow, child_gold, child_gnow)


def solution(mesh):
    ocean_spec = P(None, "rows", None)
    coast_spec = P(None, None, "rows", None)
    return jax.shard_map(
        functools.partial(shards, mesh.shape["rows"]),
        mesh=mesh,
        in_specs=(
            ocean_spec,
            ocean_spec,
            coast_spec,
            coast_spec,
            P("rows", None),
            P(None, "rows", None),
            P(),
            P(),
            ocean_spec,
            ocean_spec,
            coast_spec,
            coast_spec,
        ),
        out_specs=(ocean_spec, coast_spec, ocean_spec, ocean_spec, coast_spec, coast_spec),
        check_vma=False,
    )
```

```python
import functools

import jax
import jax.numpy as jnp
from jax import lax
from jax.experimental import pallas as pl
from jax.experimental.pallas import tpu as pltpu
from jax.sharding import PartitionSpec as P

MESH = pl.DeviceIdType.MESH
P_ROWS = 4
P_COLS = 8192
C_ROWS = 8
C_COLS = 4096
NCHILD = 4
RATIO = 8
FOOT_ROWS = 128
FOOT_COLS = 512
BAND = 2048
TILE = 128
PADDED = C_COLS + 2 * TILE
CHUNK = 512
COAST_UNROLL = 8
OCEAN_UNROLL = 4
HALF = 0.15
DRAG = 0.015
PARTS = FOOT_COLS // TILE
ROW_UNITS = 3 * NCHILD * PARTS
SIDE_UNITS = 2 * NCHILD * PARTS
SIDE_FIRST = 96
BACK = 3 * NCHILD * PARTS
BACK_FIRST = 48
EDGE = 8


def column_shifts(wide, width):
    ahead = pltpu.roll(wide, wide.shape[1] - 1, 1)[:, TILE : TILE + width]
    behind = pltpu.roll(wide, 1, 1)[:, TILE : TILE + width]
    return ahead, behind


def row_shifts(block, before, after):
    row = lax.broadcasted_iota(jnp.int32, block.shape, 0)
    ahead = jnp.where(row == C_ROWS - 1, after, pltpu.roll(block, C_ROWS - 1, 0))
    behind = jnp.where(row == 0, before, pltpu.roll(block, 1, 0))
    return ahead, behind


def moved_left(block, amount, bits):
    width = block.shape[1]
    amounts = jnp.full(block.shape, amount, jnp.int32)
    for bit in range(bits):
        block = jnp.where((amounts >> bit) & 1 == 1, pltpu.roll(block, width - (1 << bit), 1), block)
    return block


def cut_window(tiles, amount):
    shape = tiles[0].shape
    amounts = jnp.full(shape, amount, jnp.int32)
    blank = jnp.zeros(shape, jnp.float32)
    wanted = PARTS + 3
    for bit, count in ((10, wanted + 7), (9, wanted + 3), (8, wanted + 1), (7, wanted)):
        step = 1 << (bit - 7)
        chosen = (amounts >> bit) & 1 == 1
        tiles = [
            jnp.where(chosen, tiles[q + step] if q + step < len(tiles) else blank, tiles[q])
            for q in range(count)
        ]
    return moved_left(jnp.concatenate(tiles, axis=1), amount, 7)


def rates(shifted, bed):
    (e, ee, ew, en, es), (u, ue, uw, un, us), (v, ve, vw, vn, vs) = shifted
    ux, uy, vx, vy = ue - uw, un - us, ve - vw, vn - vs
    changes = (
        HALF * (bed * (ux + vy) + (ee * ue - ew * uw) + (en * vn - es * vs)),
        HALF * (u * ux + v * uy + (ee - ew)) + DRAG * u,
        HALF * (u * vx + v * vy + (en - es)) + DRAG * v,
    )
    return changes, (ux, uy, vx, vy)


def pulled(wides, e, v, dy, slopes):
    wae, wau, wav, wu, wbed = wides
    width = wae.shape[1] - 2 * TILE
    ae, au, av, u, bed = [wide[:, TILE : TILE + width] for wide in wides]
    ux, uy, vx, vy = slopes

    def dx(field):
        ahead, behind = column_shifts(field, width)
        return ahead - behind

    xe, ye = dx(wae), dy(ae, 0)
    ge = u * xe + v * ye + dx(wau) + dy(av, 1)
    gu = dx(wbed * wae + wu * wau) + dy(v * au, 2) + e * xe - ux * au - vx * av - 0.1 * au
    gv = dy(bed * ae + v * av, 3) + dx(wu * wav) + e * ye - uy * au - vy * av - 0.1 * av
    return ge, gu, gv


def split3(value):
    high = value.astype(jnp.bfloat16)
    rest = value - high.astype(jnp.float32)
    mid = rest.astype(jnp.bfloat16)
    low = (rest - mid.astype(jnp.float32)).astype(jnp.bfloat16)
    return high, mid, low


def exact_dot(rows, matrix):
    return sum(jnp.dot(part, matrix, preferred_element_type=jnp.float32) for part in split3(rows))


def coastal_kernel(n, rows_smem, cols_smem, win_hbm, frame_hbm, *refs):
    strips_hbm, refs = refs[:5], refs[5:]
    old_hbm, now_hbm, depth_hbm, mid_hbm, end_hbm = refs[:5]
    next_out, gold_out, gnow_out, pend_out, pgold_out, pgnow_out = refs[5:11]
    (
        old,
        now,
        nxt,
        depth,
        mid,
        end,
        a2,
        a1,
        slopes1,
        slopes2,
        first_send,
        first_halo,
        send_rows,
        halo_rows,
        win,
        side_win,
        frame,
        frames,
        fvals,
        gathered,
        side_gathered,
        picked,
        beside,
        side_picked,
        rowbuf,
        besides,
        side_rows,
        lhs,
        spread,
        sums,
        rest,
        pairs,
        returned,
        placed,
        qrow,
        edges,
        packet,
        p_old,
        p_now,
        p_depth,
        p_mid,
        p_end,
        now8,
        depth8,
        second8,
        a28,
        a18,
        pslopes,
        means,
        cells,
        back,
        pend,
        pgold,
        pgnow,
        ocean_send,
        ocean_halo,
        load_sem,
        store_sem,
        halo_send,
        halo_recv,
        ag_send,
        ag_recv,
        t_send,
        t_recv,
        ocean_send_sem,
        ocean_recv_sem,
    ) = refs[11:]
    me = lax.axis_index("rows")
    up = lax.rem(me + 1, n)
    down = lax.rem(me + n - 1, n)
    has_before, has_after = me > 0, me < n - 1
    centre = pl.ds(TILE, C_COLS)

    barrier = pltpu.get_barrier_semaphore()

    def greet(j, carry):
        pl.semaphore_signal(barrier, inc=1, device_id=(lax.rem(me + j, n),), device_id_type=MESH)
        return carry

    lax.fori_loop(1, n, greet, 0)

    strips = (p_old, p_now, p_depth, p_mid, p_end)
    loads = [
        pltpu.make_async_copy(source, target, load_sem.at[index])
        for index, (source, target) in enumerate(
            zip(
                strips_hbm + (now_hbm, depth_hbm, old_hbm, end_hbm, mid_hbm, win_hbm, frame_hbm),
                strips + (now.at[:, :, :, centre], depth.at[:, :, centre], old, end, mid, win, frame),
            )
        )
    ]
    for load in loads:
        load.start()

    ocean_rows = n * P_ROWS
    frames[0:EDGE] = jnp.zeros((EDGE, 1, TILE), jnp.float32)
    frames[pl.ds(EDGE + ocean_rows, EDGE)] = jnp.zeros((EDGE, 1, TILE), jnp.float32)
    for array, depth_of in ((gathered, 2), (side_gathered, 1)):
        array[0:EDGE] = jnp.zeros((EDGE, depth_of, TILE), jnp.float32)
        array[pl.ds(EDGE + ocean_rows, EDGE)] = jnp.zeros((EDGE, depth_of, TILE), jnp.float32)
    pad = ocean_rows
    span = FOOT_ROWS
    lane = lax.broadcasted_iota(jnp.int32, (1, TILE), 1)

    def band_tiles(nested, blocks):
        first = nested * (BAND // TILE) - 1
        tiles = []
        for q in range(first, first + BAND // TILE + 2):
            if q < 0 or q >= P_COLS // TILE:
                tiles.append(jnp.zeros((P_ROWS * len(blocks), TILE), jnp.float32))
            else:
                tiles.append(jnp.concatenate([block(q) for block in blocks], axis=0))
        return cut_window(tiles, cols_smem[nested] - nested * BAND)

    mine = pl.ds(EDGE + me * P_ROWS, P_ROWS)
    loads[11].wait()
    frames[mine] = frame[...]
    pl.semaphore_wait(barrier, n - 1)

    def remote(source, target, send, recv, device):
        return pltpu.make_async_remote_copy(
            source, target, send, recv, device_id=(device,), device_id_type=MESH
        )

    def start_both(pair):
        pl.when(has_before)(pair[0].start)
        pl.when(has_after)(pair[1].start)

    def wait_both(pair):
        pl.when(has_after)(pair[0].wait_recv)
        pl.when(has_before)(pair[1].wait_recv)

    def drain_both(pair):
        pl.when(has_before)(pair[0].wait_send)
        pl.when(has_after)(pair[1].wait_send)

    def ocean_copies(first, count, stage):
        fields = pl.ds(first, count)
        return (
            remote(
                ocean_send.at[0, fields],
                ocean_halo.at[1, fields],
                ocean_send_sem.at[stage, 0],
                ocean_recv_sem.at[stage, 1],
                down,
            ),
            remote(
                ocean_send.at[1, fields],
                ocean_halo.at[0, fields],
                ocean_send_sem.at[stage, 1],
                ocean_recv_sem.at[stage, 0],
                up,
            ),
        )

    ocean_stages = ((0, 4, 0), (4, 6, 1), (10, 3, 2))

    def ocean_start(stage):
        start_both(ocean_copies(*ocean_stages[stage]))

    def ocean_wait(stage):
        wait_both(ocean_copies(*ocean_stages[stage]))

    def halo_copies(stage, nested):
        if stage == 0:
            sources = (first_send.at[nested, 0], first_send.at[nested, 1])
            targets = (first_halo.at[nested, 1], first_halo.at[nested, 0])
        else:
            sources = (send_rows.at[stage - 1, nested, 0], send_rows.at[stage - 1, nested, 1])
            targets = (halo_rows.at[stage - 1, nested, 1], halo_rows.at[stage - 1, nested, 0])
        return (
            remote(sources[0], targets[0], halo_send.at[stage, nested, 0], halo_recv.at[stage, nested, 1], down),
            remote(sources[1], targets[1], halo_send.at[stage, nested, 1], halo_recv.at[stage, nested, 0], up),
        )

    def halo_row(stage, nested, side, part, plain):
        kept = has_before if side == 0 else has_after
        if stage == 0:
            return jnp.where(kept, first_halo[nested, side, part, :, plain], 0.0)
        return jnp.where(kept, halo_rows[stage - 1, nested, side, part, :, plain], 0.0)

    def put_row(stage, nested, part, plain, value):
        send_rows[stage - 1, nested, 0, part, :, plain] = value[0:1]
        send_rows[stage - 1, nested, 1, part, :, plain] = value[C_ROWS - 1 :]

    def halo_start(stage, nested):
        start_both(halo_copies(stage, nested))

    def halo_wait(stage, nested):
        wait_both(halo_copies(stage, nested))

    def deal(count, first, source, target, send, recv):
        own = (me >= first) & (me < first + count)
        place = lax.rem(me + (n // count + 1) * count - first, count)

        def one(j, carry):
            unit = lax.rem(place + j, count)
            remote(source(unit), target, send, recv, first + unit).start()
            return carry

        lax.fori_loop(jnp.where(own, 1, 0), count, one, 0)

        @pl.when(own)
        def _():
            pltpu.make_async_copy(source(place), target, recv).start()

    def every(source, target, send, recv):
        def one(j, carry):
            other = lax.rem(me + j, n)
            remote(source(other), target, send, recv, other).start()
            return carry

        lax.fori_loop(1, n, one, 0)

    def grid_first(grid_index):
        first = rows_smem[0]
        for nested in range(1, NCHILD):
            first = jnp.where(grid_index == nested, rows_smem[nested], first)
        return first

    every(lambda other: frame, frames.at[mine], ag_send.at[0], ag_recv.at[0])
    for index in (5, 6):
        loads[index].wait()
    for nested in range(NCHILD):
        for side, row in ((0, 0), (1, C_ROWS - 1)):
            for part in range(3):
                first_send[nested, side, part] = now[nested, part, row : row + 1, centre]
            first_send[nested, side, 3] = depth[nested, row : row + 1, centre]
        halo_start(0, nested)

    loads[10].wait()
    deal(ROW_UNITS, 0, lambda unit: win.at[unit], gathered.at[mine], t_send.at[0], t_recv.at[0])
    loads[1].wait()
    loads[2].wait()
    for side, row in ((0, 0), (1, P_ROWS - 1)):
        for part in range(3):
            ocean_send[side, part] = p_now[part, row : row + 1, :]
        ocean_send[side, 3] = p_depth[row : row + 1, :]
    ocean_start(0)

    for array in (a2, a1):
        array[:, :, :, 0:TILE] = jnp.zeros((NCHILD, 3, C_ROWS, TILE), jnp.float32)
        array[:, :, :, TILE + C_COLS :] = jnp.zeros((NCHILD, 3, C_ROWS, TILE), jnp.float32)
    depth[:, :, 0:TILE] = jnp.zeros((NCHILD, C_ROWS, TILE), jnp.float32)
    depth[:, :, TILE + C_COLS :] = jnp.zeros((NCHILD, C_ROWS, TILE), jnp.float32)
    for array in (now8, second8, a28, a18):
        for lanes in (slice(0, TILE), slice(TILE + P_COLS, P_COLS + 2 * TILE)):
            array[:, :, lanes] = jnp.zeros((3, 8, TILE), jnp.float32)
        array[:, 6:8, :] = jnp.zeros((3, 2, P_COLS + 2 * TILE), jnp.float32)
    depth8[:, 0:TILE] = jnp.zeros((8, TILE), jnp.float32)
    depth8[:, TILE + P_COLS :] = jnp.zeros((8, TILE), jnp.float32)
    depth8[6:8, :] = jnp.zeros((2, P_COLS + 2 * TILE), jnp.float32)
    qrow[...] = jnp.zeros_like(qrow)
    packet[...] = jnp.zeros_like(packet)

    all_but = frames.at[pl.ds(0, (n - 1) * P_ROWS)]
    pltpu.make_async_copy(all_but, all_but, ag_recv.at[0]).wait()

    def lanes_of(offset):
        value = frames[EDGE + rows_smem[0] + me + offset]
        for nested in range(1, NCHILD):
            other = frames[EDGE + rows_smem[nested] + me + offset]
            value = jnp.where(lane >= 32 * nested, other, value)
        return value

    south, middle, north = lanes_of(-1), lanes_of(0), lanes_of(1)

    def lane_field(row, index):
        return row if index == 0 else pltpu.roll(row, TILE - index, 1)

    e_w, e_c, e_e = [lane_field(middle, i) for i in (0, 1, 2)]
    u_w, u_c, u_e = [lane_field(middle, i) for i in (3, 4, 5)]
    v_w, v_c, v_e = [lane_field(middle, i) for i in (6, 7, 8)]
    e_s, u_s, v_s = [lane_field(south, i) for i in (1, 4, 7)]
    e_n, u_n, v_n = [lane_field(north, i) for i in (1, 4, 7)]
    e_o, u_o, v_o, b_c, ce_c, cu_c, cv_c = [lane_field(middle, i) for i in range(9, 16)]
    e_2 = e_o - HALF * (
        b_c * ((u_e - u_w) + (v_n - v_s)) + (e_e * u_e - e_w * u_w) + (e_n * v_n - e_s * v_s)
    )
    u_2 = u_o - HALF * (u_c * (u_e - u_w) + v_c * (u_n - u_s) + (e_e - e_w)) - DRAG * u_c
    v_2 = v_o - HALF * (u_c * (v_e - v_w) + v_c * (v_n - v_s) + (e_n - e_s)) - DRAG * v_c
    for index, value in enumerate((e_c, u_c, v_c, e_2, u_2, v_2, b_c, ce_c, cu_c, cv_c)):
        fvals[index : index + 1, :] = value
    for nested in range(NCHILD):
        for side in range(2):
            where = 32 * nested + 16 * side
            lanes = slice(0, TILE) if side == 0 else slice(TILE + C_COLS, PADDED)
            for part in range(3):
                for base, array in ((0, now), (3, nxt)):
                    cell = fvals[base + part : base + part + 1, where : where + 1]
                    array[nested, part, :, lanes] = jnp.broadcast_to(cell, (C_ROWS, TILE))

    def forward(stage, nested, state, base, target, slopes):
        def chunk(j, carry):
            here = pl.multiple_of(j * CHUNK, CHUNK)
            wide = pl.ds(here, CHUNK + 2 * TILE)
            plain = pl.ds(here, CHUNK)
            inner = pl.ds(here + TILE, CHUNK)
            shifted = []
            for part in range(3):
                block = state[nested, part, :, wide]
                mid_block = block[:, TILE : TILE + CHUNK]
                before = halo_row(stage, nested, 0, part, plain)
                after = halo_row(stage, nested, 1, part, plain)
                shifted.append(
                    (mid_block,) + column_shifts(block, CHUNK) + row_shifts(mid_block, before, after)
                )
            changes, found = rates(shifted, depth[nested, :, inner])
            for index, slope in enumerate(found):
                slopes[index, nested, :, plain] = slope
            bases = [base(part, inner, plain) for part in range(3)]
            news = [start - change for start, change in zip(bases, changes)]
            for part in range(3):
                target(part, inner, plain, news[part], j)
            return carry

        lax.fori_loop(0, C_COLS // CHUNK, chunk, 0, unroll=COAST_UNROLL)

    def add_sums(which, nested, part, value, j):
        row = (nested * 3 + part) * 4 + j // 2
        sums[which, pl.ds(row, 1), pl.ds(pl.multiple_of(lax.rem(j, 2) * CHUNK, CHUNK), CHUNK)] = (
            jnp.sum(value, axis=0, keepdims=True)
        )

    def stage_a(nested, carry):
        halo_wait(0, nested)

        def target(part, inner, plain, value, j):
            nxt[nested, part, :, inner] = value
            put_row(1, nested, part, plain, value)
            add_sums(0, nested, part, value, j)

        forward(0, nested, now, lambda part, inner, plain: old[nested, part, :, plain], target, slopes1)
        halo_start(1, nested)
        return carry

    loads[7].wait()
    lax.fori_loop(0, NCHILD, stage_a, 0)

    @pl.when(me < ROW_UNITS)
    def _():
        whole = gathered.at[pl.ds(EDGE, ocean_rows)]
        pltpu.make_async_copy(whole, whole, t_recv.at[0]).wait()
        first = grid_first(lax.rem(me // PARTS, NCHILD))
        picked[...] = gathered[pl.ds(EDGE + first, FOOT_ROWS)]
        every(lambda other: picked.at[other], rowbuf.at[me], t_send.at[2], t_recv.at[2])
        pltpu.make_async_copy(picked.at[me], rowbuf.at[me], t_recv.at[2]).start()

        beside[0:1] = gathered[pl.ds(EDGE + first - 1, 1)]
        beside[1:2] = gathered[pl.ds(EDGE + first + FOOT_ROWS, 1)]
        for side, target in ((0, 0), (1, n - 1)):

            @pl.when(me != target)
            def _():
                remote(beside.at[side], besides.at[me], t_send.at[1], t_recv.at[1], target).start()

            @pl.when(me == target)
            def _():
                pltpu.make_async_copy(beside.at[side], besides.at[me], t_recv.at[1]).start()

    def stage_b(nested, carry):
        halo_wait(1, nested)

        def target(part, inner, plain, value, j):
            old[nested, part, :, plain] = value
            add_sums(1, nested, part, value, j)

        forward(1, nested, nxt, lambda part, inner, plain: now[nested, part, :, inner], target, slopes2)
        return carry

    lax.fori_loop(0, NCHILD, stage_b, 0)
    store_next = pltpu.make_async_copy(old, next_out, store_sem.at[0])
    store_next.start()

    fine = lax.broadcasted_iota(jnp.int32, (RATIO * TILE, TILE), 0) // RATIO
    coarse = lax.broadcasted_iota(jnp.int32, (RATIO * TILE, TILE), 1)
    gather_matrix = jnp.where(fine == coarse, 1.0 / (RATIO * RATIO), 0.0).astype(jnp.bfloat16)
    fine_t = lax.broadcasted_iota(jnp.int32, (TILE, RATIO * TILE), 1) // RATIO
    coarse_t = lax.broadcasted_iota(jnp.int32, (TILE, RATIO * TILE), 0)
    spread_matrix = jnp.where(fine_t == coarse_t, 1.0 / (RATIO * RATIO), 0.0).astype(jnp.bfloat16)
    for which in range(2):
        rest[which] = exact_dot(sums[which], gather_matrix)
    for unit in range(BACK):
        for which in range(2):
            pairs[unit, which : which + 1, :] = rest[which, unit : unit + 1, :]

    deal(BACK, BACK_FIRST, lambda unit: pairs.at[unit], returned.at[pad + me], t_send.at[3], t_recv.at[3])

    loads[0].wait()
    loads[4].wait()
    def ocean_lanes(j):
        here = pl.multiple_of(j * CHUNK, CHUNK)
        return pl.ds(here, CHUNK), pl.ds(here + TILE, CHUNK), pl.ds(here, CHUNK + 2 * TILE)

    def ocean_edge(side, field, plain):
        return jnp.where(has_before if side == 0 else has_after, ocean_halo[side, field, :, plain], 0.0)

    def put8(array, part, inner, own, field, plain):
        array[part, 1:5, inner] = own
        if field is not None:
            array[part, 0:1, inner] = ocean_edge(0, field, plain)
            array[part, 5:6, inner] = ocean_edge(1, field, plain)

    chunks = P_COLS // CHUNK
    ocean_wait(0)

    def assemble(j, carry):
        plain, inner, wide = ocean_lanes(j)
        for part in range(3):
            put8(now8, part, inner, p_now[part, :, plain], part, plain)
        depth8[1:5, inner] = p_depth[:, plain]
        depth8[0:1, inner] = ocean_edge(0, 3, plain)
        depth8[5:6, inner] = ocean_edge(1, 3, plain)
        return carry

    lax.fori_loop(0, chunks, assemble, 0, unroll=OCEAN_UNROLL)

    def turn(field):
        return pltpu.roll(field, 7, 0), pltpu.roll(field, 1, 0)

    def ocean_rates(state, j):
        plain, inner, wide = ocean_lanes(j)
        shifted = []
        for part in range(3):
            block = state[part, :, wide]
            middle = block[:, TILE : TILE + CHUNK]
            shifted.append((middle,) + column_shifts(block, CHUNK) + turn(middle))
        return rates(shifted, depth8[:, inner])

    def ocean_first(j, carry):
        plain, inner, wide = ocean_lanes(j)
        changes, found = ocean_rates(now8, j)
        for index, slope in enumerate(found):
            pslopes[index, :, plain] = slope
        for part in range(3):
            second8[part, 1:5, inner] = p_old[part, :, plain] - changes[part][1:5]
        return carry

    lax.fori_loop(0, chunks, ocean_first, 0, unroll=OCEAN_UNROLL)

    for nested in range(NCHILD):
        def first_product(q):
            tile = slice(TILE * q, TILE * (q + 1))
            return second8[2, 1:5, TILE * (q + 1) : TILE * (q + 2)] * p_end[1, :, tile]

        def second_product(q):
            tile = slice(TILE * q, TILE * (q + 1))
            v_2 = second8[2, 1:5, TILE * (q + 1) : TILE * (q + 2)]
            return p_depth[:, tile] * p_end[0, :, tile] + v_2 * p_end[2, :, tile]

        value = band_tiles(nested, (first_product, second_product))
        for which in range(2):
            for piece in range(PARTS):
                unit = (which * NCHILD + nested) * PARTS + piece
                for row in range(P_ROWS):
                    at = which * P_ROWS + row
                    side_win[unit, row] = value[at : at + 1, (piece + 1) * TILE : (piece + 2) * TILE]
    deal(SIDE_UNITS, SIDE_FIRST, lambda unit: side_win.at[unit], side_gathered.at[mine], t_send.at[5], t_recv.at[5])

    @pl.when(me >= SIDE_FIRST)
    def _():
        whole = side_gathered.at[pl.ds(EDGE, ocean_rows)]
        pltpu.make_async_copy(whole, whole, t_recv.at[5]).wait()
        first = grid_first(lax.rem((me - SIDE_FIRST) // PARTS, NCHILD))
        side_picked[0:1] = side_gathered[pl.ds(EDGE + first - 1, 1)]
        side_picked[1:2] = side_gathered[pl.ds(EDGE + first + FOOT_ROWS, 1)]
        for side, target in ((0, 0), (1, n - 1)):
            place = side_rows.at[me - SIDE_FIRST]

            @pl.when(me != target)
            def _():
                remote(side_picked.at[side], place, t_send.at[6], t_recv.at[6], target).start()

            @pl.when(me == target)
            def _():
                pltpu.make_async_copy(side_picked.at[side], place, t_recv.at[6]).start()

    pltpu.make_async_copy(rowbuf, rowbuf, t_recv.at[2]).wait()
    for which in range(2):
        for nested in range(NCHILD):
            for part in range(3):
                for piece in range(PARTS):
                    unit = (part * NCHILD + nested) * PARTS + piece
                    row = (nested * 3 + part) * PARTS + piece
                    lhs[which, row : row + 1, :] = rowbuf[unit, which : which + 1, :]
    spread[0] = exact_dot(lhs[0], spread_matrix)

    def spread_at(which, nested, part, j):
        row = (nested * 3 + part) * 4 + j // 2
        return spread[which, pl.ds(row, 1), pl.ds(pl.multiple_of(lax.rem(j, 2) * CHUNK, CHUNK), CHUNK)]

    def stage_c(nested, carry):
        def chunk(j, inner_carry):
            here = pl.multiple_of(j * CHUNK, CHUNK)
            plain = pl.ds(here, CHUNK)
            inner = pl.ds(here + TILE, CHUNK)
            scaled = []
            for part in range(3):
                total = end[nested, part, :, plain] + spread_at(0, nested, part, j)
                end[nested, part, :, plain] = total
                scaled.append(HALF * total)
                a2[nested, part, :, inner] = scaled[-1]
                put_row(2, nested, part, plain, scaled[-1])
            return inner_carry

        lax.fori_loop(0, C_COLS // CHUNK, chunk, 0, unroll=COAST_UNROLL)
        halo_start(2, nested)
        return carry

    loads[8].wait()
    lax.fori_loop(0, NCHILD, stage_c, 0)

    @pl.when((me == 0) | (me == n - 1))
    def _():
        pltpu.make_async_copy(besides, besides, t_recv.at[1]).wait()
        pltpu.make_async_copy(side_rows, side_rows, t_recv.at[6]).wait()
        sign = jnp.where(me == 0, -1.0, 1.0)
        for nested in range(NCHILD):

            def line(array, field):
                unit = (field * NCHILD + nested) * PARTS
                return HALF * jnp.concatenate([array[unit + piece, 0:1, :] for piece in range(PARTS)], axis=1)

            ce, cv = line(besides, 0), line(besides, 2)
            e_q, v_q = [
                jnp.concatenate(
                    [rest[0, (nested * 3 + part) * 4 + q : (nested * 3 + part) * 4 + q + 1, :] for q in range(4)],
                    axis=1,
                )
                for part in (0, 2)
            ]
            qrow[nested, 0:1, :] = sign * (v_q * ce + cv)
            qrow[nested, 1:2, :] = sign * line(side_rows, 0)
            qrow[nested, 2:3, :] = sign * (line(side_rows, 1) + e_q * ce)

    for nested in range(NCHILD):
        row0 = nested * 12
        for side in range(2):
            sign = -1.0 if side == 0 else 1.0
            where = 32 * nested + 16 * side
            cell = 0 if side == 0 else TILE - 1
            chunk_row = 0 if side == 0 else 3
            u2, bed, ce, cu, cv = [fvals[i : i + 1, where : where + 1] for i in (4, 6, 7, 8, 9)]
            ce, cu, cv = HALF * ce, HALF * cu, HALF * cv
            e_q = rest[0, row0 + chunk_row : row0 + chunk_row + 1, cell : cell + 1]
            u_q = rest[0, row0 + 4 + chunk_row : row0 + 5 + chunk_row, cell : cell + 1]
            adds = (
                sign * (u_q * ce + cu),
                sign * (bed * ce + u2 * cu + e_q * ce),
                sign * (u2 * cv),
            )
            for part in range(3):
                row = row0 + 4 * part + chunk_row
                lhs[1, row : row + 1, :] += jnp.where(lane == cell, adds[part], 0.0)
        for part in range(3):
            for q in range(4):
                row = row0 + 4 * part + q
                lhs[1, row : row + 1, :] += qrow[nested, part : part + 1, TILE * q : TILE * (q + 1)]
    spread[1] = exact_dot(lhs[1], spread_matrix)

    def adjoint(stage, nested, state, cots, slopes, target):
        def chunk(j, carry):
            here = pl.multiple_of(j * CHUNK, CHUNK)
            wide = pl.ds(here, CHUNK + 2 * TILE)
            plain = pl.ds(here, CHUNK)
            inner = pl.ds(here + TILE, CHUNK)
            wides = [cots[nested, part, :, wide] for part in range(3)]
            wides += [state[nested, 1, :, wide], depth[nested, :, wide]]
            e, v = state[nested, 0, :, inner], state[nested, 2, :, inner]

            edge_fields = []
            for side in range(2):
                he, hu, hv = [halo_row(stage, nested, side, part, plain) for part in range(3)]
                sv = halo_row(1 if stage == 2 else 0, nested, side, 2, plain)
                sb = halo_row(0, nested, side, 3, plain)
                edge_fields.append((he, hv, sv * hu, sb * he + sv * hv))

            def dy(field, index):
                ahead, behind = row_shifts(field, edge_fields[0][index], edge_fields[1][index])
                return ahead - behind

            grads = pulled(wides, e, v, dy, [slopes[i, nested, :, plain] for i in range(4)])
            target(inner, plain, j, grads)
            return carry

        lax.fori_loop(0, C_COLS // CHUNK, chunk, 0, unroll=COAST_UNROLL)

    def frame_cots(nested, state, cots, first):
        for side in range(2):
            near = pl.ds(TILE, TILE) if side == 0 else pl.ds(C_COLS, TILE)
            far = pl.ds(0, TILE) if side == 0 else pl.ds(TILE + C_COLS, TILE)
            cell = 0 if side == 0 else TILE - 1
            sign = 1.0 if side == 0 else -1.0
            ae, au, av = [cots[nested, part, :, near] for part in range(3)]
            u, bed = state[nested, 1, :, near], depth[nested, :, near]
            ef, uf = state[nested, 0, :, far], state[nested, 1, :, far]
            values = (uf * ae + au, bed * ae + u * au + ef * ae, u * av)
            for part in range(3):
                column = sign * jnp.sum(values[part], axis=0, keepdims=True)[:, cell : cell + 1]
                packet[...] = jnp.where(
                    lane == nested * 16 + side * 8 + first + part, column, packet[...]
                )

    @pl.when((me >= BACK_FIRST) & (me < BACK_FIRST + BACK))
    def _():
        all_back = returned.at[pl.ds(pad, span)]
        pltpu.make_async_copy(all_back, all_back, t_recv.at[3]).wait()
        first = grid_first((me - BACK_FIRST) // (3 * PARTS))
        placed[...] = returned[pl.ds(pad - first, ocean_rows)]

        def rows_for(other):
            return placed.at[pl.ds(other * P_ROWS, P_ROWS)]

        every(rows_for, back.at[me - BACK_FIRST], t_send.at[4], t_recv.at[4])
        pltpu.make_async_copy(rows_for(me), back.at[me - BACK_FIRST], t_recv.at[4]).start()

    def stage_d(nested, carry):
        halo_wait(2, nested)

        def target(inner, plain, j, grads):
            scaled = []
            for part in range(3):
                total = mid[nested, part, :, plain] + grads[part] + spread_at(1, nested, part, j)
                mid[nested, part, :, plain] = total
                scaled.append(HALF * total)
                a1[nested, part, :, inner] = scaled[-1]
                put_row(3, nested, part, plain, scaled[-1])

        adjoint(2, nested, nxt, a2, slopes2, target)
        halo_start(3, nested)
        frame_cots(nested, nxt, a2, 0)
        frame_cots(nested, now, a1, 3)
        return carry

    loads[9].wait()
    lax.fori_loop(0, NCHILD, stage_d, 0)
    store_gold = pltpu.make_async_copy(mid, gold_out, store_sem.at[1])
    store_gold.start()

    edges[me] = packet[...]
    every(lambda other: packet, edges.at[me], ag_send.at[1], ag_recv.at[1])

    def stage_e(nested, carry):
        halo_wait(3, nested)

        def target(inner, plain, j, grads):
            for part in range(3):
                end[nested, part, :, plain] = end[nested, part, :, plain] + grads[part]

        adjoint(3, nested, now, a1, slopes1, target)
        return carry

    row4 = me * P_ROWS + lax.broadcasted_iota(jnp.int32, (P_ROWS, CHUNK), 0)
    column4 = lax.broadcasted_iota(jnp.int32, (P_ROWS, CHUNK), 1)

    def covered_at(j):
        nested = j // (BAND // CHUNK)
        foot = row4 - rows_smem[nested]
        column = j * CHUNK + column4 - cols_smem[nested]
        return (foot >= 0) & (foot < FOOT_ROWS) & (column >= 0) & (column < FOOT_COLS)

    pltpu.make_async_copy(back, back, t_recv.at[4]).wait()
    for nested in range(NCHILD):
        right = cols_smem[nested] - nested * BAND
        fine_shift = TILE - lax.rem(right, TILE)
        tiles = jnp.full((2 * P_ROWS, TILE), right // TILE, jnp.int32)
        band = nested * BAND
        blank = jnp.zeros((2 * P_ROWS, TILE), jnp.float32)
        for part in range(3):
            rows_of = [
                jnp.concatenate(
                    [back[(nested * 3 + part) * PARTS + q, :, which, :] for q in range(PARTS)], axis=1
                )
                for which in range(2)
            ]
            both = jnp.concatenate([blank, jnp.concatenate(rows_of, axis=0), blank], axis=1)
            both = moved_left(both, fine_shift, 8)
            held = [both[:, TILE * q : TILE * (q + 1)] for q in range(PARTS + 1)]
            held += [blank] * (BAND // TILE - PARTS - 1)
            for bit in range(4):
                step = 1 << bit
                chosen = (tiles >> bit) & 1 == 1
                held = [
                    jnp.where(chosen, held[q - step] if q >= step else blank, held[q])
                    for q in range(len(held))
                ]
            for q, tile in enumerate(held):
                for which in range(2):
                    means[which, part, :, band + TILE * q : band + TILE * (q + 1)] = tile[
                        P_ROWS * which : P_ROWS * (which + 1)
                    ]

    def ocean_second(j, carry):
        plain, inner, wide = ocean_lanes(j)
        covered = covered_at(j)
        for part in range(3):
            state = jnp.where(covered, means[0, part, :, plain], second8[part, 1:5, inner])
            cot = jnp.where(covered, 0.0, HALF * p_end[part, :, plain])
            second8[part, 1:5, inner] = state
            a28[part, 1:5, inner] = cot
            for side, row in ((0, 0), (1, P_ROWS - 1)):
                ocean_send[side, 4 + part, :, plain] = state[row : row + 1]
                ocean_send[side, 7 + part, :, plain] = cot[row : row + 1]
        return carry

    lax.fori_loop(0, chunks, ocean_second, 0, unroll=OCEAN_UNROLL)
    ocean_start(1)

    lax.fori_loop(0, NCHILD // 2, stage_e, 0)

    loads[3].wait()
    ocean_wait(1)

    def ocean_edges(j, carry):
        plain, inner, wide = ocean_lanes(j)
        for part in range(3):
            for array, first in ((second8, 4), (a28, 7)):
                array[part, 0:1, inner] = ocean_edge(0, first + part, plain)
                array[part, 5:6, inner] = ocean_edge(1, first + part, plain)
        return carry

    lax.fori_loop(0, chunks, ocean_edges, 0, unroll=OCEAN_UNROLL)

    def ocean_dy(field, index):
        ahead, behind = turn(field)
        return ahead - behind

    def ocean_pull(j, state, cots, slopes):
        plain, inner, wide = ocean_lanes(j)
        wides = [cots[part, :, wide] for part in range(3)] + [state[1, :, wide], depth8[:, wide]]
        return pulled(wides, state[0, :, inner], state[2, :, inner], ocean_dy, slopes)

    def ocean_third(j, carry):
        plain, inner, wide = ocean_lanes(j)
        covered = covered_at(j)
        changes, found = ocean_rates(second8, j)
        grads = ocean_pull(j, second8, a28, found)
        for part in range(3):
            pend[part, :, plain] = jnp.where(
                covered, means[1, part, :, plain], p_now[part, :, plain] - changes[part][1:5]
            )
            cot = jnp.where(covered, 0.0, p_mid[part, :, plain] + grads[part][1:5])
            pgold[part, :, plain] = cot
            for side, row in ((0, 0), (1, P_ROWS - 1)):
                ocean_send[side, 10 + part, :, plain] = cot[row : row + 1]
        return carry

    lax.fori_loop(0, chunks, ocean_third, 0, unroll=OCEAN_UNROLL)
    ocean_start(2)
    store_pend = pltpu.make_async_copy(pend, pend_out, store_sem.at[3])
    store_pend.start()

    lax.fori_loop(NCHILD // 2, NCHILD, stage_e, 0)
    store_gnow = pltpu.make_async_copy(end, gnow_out, store_sem.at[2])
    store_gnow.start()

    all_edges = edges.at[pl.ds(0, n - 1)]
    pltpu.make_async_copy(all_edges, all_edges, ag_recv.at[1]).wait()
    row8 = me * P_ROWS - 1 + lax.broadcasted_iota(jnp.int32, (8, 1), 0)
    for nested in range(NCHILD):
        foot = row8 - rows_smem[nested]
        lines = jnp.concatenate(
            [
                edges[jnp.clip(me * P_ROWS - 1 + t - rows_smem[nested], 0, FOOT_ROWS - 1)]
                for t in range(8)
            ],
            axis=0,
        )
        lines = jnp.where((foot >= 0) & (foot < FOOT_ROWS), lines, 0.0)
        for side in range(2):
            for which in range(2):
                for part in range(3):
                    at = nested * 16 + side * 8 + 3 * which + part
                    cells[nested, side, which, part] = jnp.broadcast_to(lines[:, at : at + 1], (8, TILE))
    ocean_wait(2)
    column8 = lax.broadcasted_iota(jnp.int32, (8, CHUNK), 1)

    def beside_at(j, which, part):
        nested = j // (BAND // CHUNK)
        column = j * CHUNK + column8 - cols_smem[nested]
        west, east = [
            jnp.concatenate([cells[nested, side, which, part]] * (CHUNK // TILE), axis=1) for side in range(2)
        ]
        return jnp.where(column == -1, west, 0.0) + jnp.where(column == FOOT_COLS, east, 0.0)

    def ocean_fourth(j, carry):
        plain, inner, wide = ocean_lanes(j)
        for part in range(3):
            extra = beside_at(j, 0, part)
            cot = pgold[part, :, plain] + extra[1:5]
            pgold[part, :, plain] = cot
            a18[part, 1:5, inner] = HALF * cot
            a18[part, 0:1, inner] = HALF * (ocean_edge(0, 10 + part, plain) + extra[0:1])
            a18[part, 5:6, inner] = HALF * (ocean_edge(1, 10 + part, plain) + extra[5:6])
        return carry

    lax.fori_loop(0, chunks, ocean_fourth, 0, unroll=OCEAN_UNROLL)
    store_pgold = pltpu.make_async_copy(pgold, pgold_out, store_sem.at[4])
    store_pgold.start()

    def ocean_last(j, carry):
        plain, inner, wide = ocean_lanes(j)
        covered = covered_at(j)
        grads = ocean_pull(j, now8, a18, [pslopes[i, :, plain] for i in range(4)])
        for part in range(3):
            kept = jnp.where(covered, 0.0, p_end[part, :, plain])
            pgnow[part, :, plain] = kept + (grads[part] + beside_at(j, 1, part))[1:5]
        return carry

    lax.fori_loop(0, chunks, ocean_last, 0, unroll=OCEAN_UNROLL)
    store_pgnow = pltpu.make_async_copy(pgnow, pgnow_out, store_sem.at[5])
    store_pgnow.start()
    for store in (store_next, store_gold, store_gnow, store_pend, store_pgold, store_pgnow):
        store.wait()

    pltpu.make_async_copy(all_but, all_but, ag_send.at[0]).wait()
    pltpu.make_async_copy(all_edges, all_edges, ag_send.at[1]).wait()

    def drain_halo(nested, carry):
        for stage in range(4):
            drain_both(halo_copies(stage, nested))
        return carry

    lax.fori_loop(0, NCHILD, drain_halo, 0)
    for stage in range(3):
        drain_both(ocean_copies(*ocean_stages[stage]))

    def drain(count, first, like, send):
        own = (me >= first) & (me < first + count)

        @pl.when(own)
        def _():
            sent = like.at[pl.ds(0, count - 1)]
            pltpu.make_async_copy(sent, sent, send).wait()

        @pl.when(jnp.logical_not(own))
        def _():
            pltpu.make_async_copy(like, like, send).wait()

    drain(ROW_UNITS, 0, win, t_send.at[0])
    drain(SIDE_UNITS, SIDE_FIRST, side_win, t_send.at[5])
    drain(BACK, BACK_FIRST, pairs, t_send.at[3])

    @pl.when(me < ROW_UNITS)
    def _():
        sent = picked.at[pl.ds(0, n - 1)]
        pltpu.make_async_copy(sent, sent, t_send.at[2]).wait()

    for target in (0, n - 1):

        @pl.when((me != target) & (me < ROW_UNITS))
        def _():
            one = beside.at[0]
            pltpu.make_async_copy(one, one, t_send.at[1]).wait()

        @pl.when((me != target) & (me >= SIDE_FIRST))
        def _():
            one = side_picked.at[0]
            pltpu.make_async_copy(one, one, t_send.at[6]).wait()

    @pl.when((me >= BACK_FIRST) & (me < BACK_FIRST + BACK))
    def _():
        gone = placed.at[pl.ds(0, (n - 1) * P_ROWS)]
        pltpu.make_async_copy(gone, gone, t_send.at[4]).wait()


def everything(n, child_rows, child_cols, win, frame, strips, coast):
    f32 = jnp.float32
    anywhere = pl.BlockSpec(memory_space=pl.ANY)
    smem = pl.BlockSpec(memory_space=pltpu.SMEM)
    grid_shape = (NCHILD, 3, C_ROWS, C_COLS)
    wide_shape = (NCHILD, 3, C_ROWS, PADDED)
    ocean_shape = (3, P_ROWS, P_COLS)
    tall_shape = (3, 8, P_COLS + 2 * TILE)
    ocean_rows = n * P_ROWS
    dma = pltpu.SemaphoreType.DMA
    shapes = [
        grid_shape,
        wide_shape,
        wide_shape,
        (NCHILD, C_ROWS, PADDED),
        grid_shape,
        grid_shape,
        wide_shape,
        wide_shape,
        (4, NCHILD, C_ROWS, C_COLS),
        (4, NCHILD, C_ROWS, C_COLS),
        (NCHILD, 2, 4, 1, C_COLS),
        (NCHILD, 2, 4, 1, C_COLS),
        (3, NCHILD, 2, 3, 1, C_COLS),
        (3, NCHILD, 2, 3, 1, C_COLS),
        (ROW_UNITS, P_ROWS, 2, TILE),
        (SIDE_UNITS, P_ROWS, 1, TILE),
        (P_ROWS, 1, TILE),
        (ocean_rows + 2 * EDGE, 1, TILE),
        (16, TILE),
        (ocean_rows + 2 * EDGE, 2, TILE),
        (ocean_rows + 2 * EDGE, 1, TILE),
        (FOOT_ROWS, 2, TILE),
        (2, 2, TILE),
        (2, 1, TILE),
        (ROW_UNITS, 2, TILE),
        (ROW_UNITS, 2, TILE),
        (SIDE_UNITS, 1, TILE),
        (2, BACK, TILE),
        (2, BACK, RATIO * TILE),
        (2, BACK, RATIO * TILE),
        (2, BACK, TILE),
        (BACK, 2, TILE),
        (2 * ocean_rows + FOOT_ROWS, 2, TILE),
        (ocean_rows, 2, TILE),
        (NCHILD, 8, FOOT_COLS),
        (n, 1, TILE),
        (1, TILE),
        ocean_shape,
        ocean_shape,
        (P_ROWS, P_COLS),
        ocean_shape,
        ocean_shape,
        tall_shape,
        tall_shape[1:],
        tall_shape,
        tall_shape,
        tall_shape,
        (4, 8, P_COLS),
        (2, 3, P_ROWS, P_COLS),
        (NCHILD, 2, 2, 3, 8, TILE),
        (BACK, P_ROWS, 2, TILE),
        ocean_shape,
        ocean_shape,
        ocean_shape,
        (2, 13, 1, P_COLS),
        (2, 13, 1, P_COLS),
    ]
    return pl.pallas_call(
        functools.partial(coastal_kernel, n),
        out_shape=[jax.ShapeDtypeStruct(grid_shape, f32)] * 3 + [jax.ShapeDtypeStruct(ocean_shape, f32)] * 3,
        in_specs=[smem] * 2 + [anywhere] * 12,
        out_specs=[anywhere] * 6,
        scratch_shapes=[pltpu.VMEM(shape, f32) for shape in shapes]
        + [
            dma((12,)),
            dma((6,)),
            dma((4, NCHILD, 2)),
            dma((4, NCHILD, 2)),
            dma((2,)),
            dma((2,)),
            dma((7,)),
            dma((7,)),
            dma((3, 2)),
            dma((3, 2)),
        ],
        compiler_params=pltpu.CompilerParams(
            collective_id=0, has_side_effects=True, vmem_limit_bytes=56 * 1024 * 1024
        ),
    )(child_rows, child_cols, win, frame, *strips, *coast)


def window_kernel(cols, *refs):
    sources, (win, frame), held, sem = refs[:5], refs[5:7], refs[7:12], refs[12]
    reach = FOOT_COLS + 2 * TILE
    shifts, copies = [], []
    for nested in range(NCHILD):
        left = cols[nested]
        start = pl.multiple_of(jnp.clip((left - 2) // TILE * TILE, 0, P_COLS - reach), TILE)
        shifts.append(reach - (left - start))
        for index, (source, target) in enumerate(zip(sources, held)):
            lanes = pl.ds(start, reach)
            part = source.at[:, lanes] if index == 2 else source.at[:, :, lanes]
            copies.append(pltpu.make_async_copy(part, target.at[nested], sem.at[index, nested]))
    for copy in copies:
        copy.start()
    for copy in copies:
        copy.wait()
    old, now, depth, mid, end = held
    lane = lax.broadcasted_iota(jnp.int32, (P_ROWS, TILE), 1)
    packet = jnp.zeros((P_ROWS, TILE), jnp.float32)
    for nested in range(NCHILD):
        fields = [end[nested, i] for i in range(3)] + [mid[nested, i] for i in range(3)]
        fields += [now[nested, i] for i in range(3)] + [old[nested, i] for i in range(3)] + [depth[nested]]
        blocks = []
        for first in range(0, len(fields), 2):
            pair = fields[first : first + 2]
            both = pltpu.roll(jnp.concatenate(pair, axis=0), shifts[nested], 1)
            blocks += [both[P_ROWS * i : P_ROWS * (i + 1)] for i in range(len(pair))]
        for which in range(2):
            for part in range(3):
                for piece in range(PARTS):
                    unit = (part * NCHILD + nested) * PARTS + piece
                    lanes = slice(piece * TILE, (piece + 1) * TILE)
                    for row in range(P_ROWS):
                        win[unit, row, which : which + 1, :] = blocks[3 * which + part][row : row + 1, lanes]
        first_ok = jnp.where(cols[nested] >= 2, 1.0, 0.0)
        last_ok = jnp.where(cols[nested] + FOOT_COLS + 1 < P_COLS, 1.0, 0.0)
        for side, lanes in enumerate(((reach - 2, reach - 1, 0), (FOOT_COLS - 1, FOOT_COLS, FOOT_COLS + 1))):
            found = []
            for part in range(3):
                for which, at in enumerate(lanes):
                    cell = blocks[6 + part][:, at : at + 1]
                    if side == 0 and which == 0:
                        cell = cell * first_ok
                    if side == 1 and which == 2:
                        cell = cell * last_ok
                    found.append(cell)
            found += [blocks[index][:, lanes[1] : lanes[1] + 1] for index in (9, 10, 11, 12, 0, 1, 2)]
            for index, cell in enumerate(found):
                packet = jnp.where(lane == 32 * nested + 16 * side + index, cell, packet)
    for row in range(P_ROWS):
        frame[row] = packet[row : row + 1]


def windows(strips, child_cols):
    f32 = jnp.float32
    reach = FOOT_COLS + 2 * TILE
    return pl.pallas_call(
        window_kernel,
        out_shape=[
            jax.ShapeDtypeStruct((ROW_UNITS, P_ROWS, 2, TILE), f32),
            jax.ShapeDtypeStruct((P_ROWS, 1, TILE), f32),
        ],
        in_specs=[pl.BlockSpec(memory_space=pltpu.SMEM)] + [pl.BlockSpec(memory_space=pl.ANY)] * 5,
        out_specs=[pl.BlockSpec(memory_space=pltpu.VMEM)] * 2,
        scratch_shapes=[pltpu.VMEM((NCHILD,) + strip.shape[:-1] + (reach,), f32) for strip in strips]
        + [pltpu.SemaphoreType.DMA((5, NCHILD))],
        compiler_params=pltpu.CompilerParams(vmem_limit_bytes=60 * 1024 * 1024),
    )(child_cols, *strips)


def bounce_kernel(*refs):
    sources, targets, held, sems = refs[:6], refs[6:12], refs[12:18], refs[18]
    pieces = []
    for index in range(6):
        for part in range(sources[index].shape[0]):
            pieces.append(
                (
                    pltpu.make_async_copy(
                        sources[index].at[part], held[index].at[part], sems.at[0, index, part]
                    ),
                    pltpu.make_async_copy(
                        held[index].at[part], targets[index].at[part], sems.at[1, index, part]
                    ),
                )
            )
    for fetch, store in pieces:
        fetch.start()
    for fetch, store in pieces:
        fetch.wait()
        store.start()
    for fetch, store in pieces:
        store.wait()


def bounce(arrays):
    anywhere = pl.BlockSpec(memory_space=pl.ANY)
    return pl.pallas_call(
        bounce_kernel,
        out_shape=[jax.ShapeDtypeStruct(array.shape, array.dtype) for array in arrays],
        in_specs=[anywhere] * 6,
        out_specs=[anywhere] * 6,
        scratch_shapes=[pltpu.VMEM(array.shape, array.dtype) for array in arrays]
        + [pltpu.SemaphoreType.DMA((2, 6, NCHILD))],
        compiler_params=pltpu.CompilerParams(vmem_limit_bytes=60 * 1024 * 1024),
    )(*arrays)


def shards(
    n,
    parent_old,
    parent_now,
    child_old,
    child_now,
    parent_depth,
    child_depth,
    child_rows,
    child_cols,
    parent_cot_mid,
    parent_cot_end,
    child_cot_mid,
    child_cot_end,
):
    strips = (parent_old, parent_now, parent_depth, parent_cot_mid, parent_cot_end)
    coast = (child_old, child_now, child_depth, child_cot_mid, child_cot_end)
    win, frame = windows(strips, child_cols)
    results = bounce(everything(n, child_rows, child_cols, win, frame, strips, coast))
    child_end, child_gold, child_gnow, parent_end, parent_gold, parent_gnow = results
    return (parent_end, child_end, parent_gold, parent_gnow, child_gold, child_gnow)


def solution(mesh):
    ocean_spec = P(None, "rows", None)
    coast_spec = P(None, None, "rows", None)
    return jax.shard_map(
        functools.partial(shards, mesh.shape["rows"]),
        mesh=mesh,
        in_specs=(
            ocean_spec,
            ocean_spec,
            coast_spec,
            coast_spec,
            P("rows", None),
            P(None, "rows", None),
            P(),
            P(),
            ocean_spec,
            ocean_spec,
            coast_spec,
            coast_spec,
        ),
        out_specs=(ocean_spec, coast_spec, ocean_spec, ocean_spec, coast_spec, coast_spec),
        check_vma=False,
    )
```

```python
import functools

import jax
import jax.numpy as jnp
from jax import lax
from jax.experimental import pallas as pl
from jax.experimental.pallas import tpu as pltpu
from jax.sharding import PartitionSpec as P

MESH = pl.DeviceIdType.MESH
P_ROWS = 4
P_COLS = 8192
C_ROWS = 8
C_COLS = 4096
NCHILD = 4
RATIO = 8
FOOT_ROWS = 128
FOOT_COLS = 512
BAND = 2048
TILE = 128
PADDED = C_COLS + 2 * TILE
CHUNK = 512
COAST_UNROLL = 8
OCEAN_UNROLL = 4
HALF = 0.15
DRAG = 0.015
PARTS = FOOT_COLS // TILE
ROW_UNITS = 3 * NCHILD * PARTS
SIDE_UNITS = 2 * NCHILD * PARTS
SIDE_FIRST = 96
BACK = 3 * NCHILD * PARTS
BACK_FIRST = 48
EDGE = 8


def column_shifts(wide, width):
    ahead = pltpu.roll(wide, wide.shape[1] - 1, 1)[:, TILE : TILE + width]
    behind = pltpu.roll(wide, 1, 1)[:, TILE : TILE + width]
    return ahead, behind


def row_shifts(block, before, after):
    row = lax.broadcasted_iota(jnp.int32, block.shape, 0)
    ahead = jnp.where(row == C_ROWS - 1, after, pltpu.roll(block, C_ROWS - 1, 0))
    behind = jnp.where(row == 0, before, pltpu.roll(block, 1, 0))
    return ahead, behind


def moved_left(block, amount, bits):
    width = block.shape[1]
    amounts = jnp.full(block.shape, amount, jnp.int32)
    for bit in range(bits):
        block = jnp.where((amounts >> bit) & 1 == 1, pltpu.roll(block, width - (1 << bit), 1), block)
    return block


def cut_window(tiles, amount):
    shape = tiles[0].shape
    amounts = jnp.full(shape, amount, jnp.int32)
    blank = jnp.zeros(shape, jnp.float32)
    wanted = PARTS + 3
    for bit, count in ((10, wanted + 7), (9, wanted + 3), (8, wanted + 1), (7, wanted)):
        step = 1 << (bit - 7)
        chosen = (amounts >> bit) & 1 == 1
        tiles = [
            jnp.where(chosen, tiles[q + step] if q + step < len(tiles) else blank, tiles[q])
            for q in range(count)
        ]
    return moved_left(jnp.concatenate(tiles, axis=1), amount, 7)


def rates(shifted, bed):
    (e, ee, ew, en, es), (u, ue, uw, un, us), (v, ve, vw, vn, vs) = shifted
    ux, uy, vx, vy = ue - uw, un - us, ve - vw, vn - vs
    changes = (
        HALF * (bed * (ux + vy) + (ee * ue - ew * uw) + (en * vn - es * vs)),
        HALF * (u * ux + v * uy + (ee - ew)) + DRAG * u,
        HALF * (u * vx + v * vy + (en - es)) + DRAG * v,
    )
    return changes, (ux, uy, vx, vy)


def pulled(wides, e, v, dy, slopes):
    wae, wau, wav, wu, wbed = wides
    width = wae.shape[1] - 2 * TILE
    ae, au, av, u, bed = [wide[:, TILE : TILE + width] for wide in wides]
    ux, uy, vx, vy = slopes

    def dx(field):
        ahead, behind = column_shifts(field, width)
        return ahead - behind

    xe, ye = dx(wae), dy(ae, 0)
    ge = u * xe + v * ye + dx(wau) + dy(av, 1)
    gu = dx(wbed * wae + wu * wau) + dy(v * au, 2) + e * xe - ux * au - vx * av - 0.1 * au
    gv = dy(bed * ae + v * av, 3) + dx(wu * wav) + e * ye - uy * au - vy * av - 0.1 * av
    return ge, gu, gv


def split3(value):
    high = value.astype(jnp.bfloat16)
    rest = value - high.astype(jnp.float32)
    mid = rest.astype(jnp.bfloat16)
    low = (rest - mid.astype(jnp.float32)).astype(jnp.bfloat16)
    return high, mid, low


def exact_dot(rows, matrix):
    return sum(jnp.dot(part, matrix, preferred_element_type=jnp.float32) for part in split3(rows))


def coastal_kernel(n, rows_smem, cols_smem, win_hbm, frame_hbm, *refs):
    strips_hbm, refs = refs[:5], refs[5:]
    old_hbm, now_hbm, depth_hbm, mid_hbm, end_hbm = refs[:5]
    next_out, gold_out, gnow_out, pend_out, pgold_out, pgnow_out = refs[5:11]
    (
        old,
        now,
        nxt,
        depth,
        mid,
        end,
        a2,
        a1,
        slopes1,
        slopes2,
        first_send,
        first_halo,
        send_rows,
        halo_rows,
        win,
        side_win,
        frame,
        frames,
        fvals,
        gathered,
        side_gathered,
        picked,
        beside,
        side_picked,
        rowbuf,
        besides,
        side_rows,
        lhs,
        spread,
        sums,
        rest,
        pairs,
        returned,
        placed,
        qrow,
        edges,
        packet,
        p_old,
        p_now,
        p_depth,
        p_mid,
        p_end,
        now8,
        depth8,
        second8,
        a28,
        a18,
        pslopes,
        means,
        cells,
        back,
        pend,
        pgold,
        pgnow,
        ocean_send,
        ocean_halo,
        load_sem,
        store_sem,
        halo_send,
        halo_recv,
        ag_send,
        ag_recv,
        t_send,
        t_recv,
        ocean_send_sem,
        ocean_recv_sem,
    ) = refs[11:]
    me = lax.axis_index("rows")
    up = lax.rem(me + 1, n)
    down = lax.rem(me + n - 1, n)
    has_before, has_after = me > 0, me < n - 1
    centre = pl.ds(TILE, C_COLS)

    barrier = pltpu.get_barrier_semaphore()

    def greet(j, carry):
        pl.semaphore_signal(barrier, inc=1, device_id=(lax.rem(me + j, n),), device_id_type=MESH)
        return carry

    lax.fori_loop(1, n, greet, 0)

    strips = (p_old, p_now, p_depth, p_mid, p_end)
    loads = [
        pltpu.make_async_copy(source, target, load_sem.at[index])
        for index, (source, target) in enumerate(
            zip(
                strips_hbm + (now_hbm, depth_hbm, old_hbm, end_hbm, mid_hbm, win_hbm, frame_hbm),
                strips + (now.at[:, :, :, centre], depth.at[:, :, centre], old, end, mid, win, frame),
            )
        )
    ]
    for load in loads:
        load.start()

    ocean_rows = n * P_ROWS
    frames[0:EDGE] = jnp.zeros((EDGE, 1, TILE), jnp.float32)
    frames[pl.ds(EDGE + ocean_rows, EDGE)] = jnp.zeros((EDGE, 1, TILE), jnp.float32)
    for array, depth_of in ((gathered, 2), (side_gathered, 1)):
        array[0:EDGE] = jnp.zeros((EDGE, depth_of, TILE), jnp.float32)
        array[pl.ds(EDGE + ocean_rows, EDGE)] = jnp.zeros((EDGE, depth_of, TILE), jnp.float32)
    pad = ocean_rows
    span = FOOT_ROWS
    lane = lax.broadcasted_iota(jnp.int32, (1, TILE), 1)

    def band_tiles(nested, blocks):
        first = nested * (BAND // TILE) - 1
        tiles = []
        for q in range(first, first + BAND // TILE + 2):
            if q < 0 or q >= P_COLS // TILE:
                tiles.append(jnp.zeros((P_ROWS * len(blocks), TILE), jnp.float32))
            else:
                tiles.append(jnp.concatenate([block(q) for block in blocks], axis=0))
        return cut_window(tiles, cols_smem[nested] - nested * BAND)

    mine = pl.ds(EDGE + me * P_ROWS, P_ROWS)
    loads[11].wait()
    frames[mine] = frame[...]
    pl.semaphore_wait(barrier, n - 1)

    def remote(source, target, send, recv, device):
        return pltpu.make_async_remote_copy(
            source, target, send, recv, device_id=(device,), device_id_type=MESH
        )

    def start_both(pair):
        pl.when(has_before)(pair[0].start)
        pl.when(has_after)(pair[1].start)

    def wait_both(pair):
        pl.when(has_after)(pair[0].wait_recv)
        pl.when(has_before)(pair[1].wait_recv)

    def drain_both(pair):
        pl.when(has_before)(pair[0].wait_send)
        pl.when(has_after)(pair[1].wait_send)

    def ocean_copies(first, count, stage, lanes=pl.ds(0, P_COLS)):
        fields, all_rows = pl.ds(first, count), pl.ds(0, 1)
        return (
            remote(
                ocean_send.at[0, fields, all_rows, lanes],
                ocean_halo.at[1, fields, all_rows, lanes],
                ocean_send_sem.at[stage, 0],
                ocean_recv_sem.at[stage, 1],
                down,
            ),
            remote(
                ocean_send.at[1, fields, all_rows, lanes],
                ocean_halo.at[0, fields, all_rows, lanes],
                ocean_send_sem.at[stage, 1],
                ocean_recv_sem.at[stage, 0],
                up,
            ),
        )

    ocean_stages = ((0, 4, 0), (4, 6, 1), (10, 3, 2))

    def ocean_start(stage, band):
        lanes = pl.ds(pl.multiple_of(band * BAND, BAND), BAND)
        start_both(ocean_copies(*ocean_stages[stage], lanes))

    def ocean_wait(stage):
        wait_both(ocean_copies(*ocean_stages[stage]))

    def halo_copies(stage, nested):
        if stage == 0:
            sources = (first_send.at[nested, 0], first_send.at[nested, 1])
            targets = (first_halo.at[nested, 1], first_halo.at[nested, 0])
        else:
            sources = (send_rows.at[stage - 1, nested, 0], send_rows.at[stage - 1, nested, 1])
            targets = (halo_rows.at[stage - 1, nested, 1], halo_rows.at[stage - 1, nested, 0])
        return (
            remote(sources[0], targets[0], halo_send.at[stage, nested, 0], halo_recv.at[stage, nested, 1], down),
            remote(sources[1], targets[1], halo_send.at[stage, nested, 1], halo_recv.at[stage, nested, 0], up),
        )

    def halo_row(stage, nested, side, part, plain):
        kept = has_before if side == 0 else has_after
        if stage == 0:
            return jnp.where(kept, first_halo[nested, side, part, :, plain], 0.0)
        return jnp.where(kept, halo_rows[stage - 1, nested, side, part, :, plain], 0.0)

    def put_row(stage, nested, part, plain, value):
        send_rows[stage - 1, nested, 0, part, :, plain] = value[0:1]
        send_rows[stage - 1, nested, 1, part, :, plain] = value[C_ROWS - 1 :]

    def halo_start(stage, nested):
        start_both(halo_copies(stage, nested))

    def halo_wait(stage, nested):
        wait_both(halo_copies(stage, nested))

    def deal(count, first, source, target, send, recv):
        own = (me >= first) & (me < first + count)
        place = lax.rem(me + (n // count + 1) * count - first, count)

        def one(j, carry):
            unit = lax.rem(place + j, count)
            remote(source(unit), target, send, recv, first + unit).start()
            return carry

        lax.fori_loop(jnp.where(own, 1, 0), count, one, 0)

        @pl.when(own)
        def _():
            pltpu.make_async_copy(source(place), target, recv).start()

    def every(source, target, send, recv):
        def one(j, carry):
            other = lax.rem(me + j, n)
            remote(source(other), target, send, recv, other).start()
            return carry

        lax.fori_loop(1, n, one, 0, unroll=4)

    def grid_first(grid_index):
        first = rows_smem[0]
        for nested in range(1, NCHILD):
            first = jnp.where(grid_index == nested, rows_smem[nested], first)
        return first

    every(lambda other: frame, frames.at[mine], ag_send.at[0], ag_recv.at[0])
    for index in (5, 6):
        loads[index].wait()
    for nested in range(NCHILD):
        for side, row in ((0, 0), (1, C_ROWS - 1)):
            for part in range(3):
                first_send[nested, side, part] = now[nested, part, row : row + 1, centre]
            first_send[nested, side, 3] = depth[nested, row : row + 1, centre]
        halo_start(0, nested)

    loads[10].wait()
    loads[1].wait()
    loads[2].wait()
    for side, row in ((0, 0), (1, P_ROWS - 1)):
        for part in range(3):
            ocean_send[side, part] = p_now[part, row : row + 1, :]
        ocean_send[side, 3] = p_depth[row : row + 1, :]

    for array in (a2, a1):
        array[:, :, :, 0:TILE] = jnp.zeros((NCHILD, 3, C_ROWS, TILE), jnp.float32)
        array[:, :, :, TILE + C_COLS :] = jnp.zeros((NCHILD, 3, C_ROWS, TILE), jnp.float32)
    depth[:, :, 0:TILE] = jnp.zeros((NCHILD, C_ROWS, TILE), jnp.float32)
    depth[:, :, TILE + C_COLS :] = jnp.zeros((NCHILD, C_ROWS, TILE), jnp.float32)
    for array in (now8, second8, a28, a18):
        for lanes in (slice(0, TILE), slice(TILE + P_COLS, P_COLS + 2 * TILE)):
            array[:, :, lanes] = jnp.zeros((3, 8, TILE), jnp.float32)
        array[:, 6:8, :] = jnp.zeros((3, 2, P_COLS + 2 * TILE), jnp.float32)
    depth8[:, 0:TILE] = jnp.zeros((8, TILE), jnp.float32)
    depth8[:, TILE + P_COLS :] = jnp.zeros((8, TILE), jnp.float32)
    depth8[6:8, :] = jnp.zeros((2, P_COLS + 2 * TILE), jnp.float32)
    qrow[...] = jnp.zeros_like(qrow)
    packet[...] = jnp.zeros_like(packet)

    all_but = frames.at[pl.ds(0, (n - 1) * P_ROWS)]
    pltpu.make_async_copy(all_but, all_but, ag_recv.at[0]).wait()

    def lanes_of(offset):
        value = frames[EDGE + rows_smem[0] + me + offset]
        for nested in range(1, NCHILD):
            other = frames[EDGE + rows_smem[nested] + me + offset]
            value = jnp.where(lane >= 32 * nested, other, value)
        return value

    south, middle, north = lanes_of(-1), lanes_of(0), lanes_of(1)

    def lane_field(row, index):
        return row if index == 0 else pltpu.roll(row, TILE - index, 1)

    e_w, e_c, e_e = [lane_field(middle, i) for i in (0, 1, 2)]
    u_w, u_c, u_e = [lane_field(middle, i) for i in (3, 4, 5)]
    v_w, v_c, v_e = [lane_field(middle, i) for i in (6, 7, 8)]
    e_s, u_s, v_s = [lane_field(south, i) for i in (1, 4, 7)]
    e_n, u_n, v_n = [lane_field(north, i) for i in (1, 4, 7)]
    e_o, u_o, v_o, b_c, ce_c, cu_c, cv_c = [lane_field(middle, i) for i in range(9, 16)]
    e_2 = e_o - HALF * (
        b_c * ((u_e - u_w) + (v_n - v_s)) + (e_e * u_e - e_w * u_w) + (e_n * v_n - e_s * v_s)
    )
    u_2 = u_o - HALF * (u_c * (u_e - u_w) + v_c * (u_n - u_s) + (e_e - e_w)) - DRAG * u_c
    v_2 = v_o - HALF * (u_c * (v_e - v_w) + v_c * (v_n - v_s) + (e_n - e_s)) - DRAG * v_c
    for index, value in enumerate((e_c, u_c, v_c, e_2, u_2, v_2, b_c, ce_c, cu_c, cv_c)):
        fvals[index : index + 1, :] = value
    for nested in range(NCHILD):
        for side in range(2):
            where = 32 * nested + 16 * side
            lanes = slice(0, TILE) if side == 0 else slice(TILE + C_COLS, PADDED)
            for part in range(3):
                for base, array in ((0, now), (3, nxt)):
                    cell = fvals[base + part : base + part + 1, where : where + 1]
                    array[nested, part, :, lanes] = jnp.broadcast_to(cell, (C_ROWS, TILE))

    def forward(stage, nested, state, base, target, slopes):
        def chunk(j, carry):
            here = pl.multiple_of(j * CHUNK, CHUNK)
            wide = pl.ds(here, CHUNK + 2 * TILE)
            plain = pl.ds(here, CHUNK)
            inner = pl.ds(here + TILE, CHUNK)
            shifted = []
            for part in range(3):
                block = state[nested, part, :, wide]
                mid_block = block[:, TILE : TILE + CHUNK]
                before = halo_row(stage, nested, 0, part, plain)
                after = halo_row(stage, nested, 1, part, plain)
                shifted.append(
                    (mid_block,) + column_shifts(block, CHUNK) + row_shifts(mid_block, before, after)
                )
            changes, found = rates(shifted, depth[nested, :, inner])
            for index, slope in enumerate(found):
                slopes[index, nested, :, plain] = slope
            bases = [base(part, inner, plain) for part in range(3)]
            news = [start - change for start, change in zip(bases, changes)]
            for part in range(3):
                target(part, inner, plain, news[part], j)
            return carry

        lax.fori_loop(0, C_COLS // CHUNK, chunk, 0, unroll=COAST_UNROLL)

    def add_sums(which, nested, part, value, j):
        row = (nested * 3 + part) * 4 + j // 2
        sums[which, pl.ds(row, 1), pl.ds(pl.multiple_of(lax.rem(j, 2) * CHUNK, CHUNK), CHUNK)] = (
            jnp.sum(value, axis=0, keepdims=True)
        )

    def stage_a(nested, carry):
        halo_wait(0, nested)

        def target(part, inner, plain, value, j):
            nxt[nested, part, :, inner] = value
            put_row(1, nested, part, plain, value)
            add_sums(0, nested, part, value, j)

        forward(0, nested, now, lambda part, inner, plain: old[nested, part, :, plain], target, slopes1)
        halo_start(1, nested)
        return carry

    loads[7].wait()
    lax.fori_loop(0, NCHILD, stage_a, 0)

    deal(ROW_UNITS, 0, lambda unit: win.at[unit], gathered.at[mine], t_send.at[0], t_recv.at[0])
    for band in range(P_COLS // BAND):
        ocean_start(0, band)
    def stage_b(nested, carry):
        halo_wait(1, nested)

        def target(part, inner, plain, value, j):
            old[nested, part, :, plain] = value
            add_sums(1, nested, part, value, j)

        forward(1, nested, nxt, lambda part, inner, plain: now[nested, part, :, inner], target, slopes2)
        return carry

    lax.fori_loop(0, NCHILD, stage_b, 0)
    store_next = pltpu.make_async_copy(old, next_out, store_sem.at[0])
    store_next.start()

    fine = lax.broadcasted_iota(jnp.int32, (RATIO * TILE, TILE), 0) // RATIO
    coarse = lax.broadcasted_iota(jnp.int32, (RATIO * TILE, TILE), 1)
    gather_matrix = jnp.where(fine == coarse, 1.0 / (RATIO * RATIO), 0.0).astype(jnp.bfloat16)
    fine_t = lax.broadcasted_iota(jnp.int32, (TILE, RATIO * TILE), 1) // RATIO
    coarse_t = lax.broadcasted_iota(jnp.int32, (TILE, RATIO * TILE), 0)
    spread_matrix = jnp.where(fine_t == coarse_t, 1.0 / (RATIO * RATIO), 0.0).astype(jnp.bfloat16)
    for which in range(2):
        rest[which] = exact_dot(sums[which], gather_matrix)
    for unit in range(BACK):
        for which in range(2):
            pairs[unit, which : which + 1, :] = rest[which, unit : unit + 1, :]

    deal(BACK, BACK_FIRST, lambda unit: pairs.at[unit], returned.at[pad + me], t_send.at[3], t_recv.at[3])

    @pl.when(me < ROW_UNITS)
    def _():
        whole = gathered.at[pl.ds(EDGE, ocean_rows)]
        pltpu.make_async_copy(whole, whole, t_recv.at[0]).wait()
        first = grid_first(lax.rem(me // PARTS, NCHILD))
        picked[...] = gathered[pl.ds(EDGE + first, FOOT_ROWS)]
        every(lambda other: picked.at[other], rowbuf.at[me], t_send.at[2], t_recv.at[2])
        pltpu.make_async_copy(picked.at[me], rowbuf.at[me], t_recv.at[2]).start()

        beside[0:1] = gathered[pl.ds(EDGE + first - 1, 1)]
        beside[1:2] = gathered[pl.ds(EDGE + first + FOOT_ROWS, 1)]
        for side, target in ((0, 0), (1, n - 1)):

            @pl.when(me != target)
            def _():
                remote(beside.at[side], besides.at[me], t_send.at[1], t_recv.at[1], target).start()

            @pl.when(me == target)
            def _():
                pltpu.make_async_copy(beside.at[side], besides.at[me], t_recv.at[1]).start()

    loads[0].wait()
    loads[4].wait()
    def ocean_lanes(j):
        here = pl.multiple_of(j * CHUNK, CHUNK)
        return pl.ds(here, CHUNK), pl.ds(here + TILE, CHUNK), pl.ds(here, CHUNK + 2 * TILE)

    def ocean_edge(side, field, plain):
        return jnp.where(has_before if side == 0 else has_after, ocean_halo[side, field, :, plain], 0.0)

    def put8(array, part, inner, own, field, plain):
        array[part, 1:5, inner] = own
        if field is not None:
            array[part, 0:1, inner] = ocean_edge(0, field, plain)
            array[part, 5:6, inner] = ocean_edge(1, field, plain)

    chunks = P_COLS // CHUNK
    ocean_wait(0)

    def assemble(j, carry):
        plain, inner, wide = ocean_lanes(j)
        for part in range(3):
            put8(now8, part, inner, p_now[part, :, plain], part, plain)
        depth8[1:5, inner] = p_depth[:, plain]
        depth8[0:1, inner] = ocean_edge(0, 3, plain)
        depth8[5:6, inner] = ocean_edge(1, 3, plain)
        return carry

    lax.fori_loop(0, chunks, assemble, 0, unroll=OCEAN_UNROLL)

    def turn(field):
        return pltpu.roll(field, 7, 0), pltpu.roll(field, 1, 0)

    def ocean_rates(state, j):
        plain, inner, wide = ocean_lanes(j)
        shifted = []
        for part in range(3):
            block = state[part, :, wide]
            middle = block[:, TILE : TILE + CHUNK]
            shifted.append((middle,) + column_shifts(block, CHUNK) + turn(middle))
        return rates(shifted, depth8[:, inner])

    def ocean_first(j, carry):
        plain, inner, wide = ocean_lanes(j)
        changes, found = ocean_rates(now8, j)
        for index, slope in enumerate(found):
            pslopes[index, :, plain] = slope
        for part in range(3):
            second8[part, 1:5, inner] = p_old[part, :, plain] - changes[part][1:5]
        return carry

    lax.fori_loop(0, chunks, ocean_first, 0, unroll=OCEAN_UNROLL)

    for nested in range(NCHILD):
        def first_product(q):
            tile = slice(TILE * q, TILE * (q + 1))
            return second8[2, 1:5, TILE * (q + 1) : TILE * (q + 2)] * p_end[1, :, tile]

        def second_product(q):
            tile = slice(TILE * q, TILE * (q + 1))
            v_2 = second8[2, 1:5, TILE * (q + 1) : TILE * (q + 2)]
            return p_depth[:, tile] * p_end[0, :, tile] + v_2 * p_end[2, :, tile]

        value = band_tiles(nested, (first_product, second_product))
        for which in range(2):
            for piece in range(PARTS):
                unit = (which * NCHILD + nested) * PARTS + piece
                for row in range(P_ROWS):
                    at = which * P_ROWS + row
                    side_win[unit, row] = value[at : at + 1, (piece + 1) * TILE : (piece + 2) * TILE]
    deal(SIDE_UNITS, SIDE_FIRST, lambda unit: side_win.at[unit], side_gathered.at[mine], t_send.at[5], t_recv.at[5])

    @pl.when(me >= SIDE_FIRST)
    def _():
        whole = side_gathered.at[pl.ds(EDGE, ocean_rows)]
        pltpu.make_async_copy(whole, whole, t_recv.at[5]).wait()
        first = grid_first(lax.rem((me - SIDE_FIRST) // PARTS, NCHILD))
        side_picked[0:1] = side_gathered[pl.ds(EDGE + first - 1, 1)]
        side_picked[1:2] = side_gathered[pl.ds(EDGE + first + FOOT_ROWS, 1)]
        for side, target in ((0, 0), (1, n - 1)):
            place = side_rows.at[me - SIDE_FIRST]

            @pl.when(me != target)
            def _():
                remote(side_picked.at[side], place, t_send.at[6], t_recv.at[6], target).start()

            @pl.when(me == target)
            def _():
                pltpu.make_async_copy(side_picked.at[side], place, t_recv.at[6]).start()

    @pl.when((me >= BACK_FIRST) & (me < BACK_FIRST + BACK))
    def _():
        all_back = returned.at[pl.ds(pad, span)]
        pltpu.make_async_copy(all_back, all_back, t_recv.at[3]).wait()
        first = grid_first((me - BACK_FIRST) // (3 * PARTS))
        placed[...] = returned[pl.ds(pad - first, ocean_rows)]

        def rows_for(other):
            return placed.at[pl.ds(other * P_ROWS, P_ROWS)]

        every(rows_for, back.at[me - BACK_FIRST], t_send.at[4], t_recv.at[4])
        pltpu.make_async_copy(rows_for(me), back.at[me - BACK_FIRST], t_recv.at[4]).start()

    pltpu.make_async_copy(rowbuf, rowbuf, t_recv.at[2]).wait()
    for which in range(2):
        for nested in range(NCHILD):
            for part in range(3):
                for piece in range(PARTS):
                    unit = (part * NCHILD + nested) * PARTS + piece
                    row = (nested * 3 + part) * PARTS + piece
                    lhs[which, row : row + 1, :] = rowbuf[unit, which : which + 1, :]
    spread[0] = exact_dot(lhs[0], spread_matrix)

    def spread_at(which, nested, part, j):
        row = (nested * 3 + part) * 4 + j // 2
        return spread[which, pl.ds(row, 1), pl.ds(pl.multiple_of(lax.rem(j, 2) * CHUNK, CHUNK), CHUNK)]

    def stage_c(nested, carry):
        def chunk(j, inner_carry):
            here = pl.multiple_of(j * CHUNK, CHUNK)
            plain = pl.ds(here, CHUNK)
            inner = pl.ds(here + TILE, CHUNK)
            scaled = []
            for part in range(3):
                total = end[nested, part, :, plain] + spread_at(0, nested, part, j)
                end[nested, part, :, plain] = total
                scaled.append(HALF * total)
                a2[nested, part, :, inner] = scaled[-1]
                put_row(2, nested, part, plain, scaled[-1])
            return inner_carry

        lax.fori_loop(0, C_COLS // CHUNK, chunk, 0, unroll=COAST_UNROLL)
        halo_start(2, nested)
        return carry

    loads[8].wait()
    lax.fori_loop(0, NCHILD, stage_c, 0)

    @pl.when((me == 0) | (me == n - 1))
    def _():
        pltpu.make_async_copy(besides, besides, t_recv.at[1]).wait()
        pltpu.make_async_copy(side_rows, side_rows, t_recv.at[6]).wait()
        sign = jnp.where(me == 0, -1.0, 1.0)
        for nested in range(NCHILD):

            def line(array, field):
                unit = (field * NCHILD + nested) * PARTS
                return HALF * jnp.concatenate([array[unit + piece, 0:1, :] for piece in range(PARTS)], axis=1)

            ce, cv = line(besides, 0), line(besides, 2)
            e_q, v_q = [
                jnp.concatenate(
                    [rest[0, (nested * 3 + part) * 4 + q : (nested * 3 + part) * 4 + q + 1, :] for q in range(4)],
                    axis=1,
                )
                for part in (0, 2)
            ]
            qrow[nested, 0:1, :] = sign * (v_q * ce + cv)
            qrow[nested, 1:2, :] = sign * line(side_rows, 0)
            qrow[nested, 2:3, :] = sign * (line(side_rows, 1) + e_q * ce)

    for nested in range(NCHILD):
        row0 = nested * 12
        for side in range(2):
            sign = -1.0 if side == 0 else 1.0
            where = 32 * nested + 16 * side
            cell = 0 if side == 0 else TILE - 1
            chunk_row = 0 if side == 0 else 3
            u2, bed, ce, cu, cv = [fvals[i : i + 1, where : where + 1] for i in (4, 6, 7, 8, 9)]
            ce, cu, cv = HALF * ce, HALF * cu, HALF * cv
            e_q = rest[0, row0 + chunk_row : row0 + chunk_row + 1, cell : cell + 1]
            u_q = rest[0, row0 + 4 + chunk_row : row0 + 5 + chunk_row, cell : cell + 1]
            adds = (
                sign * (u_q * ce + cu),
                sign * (bed * ce + u2 * cu + e_q * ce),
                sign * (u2 * cv),
            )
            for part in range(3):
                row = row0 + 4 * part + chunk_row
                lhs[1, row : row + 1, :] += jnp.where(lane == cell, adds[part], 0.0)
        for part in range(3):
            for q in range(4):
                row = row0 + 4 * part + q
                lhs[1, row : row + 1, :] += qrow[nested, part : part + 1, TILE * q : TILE * (q + 1)]
    spread[1] = exact_dot(lhs[1], spread_matrix)

    def adjoint(stage, nested, state, cots, slopes, target):
        def chunk(j, carry):
            here = pl.multiple_of(j * CHUNK, CHUNK)
            wide = pl.ds(here, CHUNK + 2 * TILE)
            plain = pl.ds(here, CHUNK)
            inner = pl.ds(here + TILE, CHUNK)
            wides = [cots[nested, part, :, wide] for part in range(3)]
            wides += [state[nested, 1, :, wide], depth[nested, :, wide]]
            e, v = state[nested, 0, :, inner], state[nested, 2, :, inner]

            edge_fields = []
            for side in range(2):
                he, hu, hv = [halo_row(stage, nested, side, part, plain) for part in range(3)]
                sv = halo_row(1 if stage == 2 else 0, nested, side, 2, plain)
                sb = halo_row(0, nested, side, 3, plain)
                edge_fields.append((he, hv, sv * hu, sb * he + sv * hv))

            def dy(field, index):
                ahead, behind = row_shifts(field, edge_fields[0][index], edge_fields[1][index])
                return ahead - behind

            grads = pulled(wides, e, v, dy, [slopes[i, nested, :, plain] for i in range(4)])
            target(inner, plain, j, grads)
            return carry

        lax.fori_loop(0, C_COLS // CHUNK, chunk, 0, unroll=COAST_UNROLL)

    def frame_cots(nested, state, cots, first):
        for side in range(2):
            near = pl.ds(TILE, TILE) if side == 0 else pl.ds(C_COLS, TILE)
            far = pl.ds(0, TILE) if side == 0 else pl.ds(TILE + C_COLS, TILE)
            cell = 0 if side == 0 else TILE - 1
            sign = 1.0 if side == 0 else -1.0
            ae, au, av = [cots[nested, part, :, near] for part in range(3)]
            u, bed = state[nested, 1, :, near], depth[nested, :, near]
            ef, uf = state[nested, 0, :, far], state[nested, 1, :, far]
            values = (uf * ae + au, bed * ae + u * au + ef * ae, u * av)
            for part in range(3):
                column = sign * jnp.sum(values[part], axis=0, keepdims=True)[:, cell : cell + 1]
                packet[...] = jnp.where(
                    lane == nested * 16 + side * 8 + first + part, column, packet[...]
                )

    def stage_d(nested, carry):
        halo_wait(2, nested)

        def target(inner, plain, j, grads):
            scaled = []
            for part in range(3):
                total = mid[nested, part, :, plain] + grads[part] + spread_at(1, nested, part, j)
                mid[nested, part, :, plain] = total
                scaled.append(HALF * total)
                a1[nested, part, :, inner] = scaled[-1]
                put_row(3, nested, part, plain, scaled[-1])

        adjoint(2, nested, nxt, a2, slopes2, target)
        halo_start(3, nested)
        frame_cots(nested, nxt, a2, 0)
        frame_cots(nested, now, a1, 3)
        return carry

    loads[9].wait()
    lax.fori_loop(0, NCHILD, stage_d, 0)
    store_gold = pltpu.make_async_copy(mid, gold_out, store_sem.at[1])
    store_gold.start()

    edges[me] = packet[...]

    def stage_e(nested, carry):
        halo_wait(3, nested)

        def target(inner, plain, j, grads):
            for part in range(3):
                end[nested, part, :, plain] = end[nested, part, :, plain] + grads[part]

        adjoint(3, nested, now, a1, slopes1, target)
        return carry

    row4 = me * P_ROWS + lax.broadcasted_iota(jnp.int32, (P_ROWS, CHUNK), 0)
    column4 = lax.broadcasted_iota(jnp.int32, (P_ROWS, CHUNK), 1)

    def covered_at(j):
        nested = j // (BAND // CHUNK)
        foot = row4 - rows_smem[nested]
        column = j * CHUNK + column4 - cols_smem[nested]
        return (foot >= 0) & (foot < FOOT_ROWS) & (column >= 0) & (column < FOOT_COLS)

    pltpu.make_async_copy(back, back, t_recv.at[4]).wait()
    for nested in range(NCHILD):
        right = cols_smem[nested] - nested * BAND
        fine_shift = TILE - lax.rem(right, TILE)
        tiles = jnp.full((2 * P_ROWS, TILE), right // TILE, jnp.int32)
        band = nested * BAND
        blank = jnp.zeros((2 * P_ROWS, TILE), jnp.float32)
        for part in range(3):
            rows_of = [
                jnp.concatenate(
                    [back[(nested * 3 + part) * PARTS + q, :, which, :] for q in range(PARTS)], axis=1
                )
                for which in range(2)
            ]
            both = jnp.concatenate([blank, jnp.concatenate(rows_of, axis=0), blank], axis=1)
            both = moved_left(both, fine_shift, 8)
            held = [both[:, TILE * q : TILE * (q + 1)] for q in range(PARTS + 1)]
            held += [blank] * (BAND // TILE - PARTS - 1)
            for bit in range(4):
                step = 1 << bit
                chosen = (tiles >> bit) & 1 == 1
                held = [
                    jnp.where(chosen, held[q - step] if q >= step else blank, held[q])
                    for q in range(len(held))
                ]
            for q, tile in enumerate(held):
                for which in range(2):
                    means[which, part, :, band + TILE * q : band + TILE * (q + 1)] = tile[
                        P_ROWS * which : P_ROWS * (which + 1)
                    ]

    def ocean_second(j, carry):
        plain, inner, wide = ocean_lanes(j)
        covered = covered_at(j)
        for part in range(3):
            state = jnp.where(covered, means[0, part, :, plain], second8[part, 1:5, inner])
            cot = jnp.where(covered, 0.0, HALF * p_end[part, :, plain])
            second8[part, 1:5, inner] = state
            a28[part, 1:5, inner] = cot
            for side, row in ((0, 0), (1, P_ROWS - 1)):
                ocean_send[side, 4 + part, :, plain] = state[row : row + 1]
                ocean_send[side, 7 + part, :, plain] = cot[row : row + 1]
        return carry

    def ocean_second_band(band, carry):
        per = BAND // CHUNK
        lax.fori_loop(0, per, lambda j, inner: ocean_second(band * per + j, inner), 0, unroll=OCEAN_UNROLL)
        ocean_start(1, band)
        return carry

    lax.fori_loop(0, P_COLS // BAND, ocean_second_band, 0)

    lax.fori_loop(0, NCHILD // 2, stage_e, 0)
    every(lambda other: packet, edges.at[me], ag_send.at[1], ag_recv.at[1])

    loads[3].wait()
    ocean_wait(1)

    def ocean_edges(j, carry):
        plain, inner, wide = ocean_lanes(j)
        for part in range(3):
            for array, first in ((second8, 4), (a28, 7)):
                array[part, 0:1, inner] = ocean_edge(0, first + part, plain)
                array[part, 5:6, inner] = ocean_edge(1, first + part, plain)
        return carry

    lax.fori_loop(0, chunks, ocean_edges, 0, unroll=OCEAN_UNROLL)

    def ocean_dy(field, index):
        ahead, behind = turn(field)
        return ahead - behind

    def ocean_pull(j, state, cots, slopes):
        plain, inner, wide = ocean_lanes(j)
        wides = [cots[part, :, wide] for part in range(3)] + [state[1, :, wide], depth8[:, wide]]
        return pulled(wides, state[0, :, inner], state[2, :, inner], ocean_dy, slopes)

    def ocean_third(j, carry):
        plain, inner, wide = ocean_lanes(j)
        covered = covered_at(j)
        changes, found = ocean_rates(second8, j)
        grads = ocean_pull(j, second8, a28, found)
        for part in range(3):
            pend[part, :, plain] = jnp.where(
                covered, means[1, part, :, plain], p_now[part, :, plain] - changes[part][1:5]
            )
            cot = jnp.where(covered, 0.0, p_mid[part, :, plain] + grads[part][1:5])
            pgold[part, :, plain] = cot
            for side, row in ((0, 0), (1, P_ROWS - 1)):
                ocean_send[side, 10 + part, :, plain] = cot[row : row + 1]
        return carry

    def ocean_third_band(band, carry):
        per = BAND // CHUNK
        lax.fori_loop(0, per, lambda j, inner: ocean_third(band * per + j, inner), 0, unroll=OCEAN_UNROLL)
        ocean_start(2, band)
        return carry

    lax.fori_loop(0, P_COLS // BAND, ocean_third_band, 0)
    store_pend = pltpu.make_async_copy(pend, pend_out, store_sem.at[3])
    store_pend.start()

    lax.fori_loop(NCHILD // 2, NCHILD, stage_e, 0)
    store_gnow = pltpu.make_async_copy(end, gnow_out, store_sem.at[2])
    store_gnow.start()

    all_edges = edges.at[pl.ds(0, n - 1)]
    pltpu.make_async_copy(all_edges, all_edges, ag_recv.at[1]).wait()
    row8 = me * P_ROWS - 1 + lax.broadcasted_iota(jnp.int32, (8, 1), 0)
    for nested in range(NCHILD):
        foot = row8 - rows_smem[nested]
        lines = jnp.concatenate(
            [
                edges[jnp.clip(me * P_ROWS - 1 + t - rows_smem[nested], 0, FOOT_ROWS - 1)]
                for t in range(8)
            ],
            axis=0,
        )
        lines = jnp.where((foot >= 0) & (foot < FOOT_ROWS), lines, 0.0)
        for side in range(2):
            for which in range(2):
                for part in range(3):
                    at = nested * 16 + side * 8 + 3 * which + part
                    cells[nested, side, which, part] = jnp.broadcast_to(lines[:, at : at + 1], (8, TILE))
    ocean_wait(2)
    column8 = lax.broadcasted_iota(jnp.int32, (8, CHUNK), 1)

    def beside_at(j, which, part):
        nested = j // (BAND // CHUNK)
        column = j * CHUNK + column8 - cols_smem[nested]
        west, east = [
            jnp.concatenate([cells[nested, side, which, part]] * (CHUNK // TILE), axis=1) for side in range(2)
        ]
        return jnp.where(column == -1, west, 0.0) + jnp.where(column == FOOT_COLS, east, 0.0)

    def ocean_fourth(j, carry):
        plain, inner, wide = ocean_lanes(j)
        for part in range(3):
            extra = beside_at(j, 0, part)
            cot = pgold[part, :, plain] + extra[1:5]
            pgold[part, :, plain] = cot
            a18[part, 1:5, inner] = HALF * cot
            a18[part, 0:1, inner] = HALF * (ocean_edge(0, 10 + part, plain) + extra[0:1])
            a18[part, 5:6, inner] = HALF * (ocean_edge(1, 10 + part, plain) + extra[5:6])
        return carry

    lax.fori_loop(0, chunks, ocean_fourth, 0, unroll=OCEAN_UNROLL)
    store_pgold = pltpu.make_async_copy(pgold, pgold_out, store_sem.at[4])
    store_pgold.start()

    def ocean_last(j, carry):
        plain, inner, wide = ocean_lanes(j)
        covered = covered_at(j)
        grads = ocean_pull(j, now8, a18, [pslopes[i, :, plain] for i in range(4)])
        for part in range(3):
            kept = jnp.where(covered, 0.0, p_end[part, :, plain])
            pgnow[part, :, plain] = kept + (grads[part] + beside_at(j, 1, part))[1:5]
        return carry

    lax.fori_loop(0, chunks, ocean_last, 0, unroll=OCEAN_UNROLL)
    store_pgnow = pltpu.make_async_copy(pgnow, pgnow_out, store_sem.at[5])
    store_pgnow.start()
    for store in (store_next, store_gold, store_gnow, store_pend, store_pgold, store_pgnow):
        store.wait()

    pltpu.make_async_copy(all_but, all_but, ag_send.at[0]).wait()
    pltpu.make_async_copy(all_edges, all_edges, ag_send.at[1]).wait()

    def drain_halo(nested, carry):
        for stage in range(4):
            drain_both(halo_copies(stage, nested))
        return carry

    lax.fori_loop(0, NCHILD, drain_halo, 0)
    for stage in range(3):
        drain_both(ocean_copies(*ocean_stages[stage]))

    def drain(count, first, like, send):
        own = (me >= first) & (me < first + count)

        @pl.when(own)
        def _():
            sent = like.at[pl.ds(0, count - 1)]
            pltpu.make_async_copy(sent, sent, send).wait()

        @pl.when(jnp.logical_not(own))
        def _():
            pltpu.make_async_copy(like, like, send).wait()

    drain(ROW_UNITS, 0, win, t_send.at[0])
    drain(SIDE_UNITS, SIDE_FIRST, side_win, t_send.at[5])
    drain(BACK, BACK_FIRST, pairs, t_send.at[3])

    @pl.when(me < ROW_UNITS)
    def _():
        sent = picked.at[pl.ds(0, n - 1)]
        pltpu.make_async_copy(sent, sent, t_send.at[2]).wait()

    for target in (0, n - 1):

        @pl.when((me != target) & (me < ROW_UNITS))
        def _():
            one = beside.at[0]
            pltpu.make_async_copy(one, one, t_send.at[1]).wait()

        @pl.when((me != target) & (me >= SIDE_FIRST))
        def _():
            one = side_picked.at[0]
            pltpu.make_async_copy(one, one, t_send.at[6]).wait()

    @pl.when((me >= BACK_FIRST) & (me < BACK_FIRST + BACK))
    def _():
        gone = placed.at[pl.ds(0, (n - 1) * P_ROWS)]
        pltpu.make_async_copy(gone, gone, t_send.at[4]).wait()


def everything(n, child_rows, child_cols, win, frame, strips, coast):
    f32 = jnp.float32
    anywhere = pl.BlockSpec(memory_space=pl.ANY)
    smem = pl.BlockSpec(memory_space=pltpu.SMEM)
    grid_shape = (NCHILD, 3, C_ROWS, C_COLS)
    wide_shape = (NCHILD, 3, C_ROWS, PADDED)
    ocean_shape = (3, P_ROWS, P_COLS)
    tall_shape = (3, 8, P_COLS + 2 * TILE)
    ocean_rows = n * P_ROWS
    dma = pltpu.SemaphoreType.DMA
    shapes = [
        grid_shape,
        wide_shape,
        wide_shape,
        (NCHILD, C_ROWS, PADDED),
        grid_shape,
        grid_shape,
        wide_shape,
        wide_shape,
        (4, NCHILD, C_ROWS, C_COLS),
        (4, NCHILD, C_ROWS, C_COLS),
        (NCHILD, 2, 4, 1, C_COLS),
        (NCHILD, 2, 4, 1, C_COLS),
        (3, NCHILD, 2, 3, 1, C_COLS),
        (3, NCHILD, 2, 3, 1, C_COLS),
        (ROW_UNITS, P_ROWS, 2, TILE),
        (SIDE_UNITS, P_ROWS, 1, TILE),
        (P_ROWS, 1, TILE),
        (ocean_rows + 2 * EDGE, 1, TILE),
        (16, TILE),
        (ocean_rows + 2 * EDGE, 2, TILE),
        (ocean_rows + 2 * EDGE, 1, TILE),
        (FOOT_ROWS, 2, TILE),
        (2, 2, TILE),
        (2, 1, TILE),
        (ROW_UNITS, 2, TILE),
        (ROW_UNITS, 2, TILE),
        (SIDE_UNITS, 1, TILE),
        (2, BACK, TILE),
        (2, BACK, RATIO * TILE),
        (2, BACK, RATIO * TILE),
        (2, BACK, TILE),
        (BACK, 2, TILE),
        (2 * ocean_rows + FOOT_ROWS, 2, TILE),
        (ocean_rows, 2, TILE),
        (NCHILD, 8, FOOT_COLS),
        (n, 1, TILE),
        (1, TILE),
        ocean_shape,
        ocean_shape,
        (P_ROWS, P_COLS),
        ocean_shape,
        ocean_shape,
        tall_shape,
        tall_shape[1:],
        tall_shape,
        tall_shape,
        tall_shape,
        (4, 8, P_COLS),
        (2, 3, P_ROWS, P_COLS),
        (NCHILD, 2, 2, 3, 8, TILE),
        (BACK, P_ROWS, 2, TILE),
        ocean_shape,
        ocean_shape,
        ocean_shape,
        (2, 13, 1, P_COLS),
        (2, 13, 1, P_COLS),
    ]
    return pl.pallas_call(
        functools.partial(coastal_kernel, n),
        out_shape=[jax.ShapeDtypeStruct(grid_shape, f32)] * 3 + [jax.ShapeDtypeStruct(ocean_shape, f32)] * 3,
        in_specs=[smem] * 2 + [anywhere] * 12,
        out_specs=[anywhere] * 6,
        scratch_shapes=[pltpu.VMEM(shape, f32) for shape in shapes]
        + [
            dma((12,)),
            dma((6,)),
            dma((4, NCHILD, 2)),
            dma((4, NCHILD, 2)),
            dma((2,)),
            dma((2,)),
            dma((7,)),
            dma((7,)),
            dma((3, 2)),
            dma((3, 2)),
        ],
        compiler_params=pltpu.CompilerParams(
            collective_id=0, has_side_effects=True, vmem_limit_bytes=56 * 1024 * 1024
        ),
    )(child_rows, child_cols, win, frame, *strips, *coast)


def window_kernel(cols, *refs):
    sources, (win, frame), held, sem = refs[:5], refs[5:7], refs[7:12], refs[12]
    reach = FOOT_COLS + 2 * TILE
    shifts, copies = [], []
    for nested in range(NCHILD):
        left = cols[nested]
        start = pl.multiple_of(jnp.clip((left - 2) // TILE * TILE, 0, P_COLS - reach), TILE)
        shifts.append(reach - (left - start))
        for index, (source, target) in enumerate(zip(sources, held)):
            lanes = pl.ds(start, reach)
            part = source.at[:, lanes] if index == 2 else source.at[:, :, lanes]
            copies.append(pltpu.make_async_copy(part, target.at[nested], sem.at[index, nested]))
    for copy in copies:
        copy.start()
    for copy in copies:
        copy.wait()
    old, now, depth, mid, end = held
    lane = lax.broadcasted_iota(jnp.int32, (P_ROWS, TILE), 1)
    packet = jnp.zeros((P_ROWS, TILE), jnp.float32)
    for nested in range(NCHILD):
        fields = [end[nested, i] for i in range(3)] + [mid[nested, i] for i in range(3)]
        fields += [now[nested, i] for i in range(3)] + [old[nested, i] for i in range(3)] + [depth[nested]]
        blocks = []
        for first in range(0, len(fields), 2):
            pair = fields[first : first + 2]
            both = pltpu.roll(jnp.concatenate(pair, axis=0), shifts[nested], 1)
            blocks += [both[P_ROWS * i : P_ROWS * (i + 1)] for i in range(len(pair))]
        for which in range(2):
            for part in range(3):
                for piece in range(PARTS):
                    unit = (part * NCHILD + nested) * PARTS + piece
                    lanes = slice(piece * TILE, (piece + 1) * TILE)
                    for row in range(P_ROWS):
                        win[unit, row, which : which + 1, :] = blocks[3 * which + part][row : row + 1, lanes]
        first_ok = jnp.where(cols[nested] >= 2, 1.0, 0.0)
        last_ok = jnp.where(cols[nested] + FOOT_COLS + 1 < P_COLS, 1.0, 0.0)
        for side, lanes in enumerate(((reach - 2, reach - 1, 0), (FOOT_COLS - 1, FOOT_COLS, FOOT_COLS + 1))):
            found = []
            for part in range(3):
                for which, at in enumerate(lanes):
                    cell = blocks[6 + part][:, at : at + 1]
                    if side == 0 and which == 0:
                        cell = cell * first_ok
                    if side == 1 and which == 2:
                        cell = cell * last_ok
                    found.append(cell)
            found += [blocks[index][:, lanes[1] : lanes[1] + 1] for index in (9, 10, 11, 12, 0, 1, 2)]
            for index, cell in enumerate(found):
                packet = jnp.where(lane == 32 * nested + 16 * side + index, cell, packet)
    for row in range(P_ROWS):
        frame[row] = packet[row : row + 1]


def windows(strips, child_cols):
    f32 = jnp.float32
    reach = FOOT_COLS + 2 * TILE
    return pl.pallas_call(
        window_kernel,
        out_shape=[
            jax.ShapeDtypeStruct((ROW_UNITS, P_ROWS, 2, TILE), f32),
            jax.ShapeDtypeStruct((P_ROWS, 1, TILE), f32),
        ],
        in_specs=[pl.BlockSpec(memory_space=pltpu.SMEM)] + [pl.BlockSpec(memory_space=pl.ANY)] * 5,
        out_specs=[pl.BlockSpec(memory_space=pltpu.VMEM)] * 2,
        scratch_shapes=[pltpu.VMEM((NCHILD,) + strip.shape[:-1] + (reach,), f32) for strip in strips]
        + [pltpu.SemaphoreType.DMA((5, NCHILD))],
        compiler_params=pltpu.CompilerParams(vmem_limit_bytes=60 * 1024 * 1024),
    )(child_cols, *strips)


def bounce_kernel(*refs):
    sources, targets, held, sems = refs[:6], refs[6:12], refs[12:18], refs[18]
    pieces = []
    for index in range(6):
        for part in range(sources[index].shape[0]):
            pieces.append(
                (
                    pltpu.make_async_copy(
                        sources[index].at[part], held[index].at[part], sems.at[0, index, part]
                    ),
                    pltpu.make_async_copy(
                        held[index].at[part], targets[index].at[part], sems.at[1, index, part]
                    ),
                )
            )
    for fetch, store in pieces:
        fetch.start()
    for fetch, store in pieces:
        fetch.wait()
        store.start()
    for fetch, store in pieces:
        store.wait()


def bounce(arrays):
    anywhere = pl.BlockSpec(memory_space=pl.ANY)
    return pl.pallas_call(
        bounce_kernel,
        out_shape=[jax.ShapeDtypeStruct(array.shape, array.dtype) for array in arrays],
        in_specs=[anywhere] * 6,
        out_specs=[anywhere] * 6,
        scratch_shapes=[pltpu.VMEM(array.shape, array.dtype) for array in arrays]
        + [pltpu.SemaphoreType.DMA((2, 6, NCHILD))],
        compiler_params=pltpu.CompilerParams(vmem_limit_bytes=60 * 1024 * 1024),
    )(*arrays)


def shards(
    n,
    parent_old,
    parent_now,
    child_old,
    child_now,
    parent_depth,
    child_depth,
    child_rows,
    child_cols,
    parent_cot_mid,
    parent_cot_end,
    child_cot_mid,
    child_cot_end,
):
    strips = (parent_old, parent_now, parent_depth, parent_cot_mid, parent_cot_end)
    coast = (child_old, child_now, child_depth, child_cot_mid, child_cot_end)
    win, frame = windows(strips, child_cols)
    results = bounce(everything(n, child_rows, child_cols, win, frame, strips, coast))
    child_end, child_gold, child_gnow, parent_end, parent_gold, parent_gnow = results
    return (parent_end, child_end, parent_gold, parent_gnow, child_gold, child_gnow)


def solution(mesh):
    ocean_spec = P(None, "rows", None)
    coast_spec = P(None, None, "rows", None)
    return jax.shard_map(
        functools.partial(shards, mesh.shape["rows"]),
        mesh=mesh,
        in_specs=(
            ocean_spec,
            ocean_spec,
            coast_spec,
            coast_spec,
            P("rows", None),
            P(None, "rows", None),
            P(),
            P(),
            ocean_spec,
            ocean_spec,
            coast_spec,
            coast_spec,
        ),
        out_specs=(ocean_spec, coast_spec, ocean_spec, ocean_spec, coast_spec, coast_spec),
        check_vma=False,
    )
```

```python
import functools

import jax
import jax.numpy as jnp
from jax import lax
from jax.experimental import pallas as pl
from jax.experimental.pallas import tpu as pltpu
from jax.sharding import PartitionSpec as P

MESH = pl.DeviceIdType.MESH
P_ROWS = 4
P_COLS = 8192
C_ROWS = 8
C_COLS = 4096
NCHILD = 4
RATIO = 8
FOOT_ROWS = 128
FOOT_COLS = 512
BAND = 2048
TILE = 128
PADDED = C_COLS + 2 * TILE
CHUNK = 512
COAST_UNROLL = 8
OCEAN_UNROLL = 4
HALF = 0.15
DRAG = 0.015
PARTS = FOOT_COLS // TILE
ROW_UNITS = 3 * NCHILD * PARTS
SIDE_UNITS = 2 * NCHILD * PARTS
SIDE_FIRST = 96
BACK = 3 * NCHILD * PARTS
BACK_FIRST = 48
EDGE = 8


def column_shifts(wide, width):
    ahead = pltpu.roll(wide, wide.shape[1] - 1, 1)[:, TILE : TILE + width]
    behind = pltpu.roll(wide, 1, 1)[:, TILE : TILE + width]
    return ahead, behind


def row_shifts(block, before, after):
    row = lax.broadcasted_iota(jnp.int32, block.shape, 0)
    ahead = jnp.where(row == C_ROWS - 1, after, pltpu.roll(block, C_ROWS - 1, 0))
    behind = jnp.where(row == 0, before, pltpu.roll(block, 1, 0))
    return ahead, behind


def moved_left(block, amount, bits):
    width = block.shape[1]
    amounts = jnp.full(block.shape, amount, jnp.int32)
    for bit in range(bits):
        block = jnp.where((amounts >> bit) & 1 == 1, pltpu.roll(block, width - (1 << bit), 1), block)
    return block


def cut_window(tiles, amount):
    shape = tiles[0].shape
    amounts = jnp.full(shape, amount, jnp.int32)
    blank = jnp.zeros(shape, jnp.float32)
    wanted = PARTS + 3
    for bit, count in ((10, wanted + 7), (9, wanted + 3), (8, wanted + 1), (7, wanted)):
        step = 1 << (bit - 7)
        chosen = (amounts >> bit) & 1 == 1
        tiles = [
            jnp.where(chosen, tiles[q + step] if q + step < len(tiles) else blank, tiles[q])
            for q in range(count)
        ]
    return moved_left(jnp.concatenate(tiles, axis=1), amount, 7)


def rates(shifted, bed):
    (e, ee, ew, en, es), (u, ue, uw, un, us), (v, ve, vw, vn, vs) = shifted
    ux, uy, vx, vy = ue - uw, un - us, ve - vw, vn - vs
    changes = (
        HALF * (bed * (ux + vy) + (ee * ue - ew * uw) + (en * vn - es * vs)),
        HALF * (u * ux + v * uy + (ee - ew)) + DRAG * u,
        HALF * (u * vx + v * vy + (en - es)) + DRAG * v,
    )
    return changes, (ux, uy, vx, vy)


def pulled(wides, e, v, dy, slopes):
    wae, wau, wav, wu, wbed = wides
    width = wae.shape[1] - 2 * TILE
    ae, au, av, u, bed = [wide[:, TILE : TILE + width] for wide in wides]
    ux, uy, vx, vy = slopes

    def dx(field):
        ahead, behind = column_shifts(field, width)
        return ahead - behind

    xe, ye = dx(wae), dy(ae, 0)
    ge = u * xe + v * ye + dx(wau) + dy(av, 1)
    gu = dx(wbed * wae + wu * wau) + dy(v * au, 2) + e * xe - ux * au - vx * av - 0.1 * au
    gv = dy(bed * ae + v * av, 3) + dx(wu * wav) + e * ye - uy * au - vy * av - 0.1 * av
    return ge, gu, gv


def split3(value):
    high = value.astype(jnp.bfloat16)
    rest = value - high.astype(jnp.float32)
    mid = rest.astype(jnp.bfloat16)
    low = (rest - mid.astype(jnp.float32)).astype(jnp.bfloat16)
    return high, mid, low


def exact_dot(rows, matrix):
    return sum(jnp.dot(part, matrix, preferred_element_type=jnp.float32) for part in split3(rows))


def coastal_kernel(n, rows_smem, cols_smem, win_hbm, frame_hbm, *refs):
    strips_hbm, refs = refs[:5], refs[5:]
    old_hbm, now_hbm, depth_hbm, mid_hbm, end_hbm = refs[:5]
    next_out, gold_out, gnow_out, pend_out, pgold_out, pgnow_out = refs[5:11]
    (
        old,
        now,
        nxt,
        depth,
        mid,
        end,
        a2,
        a1,
        slopes1,
        slopes2,
        first_send,
        first_halo,
        send_rows,
        halo_rows,
        win,
        side_win,
        frame,
        frames,
        fvals,
        gathered,
        side_gathered,
        picked,
        beside,
        side_picked,
        rowbuf,
        besides,
        side_rows,
        lhs,
        spread,
        sums,
        rest,
        pairs,
        returned,
        placed,
        qrow,
        edges,
        packet,
        p_old,
        p_now,
        p_depth,
        p_mid,
        p_end,
        now8,
        depth8,
        second8,
        a28,
        a18,
        pslopes,
        means,
        cells,
        back,
        pend,
        pgold,
        pgnow,
        ocean_send,
        ocean_halo,
        load_sem,
        store_sem,
        halo_send,
        halo_recv,
        ag_send,
        ag_recv,
        t_send,
        t_recv,
        ocean_send_sem,
        ocean_recv_sem,
    ) = refs[11:]
    me = lax.axis_index("rows")
    up = lax.rem(me + 1, n)
    down = lax.rem(me + n - 1, n)
    has_before, has_after = me > 0, me < n - 1
    centre = pl.ds(TILE, C_COLS)

    barrier = pltpu.get_barrier_semaphore()

    def greet(j, carry):
        pl.semaphore_signal(barrier, inc=1, device_id=(lax.rem(me + j, n),), device_id_type=MESH)
        return carry

    lax.fori_loop(1, n, greet, 0)

    strips = (p_old, p_now, p_depth, p_mid, p_end)
    loads = [
        pltpu.make_async_copy(source, target, load_sem.at[index])
        for index, (source, target) in enumerate(
            zip(
                strips_hbm + (now_hbm, depth_hbm, old_hbm, end_hbm, mid_hbm, win_hbm, frame_hbm),
                strips + (now.at[:, :, :, centre], depth.at[:, :, centre], old, end, mid, win, frame),
            )
        )
    ]
    for load in loads:
        load.start()

    ocean_rows = n * P_ROWS
    frames[0:EDGE] = jnp.zeros((EDGE, 1, TILE), jnp.float32)
    frames[pl.ds(EDGE + ocean_rows, EDGE)] = jnp.zeros((EDGE, 1, TILE), jnp.float32)
    for array, depth_of in ((gathered, 2), (side_gathered, 1)):
        array[0:EDGE] = jnp.zeros((EDGE, depth_of, TILE), jnp.float32)
        array[pl.ds(EDGE + ocean_rows, EDGE)] = jnp.zeros((EDGE, depth_of, TILE), jnp.float32)
    pad = ocean_rows
    span = FOOT_ROWS
    lane = lax.broadcasted_iota(jnp.int32, (1, TILE), 1)

    def band_tiles(nested, blocks):
        first = nested * (BAND // TILE) - 1
        tiles = []
        for q in range(first, first + BAND // TILE + 2):
            if q < 0 or q >= P_COLS // TILE:
                tiles.append(jnp.zeros((P_ROWS * len(blocks), TILE), jnp.float32))
            else:
                tiles.append(jnp.concatenate([block(q) for block in blocks], axis=0))
        return cut_window(tiles, cols_smem[nested] - nested * BAND)

    mine = pl.ds(EDGE + me * P_ROWS, P_ROWS)
    loads[11].wait()
    frames[mine] = frame[...]
    pl.semaphore_wait(barrier, n - 1)

    def remote(source, target, send, recv, device):
        return pltpu.make_async_remote_copy(
            source, target, send, recv, device_id=(device,), device_id_type=MESH
        )

    def start_both(pair):
        pl.when(has_before)(pair[0].start)
        pl.when(has_after)(pair[1].start)

    def wait_both(pair):
        pl.when(has_after)(pair[0].wait_recv)
        pl.when(has_before)(pair[1].wait_recv)

    def drain_both(pair):
        pl.when(has_before)(pair[0].wait_send)
        pl.when(has_after)(pair[1].wait_send)

    def ocean_copies(first, count, stage, lanes=pl.ds(0, P_COLS)):
        fields, all_rows = pl.ds(first, count), pl.ds(0, 1)
        return (
            remote(
                ocean_send.at[0, fields, all_rows, lanes],
                ocean_halo.at[1, fields, all_rows, lanes],
                ocean_send_sem.at[stage, 0],
                ocean_recv_sem.at[stage, 1],
                down,
            ),
            remote(
                ocean_send.at[1, fields, all_rows, lanes],
                ocean_halo.at[0, fields, all_rows, lanes],
                ocean_send_sem.at[stage, 1],
                ocean_recv_sem.at[stage, 0],
                up,
            ),
        )

    ocean_stages = ((0, 4, 0), (4, 6, 1), (10, 3, 2))

    def ocean_start(stage, band):
        lanes = pl.ds(pl.multiple_of(band * BAND, BAND), BAND)
        start_both(ocean_copies(*ocean_stages[stage], lanes))

    def ocean_wait(stage):
        wait_both(ocean_copies(*ocean_stages[stage]))

    def halo_copies(stage, nested):
        if stage == 0:
            sources = (first_send.at[nested, 0], first_send.at[nested, 1])
            targets = (first_halo.at[nested, 1], first_halo.at[nested, 0])
        else:
            sources = (send_rows.at[stage - 1, nested, 0], send_rows.at[stage - 1, nested, 1])
            targets = (halo_rows.at[stage - 1, nested, 1], halo_rows.at[stage - 1, nested, 0])
        return (
            remote(sources[0], targets[0], halo_send.at[stage, nested, 0], halo_recv.at[stage, nested, 1], down),
            remote(sources[1], targets[1], halo_send.at[stage, nested, 1], halo_recv.at[stage, nested, 0], up),
        )

    def halo_row(stage, nested, side, part, plain):
        kept = has_before if side == 0 else has_after
        if stage == 0:
            return jnp.where(kept, first_halo[nested, side, part, :, plain], 0.0)
        return jnp.where(kept, halo_rows[stage - 1, nested, side, part, :, plain], 0.0)

    def put_row(stage, nested, part, plain, value):
        send_rows[stage - 1, nested, 0, part, :, plain] = value[0:1]
        send_rows[stage - 1, nested, 1, part, :, plain] = value[C_ROWS - 1 :]

    def halo_start(stage, nested):
        start_both(halo_copies(stage, nested))

    def halo_wait(stage, nested):
        wait_both(halo_copies(stage, nested))

    def deal(count, first, source, target, send, recv):
        own = (me >= first) & (me < first + count)
        place = lax.rem(me + (n // count + 1) * count - first, count)

        def one(j, carry):
            unit = lax.rem(place + j, count)
            remote(source(unit), target, send, recv, first + unit).start()
            return carry

        lax.fori_loop(jnp.where(own, 1, 0), count, one, 0)

        @pl.when(own)
        def _():
            pltpu.make_async_copy(source(place), target, recv).start()

    def every(source, target, send, recv):
        def one(j, carry):
            other = lax.rem(me + j, n)
            remote(source(other), target, send, recv, other).start()
            return carry

        lax.fori_loop(1, n, one, 0, unroll=4)

    def grid_first(grid_index):
        first = rows_smem[0]
        for nested in range(1, NCHILD):
            first = jnp.where(grid_index == nested, rows_smem[nested], first)
        return first

    every(lambda other: frame, frames.at[mine], ag_send.at[0], ag_recv.at[0])
    for index in (5, 6):
        loads[index].wait()
    for nested in range(NCHILD):
        for side, row in ((0, 0), (1, C_ROWS - 1)):
            for part in range(3):
                first_send[nested, side, part] = now[nested, part, row : row + 1, centre]
            first_send[nested, side, 3] = depth[nested, row : row + 1, centre]
        halo_start(0, nested)

    loads[10].wait()
    loads[1].wait()
    loads[2].wait()
    for side, row in ((0, 0), (1, P_ROWS - 1)):
        for part in range(3):
            ocean_send[side, part] = p_now[part, row : row + 1, :]
        ocean_send[side, 3] = p_depth[row : row + 1, :]

    for array in (a2, a1):
        array[:, :, :, 0:TILE] = jnp.zeros((NCHILD, 3, C_ROWS, TILE), jnp.float32)
        array[:, :, :, TILE + C_COLS :] = jnp.zeros((NCHILD, 3, C_ROWS, TILE), jnp.float32)
    depth[:, :, 0:TILE] = jnp.zeros((NCHILD, C_ROWS, TILE), jnp.float32)
    depth[:, :, TILE + C_COLS :] = jnp.zeros((NCHILD, C_ROWS, TILE), jnp.float32)
    for array in (now8, second8, a28, a18):
        for lanes in (slice(0, TILE), slice(TILE + P_COLS, P_COLS + 2 * TILE)):
            array[:, :, lanes] = jnp.zeros((3, 8, TILE), jnp.float32)
        array[:, 6:8, :] = jnp.zeros((3, 2, P_COLS + 2 * TILE), jnp.float32)
    depth8[:, 0:TILE] = jnp.zeros((8, TILE), jnp.float32)
    depth8[:, TILE + P_COLS :] = jnp.zeros((8, TILE), jnp.float32)
    depth8[6:8, :] = jnp.zeros((2, P_COLS + 2 * TILE), jnp.float32)
    qrow[...] = jnp.zeros_like(qrow)
    packet[...] = jnp.zeros_like(packet)

    all_but = frames.at[pl.ds(0, (n - 1) * P_ROWS)]
    pltpu.make_async_copy(all_but, all_but, ag_recv.at[0]).wait()

    def lanes_of(offset):
        value = frames[EDGE + rows_smem[0] + me + offset]
        for nested in range(1, NCHILD):
            other = frames[EDGE + rows_smem[nested] + me + offset]
            value = jnp.where(lane >= 32 * nested, other, value)
        return value

    south, middle, north = lanes_of(-1), lanes_of(0), lanes_of(1)

    def lane_field(row, index):
        return row if index == 0 else pltpu.roll(row, TILE - index, 1)

    e_w, e_c, e_e = [lane_field(middle, i) for i in (0, 1, 2)]
    u_w, u_c, u_e = [lane_field(middle, i) for i in (3, 4, 5)]
    v_w, v_c, v_e = [lane_field(middle, i) for i in (6, 7, 8)]
    e_s, u_s, v_s = [lane_field(south, i) for i in (1, 4, 7)]
    e_n, u_n, v_n = [lane_field(north, i) for i in (1, 4, 7)]
    e_o, u_o, v_o, b_c, ce_c, cu_c, cv_c = [lane_field(middle, i) for i in range(9, 16)]
    e_2 = e_o - HALF * (
        b_c * ((u_e - u_w) + (v_n - v_s)) + (e_e * u_e - e_w * u_w) + (e_n * v_n - e_s * v_s)
    )
    u_2 = u_o - HALF * (u_c * (u_e - u_w) + v_c * (u_n - u_s) + (e_e - e_w)) - DRAG * u_c
    v_2 = v_o - HALF * (u_c * (v_e - v_w) + v_c * (v_n - v_s) + (e_n - e_s)) - DRAG * v_c
    for index, value in enumerate((e_c, u_c, v_c, e_2, u_2, v_2, b_c, ce_c, cu_c, cv_c)):
        fvals[index : index + 1, :] = value
    for nested in range(NCHILD):
        for side in range(2):
            where = 32 * nested + 16 * side
            lanes = slice(0, TILE) if side == 0 else slice(TILE + C_COLS, PADDED)
            for part in range(3):
                for base, array in ((0, now), (3, nxt)):
                    cell = fvals[base + part : base + part + 1, where : where + 1]
                    array[nested, part, :, lanes] = jnp.broadcast_to(cell, (C_ROWS, TILE))

    def forward(stage, nested, state, base, target, slopes):
        def chunk(j, carry):
            here = pl.multiple_of(j * CHUNK, CHUNK)
            wide = pl.ds(here, CHUNK + 2 * TILE)
            plain = pl.ds(here, CHUNK)
            inner = pl.ds(here + TILE, CHUNK)
            shifted = []
            for part in range(3):
                block = state[nested, part, :, wide]
                mid_block = block[:, TILE : TILE + CHUNK]
                before = halo_row(stage, nested, 0, part, plain)
                after = halo_row(stage, nested, 1, part, plain)
                shifted.append(
                    (mid_block,) + column_shifts(block, CHUNK) + row_shifts(mid_block, before, after)
                )
            changes, found = rates(shifted, depth[nested, :, inner])
            for index, slope in enumerate(found):
                slopes[index, nested, :, plain] = slope
            bases = [base(part, inner, plain) for part in range(3)]
            news = [start - change for start, change in zip(bases, changes)]
            for part in range(3):
                target(part, inner, plain, news[part], j)
            return carry

        lax.fori_loop(0, C_COLS // CHUNK, chunk, 0, unroll=COAST_UNROLL)

    def add_sums(which, nested, part, value, j):
        row = (nested * 3 + part) * 4 + j // 2
        sums[which, pl.ds(row, 1), pl.ds(pl.multiple_of(lax.rem(j, 2) * CHUNK, CHUNK), CHUNK)] = (
            jnp.sum(value, axis=0, keepdims=True)
        )

    def stage_a(nested, carry):
        halo_wait(0, nested)

        def target(part, inner, plain, value, j):
            nxt[nested, part, :, inner] = value
            put_row(1, nested, part, plain, value)
            add_sums(0, nested, part, value, j)

        forward(0, nested, now, lambda part, inner, plain: old[nested, part, :, plain], target, slopes1)
        halo_start(1, nested)
        return carry

    loads[7].wait()
    lax.fori_loop(0, NCHILD, stage_a, 0)

    deal(ROW_UNITS, 0, lambda unit: win.at[unit], gathered.at[mine], t_send.at[0], t_recv.at[0])
    for band in range(P_COLS // BAND):
        ocean_start(0, band)
    def stage_b(nested, carry):
        halo_wait(1, nested)

        def target(part, inner, plain, value, j):
            old[nested, part, :, plain] = value
            add_sums(1, nested, part, value, j)

        forward(1, nested, nxt, lambda part, inner, plain: now[nested, part, :, inner], target, slopes2)
        return carry

    lax.fori_loop(0, NCHILD, stage_b, 0)
    store_next = pltpu.make_async_copy(old, next_out, store_sem.at[0])
    store_next.start()

    fine = lax.broadcasted_iota(jnp.int32, (RATIO * TILE, TILE), 0) // RATIO
    coarse = lax.broadcasted_iota(jnp.int32, (RATIO * TILE, TILE), 1)
    gather_matrix = jnp.where(fine == coarse, 1.0 / (RATIO * RATIO), 0.0).astype(jnp.bfloat16)
    fine_t = lax.broadcasted_iota(jnp.int32, (TILE, RATIO * TILE), 1) // RATIO
    coarse_t = lax.broadcasted_iota(jnp.int32, (TILE, RATIO * TILE), 0)
    spread_matrix = jnp.where(fine_t == coarse_t, 1.0 / (RATIO * RATIO), 0.0).astype(jnp.bfloat16)
    for which in range(2):
        rest[which] = exact_dot(sums[which], gather_matrix)
    for unit in range(BACK):
        for which in range(2):
            pairs[unit, which : which + 1, :] = rest[which, unit : unit + 1, :]

    deal(BACK, BACK_FIRST, lambda unit: pairs.at[unit], returned.at[pad + me], t_send.at[3], t_recv.at[3])

    @pl.when(me < ROW_UNITS)
    def _():
        whole = gathered.at[pl.ds(EDGE, ocean_rows)]
        pltpu.make_async_copy(whole, whole, t_recv.at[0]).wait()
        first = grid_first(lax.rem(me // PARTS, NCHILD))
        picked[...] = gathered[pl.ds(EDGE + first, FOOT_ROWS)]
        every(lambda other: picked.at[other], rowbuf.at[me], t_send.at[2], t_recv.at[2])
        pltpu.make_async_copy(picked.at[me], rowbuf.at[me], t_recv.at[2]).start()

        beside[0:1] = gathered[pl.ds(EDGE + first - 1, 1)]
        beside[1:2] = gathered[pl.ds(EDGE + first + FOOT_ROWS, 1)]
        for side, target in ((0, 0), (1, n - 1)):

            @pl.when(me != target)
            def _():
                remote(beside.at[side], besides.at[me], t_send.at[1], t_recv.at[1], target).start()

            @pl.when(me == target)
            def _():
                pltpu.make_async_copy(beside.at[side], besides.at[me], t_recv.at[1]).start()

    loads[0].wait()
    loads[4].wait()
    def ocean_lanes(j):
        here = pl.multiple_of(j * CHUNK, CHUNK)
        return pl.ds(here, CHUNK), pl.ds(here + TILE, CHUNK), pl.ds(here, CHUNK + 2 * TILE)

    def ocean_edge(side, field, plain):
        return jnp.where(has_before if side == 0 else has_after, ocean_halo[side, field, :, plain], 0.0)

    def put8(array, part, inner, own, field, plain):
        array[part, 1:5, inner] = own
        if field is not None:
            array[part, 0:1, inner] = ocean_edge(0, field, plain)
            array[part, 5:6, inner] = ocean_edge(1, field, plain)

    chunks = P_COLS // CHUNK
    ocean_wait(0)

    def assemble(j, carry):
        plain, inner, wide = ocean_lanes(j)
        for part in range(3):
            put8(now8, part, inner, p_now[part, :, plain], part, plain)
        depth8[1:5, inner] = p_depth[:, plain]
        depth8[0:1, inner] = ocean_edge(0, 3, plain)
        depth8[5:6, inner] = ocean_edge(1, 3, plain)
        return carry

    lax.fori_loop(0, chunks, assemble, 0, unroll=OCEAN_UNROLL)

    def turn(field):
        return pltpu.roll(field, 7, 0), pltpu.roll(field, 1, 0)

    def ocean_rates(state, j):
        plain, inner, wide = ocean_lanes(j)
        shifted = []
        for part in range(3):
            block = state[part, :, wide]
            middle = block[:, TILE : TILE + CHUNK]
            shifted.append((middle,) + column_shifts(block, CHUNK) + turn(middle))
        return rates(shifted, depth8[:, inner])

    def ocean_first(j, carry):
        plain, inner, wide = ocean_lanes(j)
        changes, found = ocean_rates(now8, j)
        for index, slope in enumerate(found):
            pslopes[index, :, plain] = slope
        for part in range(3):
            second8[part, 1:5, inner] = p_old[part, :, plain] - changes[part][1:5]
        return carry

    lax.fori_loop(0, chunks, ocean_first, 0, unroll=OCEAN_UNROLL)

    for nested in range(NCHILD):
        def first_product(q):
            tile = slice(TILE * q, TILE * (q + 1))
            return second8[2, 1:5, TILE * (q + 1) : TILE * (q + 2)] * p_end[1, :, tile]

        def second_product(q):
            tile = slice(TILE * q, TILE * (q + 1))
            v_2 = second8[2, 1:5, TILE * (q + 1) : TILE * (q + 2)]
            return p_depth[:, tile] * p_end[0, :, tile] + v_2 * p_end[2, :, tile]

        value = band_tiles(nested, (first_product, second_product))
        for which in range(2):
            for piece in range(PARTS):
                unit = (which * NCHILD + nested) * PARTS + piece
                for row in range(P_ROWS):
                    at = which * P_ROWS + row
                    side_win[unit, row] = value[at : at + 1, (piece + 1) * TILE : (piece + 2) * TILE]
    deal(SIDE_UNITS, SIDE_FIRST, lambda unit: side_win.at[unit], side_gathered.at[mine], t_send.at[5], t_recv.at[5])

    @pl.when(me >= SIDE_FIRST)
    def _():
        whole = side_gathered.at[pl.ds(EDGE, ocean_rows)]
        pltpu.make_async_copy(whole, whole, t_recv.at[5]).wait()
        first = grid_first(lax.rem((me - SIDE_FIRST) // PARTS, NCHILD))
        side_picked[0:1] = side_gathered[pl.ds(EDGE + first - 1, 1)]
        side_picked[1:2] = side_gathered[pl.ds(EDGE + first + FOOT_ROWS, 1)]
        for side, target in ((0, 0), (1, n - 1)):
            place = side_rows.at[me - SIDE_FIRST]

            @pl.when(me != target)
            def _():
                remote(side_picked.at[side], place, t_send.at[6], t_recv.at[6], target).start()

            @pl.when(me == target)
            def _():
                pltpu.make_async_copy(side_picked.at[side], place, t_recv.at[6]).start()

    @pl.when((me >= BACK_FIRST) & (me < BACK_FIRST + BACK))
    def _():
        all_back = returned.at[pl.ds(pad, span)]
        pltpu.make_async_copy(all_back, all_back, t_recv.at[3]).wait()
        first = grid_first((me - BACK_FIRST) // (3 * PARTS))
        placed[...] = returned[pl.ds(pad - first, ocean_rows)]

        def rows_for(other):
            return placed.at[pl.ds(other * P_ROWS, P_ROWS)]

        every(rows_for, back.at[me - BACK_FIRST], t_send.at[4], t_recv.at[4])
        pltpu.make_async_copy(rows_for(me), back.at[me - BACK_FIRST], t_recv.at[4]).start()

    pltpu.make_async_copy(rowbuf, rowbuf, t_recv.at[2]).wait()
    for which in range(2):
        for nested in range(NCHILD):
            for part in range(3):
                for piece in range(PARTS):
                    unit = (part * NCHILD + nested) * PARTS + piece
                    row = (nested * 3 + part) * PARTS + piece
                    lhs[which, row : row + 1, :] = rowbuf[unit, which : which + 1, :]
    spread[0] = exact_dot(lhs[0], spread_matrix)

    def spread_at(which, nested, part, j):
        row = (nested * 3 + part) * 4 + j // 2
        return spread[which, pl.ds(row, 1), pl.ds(pl.multiple_of(lax.rem(j, 2) * CHUNK, CHUNK), CHUNK)]

    def stage_c(nested, carry):
        def chunk(j, inner_carry):
            here = pl.multiple_of(j * CHUNK, CHUNK)
            plain = pl.ds(here, CHUNK)
            inner = pl.ds(here + TILE, CHUNK)
            scaled = []
            for part in range(3):
                total = end[nested, part, :, plain] + spread_at(0, nested, part, j)
                end[nested, part, :, plain] = total
                scaled.append(HALF * total)
                a2[nested, part, :, inner] = scaled[-1]
                put_row(2, nested, part, plain, scaled[-1])
            return inner_carry

        lax.fori_loop(0, C_COLS // CHUNK, chunk, 0, unroll=COAST_UNROLL)
        halo_start(2, nested)
        return carry

    loads[8].wait()
    lax.fori_loop(0, NCHILD, stage_c, 0)

    @pl.when((me == 0) | (me == n - 1))
    def _():
        pltpu.make_async_copy(besides, besides, t_recv.at[1]).wait()
        pltpu.make_async_copy(side_rows, side_rows, t_recv.at[6]).wait()
        sign = jnp.where(me == 0, -1.0, 1.0)
        for nested in range(NCHILD):

            def line(array, field):
                unit = (field * NCHILD + nested) * PARTS
                return HALF * jnp.concatenate([array[unit + piece, 0:1, :] for piece in range(PARTS)], axis=1)

            ce, cv = line(besides, 0), line(besides, 2)
            e_q, v_q = [
                jnp.concatenate(
                    [rest[0, (nested * 3 + part) * 4 + q : (nested * 3 + part) * 4 + q + 1, :] for q in range(4)],
                    axis=1,
                )
                for part in (0, 2)
            ]
            qrow[nested, 0:1, :] = sign * (v_q * ce + cv)
            qrow[nested, 1:2, :] = sign * line(side_rows, 0)
            qrow[nested, 2:3, :] = sign * (line(side_rows, 1) + e_q * ce)

    for nested in range(NCHILD):
        row0 = nested * 12
        for side in range(2):
            sign = -1.0 if side == 0 else 1.0
            where = 32 * nested + 16 * side
            cell = 0 if side == 0 else TILE - 1
            chunk_row = 0 if side == 0 else 3
            u2, bed, ce, cu, cv = [fvals[i : i + 1, where : where + 1] for i in (4, 6, 7, 8, 9)]
            ce, cu, cv = HALF * ce, HALF * cu, HALF * cv
            e_q = rest[0, row0 + chunk_row : row0 + chunk_row + 1, cell : cell + 1]
            u_q = rest[0, row0 + 4 + chunk_row : row0 + 5 + chunk_row, cell : cell + 1]
            adds = (
                sign * (u_q * ce + cu),
                sign * (bed * ce + u2 * cu + e_q * ce),
                sign * (u2 * cv),
            )
            for part in range(3):
                row = row0 + 4 * part + chunk_row
                lhs[1, row : row + 1, :] += jnp.where(lane == cell, adds[part], 0.0)
        for part in range(3):
            for q in range(4):
                row = row0 + 4 * part + q
                lhs[1, row : row + 1, :] += qrow[nested, part : part + 1, TILE * q : TILE * (q + 1)]
    spread[1] = exact_dot(lhs[1], spread_matrix)

    def adjoint(stage, nested, state, cots, slopes, target):
        def chunk(j, carry):
            here = pl.multiple_of(j * CHUNK, CHUNK)
            wide = pl.ds(here, CHUNK + 2 * TILE)
            plain = pl.ds(here, CHUNK)
            inner = pl.ds(here + TILE, CHUNK)
            wides = [cots[nested, part, :, wide] for part in range(3)]
            wides += [state[nested, 1, :, wide], depth[nested, :, wide]]
            e, v = state[nested, 0, :, inner], state[nested, 2, :, inner]

            edge_fields = []
            for side in range(2):
                he, hu, hv = [halo_row(stage, nested, side, part, plain) for part in range(3)]
                sv = halo_row(1 if stage == 2 else 0, nested, side, 2, plain)
                sb = halo_row(0, nested, side, 3, plain)
                edge_fields.append((he, hv, sv * hu, sb * he + sv * hv))

            def dy(field, index):
                ahead, behind = row_shifts(field, edge_fields[0][index], edge_fields[1][index])
                return ahead - behind

            grads = pulled(wides, e, v, dy, [slopes[i, nested, :, plain] for i in range(4)])
            target(inner, plain, j, grads)
            return carry

        lax.fori_loop(0, C_COLS // CHUNK, chunk, 0, unroll=COAST_UNROLL)

    def frame_cots(nested, state, cots, first):
        for side in range(2):
            near = pl.ds(TILE, TILE) if side == 0 else pl.ds(C_COLS, TILE)
            far = pl.ds(0, TILE) if side == 0 else pl.ds(TILE + C_COLS, TILE)
            cell = 0 if side == 0 else TILE - 1
            sign = 1.0 if side == 0 else -1.0
            ae, au, av = [cots[nested, part, :, near] for part in range(3)]
            u, bed = state[nested, 1, :, near], depth[nested, :, near]
            ef, uf = state[nested, 0, :, far], state[nested, 1, :, far]
            values = (uf * ae + au, bed * ae + u * au + ef * ae, u * av)
            for part in range(3):
                column = sign * jnp.sum(values[part], axis=0, keepdims=True)[:, cell : cell + 1]
                packet[...] = jnp.where(
                    lane == nested * 16 + side * 8 + first + part, column, packet[...]
                )

    def stage_d(nested, carry):
        halo_wait(2, nested)

        def target(inner, plain, j, grads):
            scaled = []
            for part in range(3):
                total = mid[nested, part, :, plain] + grads[part] + spread_at(1, nested, part, j)
                mid[nested, part, :, plain] = total
                scaled.append(HALF * total)
                a1[nested, part, :, inner] = scaled[-1]
                put_row(3, nested, part, plain, scaled[-1])

        adjoint(2, nested, nxt, a2, slopes2, target)
        halo_start(3, nested)
        frame_cots(nested, nxt, a2, 0)
        frame_cots(nested, now, a1, 3)
        return carry

    loads[9].wait()
    lax.fori_loop(0, NCHILD, stage_d, 0)
    store_gold = pltpu.make_async_copy(mid, gold_out, store_sem.at[1])
    store_gold.start()

    edges[me] = packet[...]

    def stage_e(nested, carry):
        halo_wait(3, nested)

        def target(inner, plain, j, grads):
            for part in range(3):
                end[nested, part, :, plain] = end[nested, part, :, plain] + grads[part]

        adjoint(3, nested, now, a1, slopes1, target)
        return carry

    row4 = me * P_ROWS + lax.broadcasted_iota(jnp.int32, (P_ROWS, CHUNK), 0)
    column4 = lax.broadcasted_iota(jnp.int32, (P_ROWS, CHUNK), 1)

    def covered_at(j):
        nested = j // (BAND // CHUNK)
        foot = row4 - rows_smem[nested]
        column = j * CHUNK + column4 - cols_smem[nested]
        return (foot >= 0) & (foot < FOOT_ROWS) & (column >= 0) & (column < FOOT_COLS)

    pltpu.make_async_copy(back, back, t_recv.at[4]).wait()
    for nested in range(NCHILD):
        right = cols_smem[nested] - nested * BAND
        fine_shift = TILE - lax.rem(right, TILE)
        tiles = jnp.full((2 * P_ROWS, TILE), right // TILE, jnp.int32)
        band = nested * BAND
        blank = jnp.zeros((2 * P_ROWS, TILE), jnp.float32)
        for part in range(3):
            rows_of = [
                jnp.concatenate(
                    [back[(nested * 3 + part) * PARTS + q, :, which, :] for q in range(PARTS)], axis=1
                )
                for which in range(2)
            ]
            both = jnp.concatenate([blank, jnp.concatenate(rows_of, axis=0), blank], axis=1)
            both = moved_left(both, fine_shift, 8)
            held = [both[:, TILE * q : TILE * (q + 1)] for q in range(PARTS + 1)]
            held += [blank] * (BAND // TILE - PARTS - 1)
            for bit in range(4):
                step = 1 << bit
                chosen = (tiles >> bit) & 1 == 1
                held = [
                    jnp.where(chosen, held[q - step] if q >= step else blank, held[q])
                    for q in range(len(held))
                ]
            for q, tile in enumerate(held):
                for which in range(2):
                    means[which, part, :, band + TILE * q : band + TILE * (q + 1)] = tile[
                        P_ROWS * which : P_ROWS * (which + 1)
                    ]

    def ocean_second(j, carry):
        plain, inner, wide = ocean_lanes(j)
        covered = covered_at(j)
        for part in range(3):
            state = jnp.where(covered, means[0, part, :, plain], second8[part, 1:5, inner])
            cot = jnp.where(covered, 0.0, HALF * p_end[part, :, plain])
            second8[part, 1:5, inner] = state
            a28[part, 1:5, inner] = cot
            for side, row in ((0, 0), (1, P_ROWS - 1)):
                ocean_send[side, 4 + part, :, plain] = state[row : row + 1]
                ocean_send[side, 7 + part, :, plain] = cot[row : row + 1]
        return carry

    def ocean_second_band(band, carry):
        per = BAND // CHUNK
        lax.fori_loop(0, per, lambda j, inner: ocean_second(band * per + j, inner), 0, unroll=OCEAN_UNROLL)
        ocean_start(1, band)
        return carry

    lax.fori_loop(0, P_COLS // BAND, ocean_second_band, 0)

    lax.fori_loop(0, NCHILD // 2, stage_e, 0)
    every(lambda other: packet, edges.at[me], ag_send.at[1], ag_recv.at[1])

    loads[3].wait()
    ocean_wait(1)

    def ocean_edges(j, carry):
        plain, inner, wide = ocean_lanes(j)
        for part in range(3):
            for array, first in ((second8, 4), (a28, 7)):
                array[part, 0:1, inner] = ocean_edge(0, first + part, plain)
                array[part, 5:6, inner] = ocean_edge(1, first + part, plain)
        return carry

    lax.fori_loop(0, chunks, ocean_edges, 0, unroll=OCEAN_UNROLL)

    def ocean_dy(field, index):
        ahead, behind = turn(field)
        return ahead - behind

    def ocean_pull(j, state, cots, slopes):
        plain, inner, wide = ocean_lanes(j)
        wides = [cots[part, :, wide] for part in range(3)] + [state[1, :, wide], depth8[:, wide]]
        return pulled(wides, state[0, :, inner], state[2, :, inner], ocean_dy, slopes)

    def ocean_third(j, carry):
        plain, inner, wide = ocean_lanes(j)
        covered = covered_at(j)
        changes, found = ocean_rates(second8, j)
        grads = ocean_pull(j, second8, a28, found)
        for part in range(3):
            pend[part, :, plain] = jnp.where(
                covered, means[1, part, :, plain], p_now[part, :, plain] - changes[part][1:5]
            )
            cot = jnp.where(covered, 0.0, p_mid[part, :, plain] + grads[part][1:5])
            pgold[part, :, plain] = cot
            for side, row in ((0, 0), (1, P_ROWS - 1)):
                ocean_send[side, 10 + part, :, plain] = cot[row : row + 1]
        return carry

    def ocean_third_band(band, carry):
        per = BAND // CHUNK
        lax.fori_loop(0, per, lambda j, inner: ocean_third(band * per + j, inner), 0, unroll=OCEAN_UNROLL)
        ocean_start(2, band)
        return carry

    lax.fori_loop(0, P_COLS // BAND, ocean_third_band, 0)
    store_pend = pltpu.make_async_copy(pend, pend_out, store_sem.at[3])
    store_pend.start()

    lax.fori_loop(NCHILD // 2, NCHILD, stage_e, 0)
    store_gnow = pltpu.make_async_copy(end, gnow_out, store_sem.at[2])
    store_gnow.start()

    all_edges = edges.at[pl.ds(0, n - 1)]
    pltpu.make_async_copy(all_edges, all_edges, ag_recv.at[1]).wait()
    row8 = me * P_ROWS - 1 + lax.broadcasted_iota(jnp.int32, (8, 1), 0)
    for nested in range(NCHILD):
        foot = row8 - rows_smem[nested]
        lines = jnp.concatenate(
            [
                edges[jnp.clip(me * P_ROWS - 1 + t - rows_smem[nested], 0, FOOT_ROWS - 1)]
                for t in range(8)
            ],
            axis=0,
        )
        lines = jnp.where((foot >= 0) & (foot < FOOT_ROWS), lines, 0.0)
        for side in range(2):
            for which in range(2):
                for part in range(3):
                    at = nested * 16 + side * 8 + 3 * which + part
                    cells[nested, side, which, part] = jnp.broadcast_to(lines[:, at : at + 1], (8, TILE))
    ocean_wait(2)
    column8 = lax.broadcasted_iota(jnp.int32, (8, CHUNK), 1)

    def beside_at(j, which, part):
        nested = j // (BAND // CHUNK)
        column = j * CHUNK + column8 - cols_smem[nested]
        west, east = [
            jnp.concatenate([cells[nested, side, which, part]] * (CHUNK // TILE), axis=1) for side in range(2)
        ]
        return jnp.where(column == -1, west, 0.0) + jnp.where(column == FOOT_COLS, east, 0.0)

    def ocean_fourth(j, carry):
        plain, inner, wide = ocean_lanes(j)
        for part in range(3):
            extra = beside_at(j, 0, part)
            cot = pgold[part, :, plain] + extra[1:5]
            pgold[part, :, plain] = cot
            a18[part, 1:5, inner] = HALF * cot
            a18[part, 0:1, inner] = HALF * (ocean_edge(0, 10 + part, plain) + extra[0:1])
            a18[part, 5:6, inner] = HALF * (ocean_edge(1, 10 + part, plain) + extra[5:6])
        return carry

    lax.fori_loop(0, chunks, ocean_fourth, 0, unroll=OCEAN_UNROLL)
    store_pgold = pltpu.make_async_copy(pgold, pgold_out, store_sem.at[4])
    store_pgold.start()

    def ocean_last(j, carry):
        plain, inner, wide = ocean_lanes(j)
        covered = covered_at(j)
        grads = ocean_pull(j, now8, a18, [pslopes[i, :, plain] for i in range(4)])
        for part in range(3):
            kept = jnp.where(covered, 0.0, p_end[part, :, plain])
            pgnow[part, :, plain] = kept + (grads[part] + beside_at(j, 1, part))[1:5]
        return carry

    lax.fori_loop(0, chunks, ocean_last, 0, unroll=OCEAN_UNROLL)
    store_pgnow = pltpu.make_async_copy(pgnow, pgnow_out, store_sem.at[5])
    store_pgnow.start()
    for store in (store_next, store_gold, store_gnow, store_pend, store_pgold, store_pgnow):
        store.wait()

    pltpu.make_async_copy(all_but, all_but, ag_send.at[0]).wait()
    pltpu.make_async_copy(all_edges, all_edges, ag_send.at[1]).wait()

    def drain_halo(nested, carry):
        for stage in range(4):
            drain_both(halo_copies(stage, nested))
        return carry

    lax.fori_loop(0, NCHILD, drain_halo, 0)
    for stage in range(3):
        drain_both(ocean_copies(*ocean_stages[stage]))

    def drain(count, first, like, send):
        own = (me >= first) & (me < first + count)

        @pl.when(own)
        def _():
            sent = like.at[pl.ds(0, count - 1)]
            pltpu.make_async_copy(sent, sent, send).wait()

        @pl.when(jnp.logical_not(own))
        def _():
            pltpu.make_async_copy(like, like, send).wait()

    drain(ROW_UNITS, 0, win, t_send.at[0])
    drain(SIDE_UNITS, SIDE_FIRST, side_win, t_send.at[5])
    drain(BACK, BACK_FIRST, pairs, t_send.at[3])

    @pl.when(me < ROW_UNITS)
    def _():
        sent = picked.at[pl.ds(0, n - 1)]
        pltpu.make_async_copy(sent, sent, t_send.at[2]).wait()

    for target in (0, n - 1):

        @pl.when((me != target) & (me < ROW_UNITS))
        def _():
            one = beside.at[0]
            pltpu.make_async_copy(one, one, t_send.at[1]).wait()

        @pl.when((me != target) & (me >= SIDE_FIRST))
        def _():
            one = side_picked.at[0]
            pltpu.make_async_copy(one, one, t_send.at[6]).wait()

    @pl.when((me >= BACK_FIRST) & (me < BACK_FIRST + BACK))
    def _():
        gone = placed.at[pl.ds(0, (n - 1) * P_ROWS)]
        pltpu.make_async_copy(gone, gone, t_send.at[4]).wait()


def everything(n, child_rows, child_cols, win, frame, strips, coast):
    f32 = jnp.float32
    anywhere = pl.BlockSpec(memory_space=pl.ANY)
    smem = pl.BlockSpec(memory_space=pltpu.SMEM)
    grid_shape = (NCHILD, 3, C_ROWS, C_COLS)
    wide_shape = (NCHILD, 3, C_ROWS, PADDED)
    ocean_shape = (3, P_ROWS, P_COLS)
    tall_shape = (3, 8, P_COLS + 2 * TILE)
    ocean_rows = n * P_ROWS
    dma = pltpu.SemaphoreType.DMA
    shapes = [
        grid_shape,
        wide_shape,
        wide_shape,
        (NCHILD, C_ROWS, PADDED),
        grid_shape,
        grid_shape,
        wide_shape,
        wide_shape,
        (4, NCHILD, C_ROWS, C_COLS),
        (4, NCHILD, C_ROWS, C_COLS),
        (NCHILD, 2, 4, 1, C_COLS),
        (NCHILD, 2, 4, 1, C_COLS),
        (3, NCHILD, 2, 3, 1, C_COLS),
        (3, NCHILD, 2, 3, 1, C_COLS),
        (ROW_UNITS, P_ROWS, 2, TILE),
        (SIDE_UNITS, P_ROWS, 1, TILE),
        (P_ROWS, 1, TILE),
        (ocean_rows + 2 * EDGE, 1, TILE),
        (16, TILE),
        (ocean_rows + 2 * EDGE, 2, TILE),
        (ocean_rows + 2 * EDGE, 1, TILE),
        (FOOT_ROWS, 2, TILE),
        (2, 2, TILE),
        (2, 1, TILE),
        (ROW_UNITS, 2, TILE),
        (ROW_UNITS, 2, TILE),
        (SIDE_UNITS, 1, TILE),
        (2, BACK, TILE),
        (2, BACK, RATIO * TILE),
        (2, BACK, RATIO * TILE),
        (2, BACK, TILE),
        (BACK, 2, TILE),
        (2 * ocean_rows + FOOT_ROWS, 2, TILE),
        (ocean_rows, 2, TILE),
        (NCHILD, 8, FOOT_COLS),
        (n, 1, TILE),
        (1, TILE),
        ocean_shape,
        ocean_shape,
        (P_ROWS, P_COLS),
        ocean_shape,
        ocean_shape,
        tall_shape,
        tall_shape[1:],
        tall_shape,
        tall_shape,
        tall_shape,
        (4, 8, P_COLS),
        (2, 3, P_ROWS, P_COLS),
        (NCHILD, 2, 2, 3, 8, TILE),
        (BACK, P_ROWS, 2, TILE),
        ocean_shape,
        ocean_shape,
        ocean_shape,
        (2, 13, 1, P_COLS),
        (2, 13, 1, P_COLS),
    ]
    return pl.pallas_call(
        functools.partial(coastal_kernel, n),
        out_shape=[jax.ShapeDtypeStruct(grid_shape, f32)] * 3 + [jax.ShapeDtypeStruct(ocean_shape, f32)] * 3,
        in_specs=[smem] * 2 + [anywhere] * 12,
        out_specs=[anywhere] * 6,
        scratch_shapes=[pltpu.VMEM(shape, f32) for shape in shapes]
        + [
            dma((12,)),
            dma((6,)),
            dma((4, NCHILD, 2)),
            dma((4, NCHILD, 2)),
            dma((2,)),
            dma((2,)),
            dma((7,)),
            dma((7,)),
            dma((3, 2)),
            dma((3, 2)),
        ],
        compiler_params=pltpu.CompilerParams(
            collective_id=0, has_side_effects=True, vmem_limit_bytes=56 * 1024 * 1024
        ),
    )(child_rows, child_cols, win, frame, *strips, *coast)


def window_kernel(cols, *refs):
    sources, (win, frame), held, sem = refs[:5], refs[5:7], refs[7:12], refs[12]
    reach = FOOT_COLS + 2 * TILE
    shifts, copies = [], []
    for nested in range(NCHILD):
        left = cols[nested]
        start = pl.multiple_of(jnp.clip((left - 2) // TILE * TILE, 0, P_COLS - reach), TILE)
        shifts.append(reach - (left - start))
        for index, (source, target) in enumerate(zip(sources, held)):
            lanes = pl.ds(start, reach)
            part = source.at[:, lanes] if index == 2 else source.at[:, :, lanes]
            copies.append(pltpu.make_async_copy(part, target.at[nested], sem.at[index, nested]))
    for copy in copies:
        copy.start()
    for copy in copies:
        copy.wait()
    old, now, depth, mid, end = held
    lane = lax.broadcasted_iota(jnp.int32, (P_ROWS, TILE), 1)
    packet = jnp.zeros((P_ROWS, TILE), jnp.float32)
    for nested in range(NCHILD):
        fields = [end[nested, i] for i in range(3)] + [mid[nested, i] for i in range(3)]
        fields += [now[nested, i] for i in range(3)] + [old[nested, i] for i in range(3)] + [depth[nested]]
        blocks = []
        for first in range(0, len(fields), 2):
            pair = fields[first : first + 2]
            both = pltpu.roll(jnp.concatenate(pair, axis=0), shifts[nested], 1)
            blocks += [both[P_ROWS * i : P_ROWS * (i + 1)] for i in range(len(pair))]
        for which in range(2):
            for part in range(3):
                for piece in range(PARTS):
                    unit = (part * NCHILD + nested) * PARTS + piece
                    lanes = slice(piece * TILE, (piece + 1) * TILE)
                    for row in range(P_ROWS):
                        win[unit, row, which : which + 1, :] = blocks[3 * which + part][row : row + 1, lanes]
        first_ok = jnp.where(cols[nested] >= 2, 1.0, 0.0)
        last_ok = jnp.where(cols[nested] + FOOT_COLS + 1 < P_COLS, 1.0, 0.0)
        for side, lanes in enumerate(((reach - 2, reach - 1, 0), (FOOT_COLS - 1, FOOT_COLS, FOOT_COLS + 1))):
            found = []
            for part in range(3):
                for which, at in enumerate(lanes):
                    cell = blocks[6 + part][:, at : at + 1]
                    if side == 0 and which == 0:
                        cell = cell * first_ok
                    if side == 1 and which == 2:
                        cell = cell * last_ok
                    found.append(cell)
            found += [blocks[index][:, lanes[1] : lanes[1] + 1] for index in (9, 10, 11, 12, 0, 1, 2)]
            for index, cell in enumerate(found):
                packet = jnp.where(lane == 32 * nested + 16 * side + index, cell, packet)
    for row in range(P_ROWS):
        frame[row] = packet[row : row + 1]


def windows(strips, child_cols):
    f32 = jnp.float32
    reach = FOOT_COLS + 2 * TILE
    return pl.pallas_call(
        window_kernel,
        out_shape=[
            jax.ShapeDtypeStruct((ROW_UNITS, P_ROWS, 2, TILE), f32),
            jax.ShapeDtypeStruct((P_ROWS, 1, TILE), f32),
        ],
        in_specs=[pl.BlockSpec(memory_space=pltpu.SMEM)] + [pl.BlockSpec(memory_space=pl.ANY)] * 5,
        out_specs=[pl.BlockSpec(memory_space=pltpu.VMEM)] * 2,
        scratch_shapes=[pltpu.VMEM((NCHILD,) + strip.shape[:-1] + (reach,), f32) for strip in strips]
        + [pltpu.SemaphoreType.DMA((5, NCHILD))],
        compiler_params=pltpu.CompilerParams(vmem_limit_bytes=60 * 1024 * 1024),
    )(child_cols, *strips)


def bounce_kernel(*refs):
    sources, targets, held, sems = refs[:6], refs[6:12], refs[12:18], refs[18]
    pieces = []
    for index in range(6):
        size = sources[index].shape[0]
        count = 1
        for place in range(count):
            part = pl.ds(place * (size // count), size // count)
            pieces.append(
                (
                    pltpu.make_async_copy(
                        sources[index].at[part], held[index].at[part], sems.at[0, index, place]
                    ),
                    pltpu.make_async_copy(
                        held[index].at[part], targets[index].at[part], sems.at[1, index, place]
                    ),
                )
            )
    for fetch, store in pieces:
        fetch.start()
    for fetch, store in pieces:
        fetch.wait()
        store.start()
    for fetch, store in pieces:
        store.wait()


def bounce(arrays):
    anywhere = pl.BlockSpec(memory_space=pl.ANY)
    return pl.pallas_call(
        bounce_kernel,
        out_shape=[jax.ShapeDtypeStruct(array.shape, array.dtype) for array in arrays],
        in_specs=[anywhere] * 6,
        out_specs=[anywhere] * 6,
        scratch_shapes=[pltpu.VMEM(array.shape, array.dtype) for array in arrays]
        + [pltpu.SemaphoreType.DMA((2, 6, NCHILD))],
        compiler_params=pltpu.CompilerParams(vmem_limit_bytes=60 * 1024 * 1024),
    )(*arrays)


def shards(
    n,
    parent_old,
    parent_now,
    child_old,
    child_now,
    parent_depth,
    child_depth,
    child_rows,
    child_cols,
    parent_cot_mid,
    parent_cot_end,
    child_cot_mid,
    child_cot_end,
):
    strips = (parent_old, parent_now, parent_depth, parent_cot_mid, parent_cot_end)
    coast = (child_old, child_now, child_depth, child_cot_mid, child_cot_end)
    win, frame = windows(strips, child_cols)
    results = bounce(everything(n, child_rows, child_cols, win, frame, strips, coast))
    child_end, child_gold, child_gnow, parent_end, parent_gold, parent_gnow = results
    return (parent_end, child_end, parent_gold, parent_gnow, child_gold, child_gnow)


def solution(mesh):
    ocean_spec = P(None, "rows", None)
    coast_spec = P(None, None, "rows", None)
    return jax.shard_map(
        functools.partial(shards, mesh.shape["rows"]),
        mesh=mesh,
        in_specs=(
            ocean_spec,
            ocean_spec,
            coast_spec,
            coast_spec,
            P("rows", None),
            P(None, "rows", None),
            P(),
            P(),
            ocean_spec,
            ocean_spec,
            coast_spec,
            coast_spec,
        ),
        out_specs=(ocean_spec, coast_spec, ocean_spec, ocean_spec, coast_spec, coast_spec),
        check_vma=False,
    )
```
